128 devices in a mesh: seq: 16 (over y, z), head: 8 (over x, core).
Axes of the slice: x: 4, y: 4, z: 4, core: 2. Of those that a mesh axis runs over, the one named last changes fastest.
Arguments:
- pre_x: bfloat16 [16384, 5120], P('seq', 'head'), may hold values from -6 to 6
- pre_bc: bfloat16 [16384, 256], P('seq'), may hold values from -6 to 6
- gate_z: bfloat16 [16384, 5120], P('seq', 'head'), may hold values from -6 to 6
- dt_raw: float32 [80, 16384], P('head', 'seq'), may hold values from -3 to 3
- conv_x: float32 [4, 5120], P(None, 'head'), may hold values from -3 to 3
- conv_bc: float32 [4, 256], replicated, may hold values from -3 to 3
- head_params: float32 [3, 80], P(None, 'head'), may hold values from -12 to 2, as said below
- norm_gain: float32 [5120], P('head'), may hold values from 0.5 to 1.5
- w_out: bfloat16 [5120, 2560], P('head'), may hold values from -0.078125 to 0.078125
- t_conv_x: float32 [4, 5120], P(None, 'head'), may hold values from -3 to 3
- t_conv_bc: float32 [4, 256], replicated, may hold values from -3 to 3
- t_heads: float32 [3, 80], P(None, 'head'), may hold values from -3 to 3
- t_gain: float32 [5120], P('head'), may hold values from -1 to 1
- t_wout: bfloat16 [5120, 2560], P('head', 'seq'), may hold values from -0.078125 to 0.078125
Outputs:
- gn_conv_x: float32 [4, 5120], P(None, 'head')
- gn_conv_bc: float32 [4, 256], replicated
- gn_heads: float32 [3, 80], P(None, 'head')
- gn_gain: float32 [5120], P('head')
- gn_wout: float32 [5120, 2560], P('head', 'seq')
The draws below stay inside these ranges and needn't reach their ends.
Inputs may be any that keep to these rules, and one draw needn't show every extreme that they name: `head_params`: row 0 is a step bias per head, row 1 a log decay rate per head, row 2 a skip gain per head.
All inputs are finite; a program needn't handle non-finite values.
Results may differ from the reference program's by a relative error of at most 0.00041.
Values may be sent and summed in bfloat16 or wider, within the bound.
A program may use at most 192 MiB of HBM per device.

```python
import math
import jax
import jax.numpy as jnp
from jax import lax

D = 2560
NH = 80
N = 128
KW = 4
BLOCK = 256
TOKENS = 16384
E = 5120


def draw_head_params(key, part):
    key = jax.random.fold_in(key, 7)
    keys = jax.random.split(key, 4)
    share = 0.5
    step_bias = jax.random.uniform(keys[0], (NH,), jnp.float32, -4.5, -2.5)
    slow = jax.random.bernoulli(keys[1], share, (NH,))
    spot = jax.random.uniform(keys[2], (NH,), jnp.float32)
    slow_log = math.log(0.2) + spot * (math.log(2.0) - math.log(0.2))
    fast_log = jnp.log(TOKENS / 400.0) + spot * math.log(400.0 / 30.0)
    reach = jnp.where(slow, slow_log, fast_log)
    log_rate = reach - jnp.log(0.03 * TOKENS)
    skip_gain = jax.random.uniform(keys[3], (NH,), jnp.float32, 0.5, 1.5)
    return jnp.stack([step_bias, log_rate, skip_gain]).astype(jnp.float32)


def block_scale(rng, shape, cuts, smallest, high):
    level = 1.0
    for axis_at, parts in cuts:
        heights = jax.random.uniform(jax.random.fold_in(jax.random.fold_in(rng, 6), axis_at), (parts,), jnp.float32, smallest / len(cuts), high / len(cuts))
        level = level * jnp.repeat(jnp.exp(heights), shape[axis_at] // parts).reshape((-1,) + (1,) * (len(shape) - 1 - axis_at))
    return level


def bell_draw(key, shape, spread, most, cuts=(), dtype=jnp.bfloat16):
    result = spread * jax.random.normal(key, shape, jnp.float32)
    if cuts:
        result = result * block_scale(key, shape, cuts, -0.22, 0.18)
    return jnp.clip(result, -most, most).astype(dtype)


def setup_inputs(seed: int = 0) -> dict:
    seeds = jax.random.split(jax.random.key(seed), 15)
    pre_x = bell_draw(seeds[0], (TOKENS, E), 1.0, 6.0, ((0, 16), (1, 8)))
    pre_bc = bell_draw(seeds[1], (TOKENS, 2 * N), 1.0, 6.0, ((0, 16),))
    gate_z = bell_draw(seeds[2], (TOKENS, E), 1.0, 6.0, ((0, 16), (1, 8)))
    dt_raw = bell_draw(seeds[3], (NH, TOKENS), 0.5, 3.0, ((0, 8), (1, 16)), jnp.float32)
    conv_x = bell_draw(seeds[4], (KW, E), 0.5, 3.0, ((1, 8),), jnp.float32)
    conv_bc = bell_draw(seeds[5], (KW, 2 * N), 0.5, 3.0, (), jnp.float32)
    head_params = draw_head_params(jax.random.fold_in(seeds[14], 71), 0)
    norm_gain = jnp.clip(1.0 + 0.1 * jax.random.normal(seeds[7], (E,), jnp.float32), 0.5, 1.5)
    w_out = bell_draw(seeds[8], (E, D), E ** -0.5, 0.078125, ((0, 8),))
    t_conv_x = bell_draw(seeds[9], (KW, E), 0.5, 3.0, ((1, 8),), jnp.float32)
    t_conv_bc = bell_draw(seeds[10], (KW, 2 * N), 0.5, 3.0, (), jnp.float32)
    t_heads = bell_draw(seeds[11], (3, NH), 0.5, 3.0, ((1, 8),), jnp.float32)
    t_gain = bell_draw(seeds[12], (E,), 0.2, 1.0, ((0, 8),), jnp.float32)
    t_wout = bell_draw(seeds[13], (E, D), E ** -0.5, 0.078125, ((0, 8), (1, 16)))
    return dict(pre_x=pre_x, pre_bc=pre_bc, gate_z=gate_z, dt_raw=dt_raw, conv_x=conv_x, conv_bc=conv_bc, head_params=head_params, norm_gain=norm_gain, w_out=w_out, t_conv_x=t_conv_x, t_conv_bc=t_conv_bc, t_heads=t_heads, t_gain=t_gain, t_wout=t_wout)


def conv_silu(padded, weight):
    width = weight.shape[0]
    length = padded.shape[0] - width + 1
    total = jnp.zeros((length, padded.shape[1]), jnp.float32)
    for offset in range(width):
        total = total + weight[offset][None, :] * padded[offset:offset + length].astype(jnp.float32)
    return jax.nn.silu(total)

def block_step(state, pieces):
    x_block, b_block, c_block, step_block, decay_rate = pieces
    high = lax.Precision.HIGHEST
    length = b_block.shape[0]
    log_decay = -step_block * decay_rate[:, None]
    cumul = jnp.cumsum(log_decay, axis=1)
    lower_mask = jnp.arange(length)[:, None] >= jnp.arange(length)[None, :]
    diffs = cumul[:, :, None] - cumul[:, None, :]
    weights_in = jnp.where(lower_mask[None], jnp.exp(jnp.where(lower_mask[None], diffs, 0.0)), 0.0)
    inner = jnp.dot(c_block, b_block.T, precision=high)
    weights_in = inner[None] * weights_in * step_block[:, None, :]
    y_inner = jnp.einsum('hij,jhp->ihp', weights_in, x_block, precision=high)
    y_carry = jnp.exp(cumul).T[:, :, None] * jnp.einsum('in,hpn->ihp', c_block, state, precision=high)
    to_end = jnp.exp(cumul[:, -1:] - cumul) * step_block
    scaled_x = to_end.T[:, :, None] * x_block
    new_state = jnp.exp(cumul[:, -1])[:, None, None] * state + jnp.einsum('jhp,jn->hpn', scaled_x, b_block, precision=high)
    return (new_state, y_inner + y_carry)

def ssd_scan(xconv, b_mat, c_mat, step_size, decay_rate, start_state):
    length = xconv.shape[0]
    heads_here = step_size.shape[0]
    head_width = xconv.shape[1] // heads_here
    count = length // BLOCK
    x_blocks = xconv.reshape(count, BLOCK, heads_here, head_width)
    b_blocks = b_mat.reshape(count, BLOCK, b_mat.shape[1])
    c_blocks = c_mat.reshape(count, BLOCK, c_mat.shape[1])
    s_blocks = step_size.reshape(heads_here, count, BLOCK).transpose(1, 0, 2)

    def stepper(state, pieces):
        return block_step(state, (pieces[0], pieces[1], pieces[2], pieces[3], decay_rate))
    end_state, ys = lax.scan(jax.checkpoint(stepper), start_state, (x_blocks, b_blocks, c_blocks, s_blocks))
    return (end_state, ys.reshape(length, heads_here * head_width))

def core_fn(padded_x, padded_bc, dt_raw, conv_x, conv_bc, head_params):
    xconv = conv_silu(padded_x, conv_x)
    bcconv = conv_silu(padded_bc, conv_bc)
    nstate = bcconv.shape[1] // 2
    step_size = jax.nn.softplus(dt_raw + head_params[0][:, None])
    decay_rate = jnp.exp(head_params[1])
    heads_here = step_size.shape[0]
    head_width = xconv.shape[1] // heads_here
    start_state = jnp.zeros((heads_here, head_width, nstate), jnp.float32)
    end_state, ys = ssd_scan(xconv, bcconv[:, :nstate], bcconv[:, nstate:], step_size, decay_rate, start_state)
    y_out = ys + jnp.repeat(head_params[2], head_width)[None, :] * xconv
    total_decay = jnp.exp(-lax.optimization_barrier(jnp.sum(step_size * decay_rate[:, None], axis=1)))
    return (y_out, total_decay, end_state)

def reference(pre_x, pre_bc, gate_z, dt_raw, conv_x, conv_bc, head_params, norm_gain, w_out, t_conv_x, t_conv_bc, t_heads, t_gain, t_wout):
    width = conv_x.shape[0] - 1
    padded_x = jnp.pad(pre_x, ((width, 0), (0, 0)))
    padded_bc = jnp.pad(pre_bc, ((width, 0), (0, 0)))

    def whole(cx, cbc, hp):
        return core_fn(padded_x, padded_bc, dt_raw, cx, cbc, hp)[0]
    y_out, d_y = jax.jvp(whole, (conv_x, conv_bc, head_params), (t_conv_x, t_conv_bc, t_heads))
    gate = jax.nn.silu(gate_z.astype(jnp.float32))
    gated = y_out * gate
    d_gated = d_y * gate
    channels = gated.shape[1] * 1.0
    inv_rms = lax.rsqrt(lax.optimization_barrier(jnp.sum(gated * gated, axis=1)) / channels + 1e-05)
    d_inv = -0.5 * inv_rms ** 3 * lax.optimization_barrier(jnp.sum(2.0 * gated * d_gated, axis=1)) / channels
    normed = (gated * inv_rms[:, None] * norm_gain).astype(jnp.bfloat16)
    d_normed = ((d_gated * inv_rms[:, None] + gated * d_inv[:, None]) * norm_gain + gated * inv_rms[:, None] * t_gain).astype(jnp.bfloat16)
    probe_out = (jnp.dot(d_normed, w_out, preferred_element_type=jnp.float32) + jnp.dot(normed, t_wout, preferred_element_type=jnp.float32)).astype(jnp.bfloat16)
    gn_wout = jnp.dot(normed.T, probe_out, preferred_element_type=jnp.float32)
    back_normed = jnp.dot(probe_out, w_out.T, preferred_element_type=jnp.float32)
    gn_gain = lax.optimization_barrier(jnp.sum(back_normed * gated * inv_rms[:, None], axis=0))
    weighted = back_normed * norm_gain
    mixed = lax.optimization_barrier(jnp.sum(weighted * gated, axis=1))
    back_y = (weighted * inv_rms[:, None] - gated * (inv_rms ** 3 * mixed / channels)[:, None]) * gate
    primal_out, pullback = jax.vjp(whole, conv_x, conv_bc, head_params)
    grads = pullback(back_y)
    return (grads[0], grads[1], grads[2], gn_gain, gn_wout)
```

```python
import jax
import jax.numpy as jnp
from jax import lax
from jax.experimental import pallas as pl
from jax.experimental.pallas import tpu as pltpu
from jax.sharding import PartitionSpec as P

QB = 128
HW = 64
F32 = jnp.float32
BF16 = jnp.bfloat16
MESH = pl.DeviceIdType.MESH
S_, DS_, C_, DC_, CS_, SG_, K_, DK_ = (16 * i for i in range(8))
LIMIT = 50 * 1024 * 1024


def split(a):
    high = a.astype(BF16)
    return high, (a - high.astype(F32)).astype(BF16)


def nn(a, b):
    return jnp.dot(a, b, preferred_element_type=F32)


def nt(a, b):
    return lax.dot_general(a, b, (((1,), (1,)), ((), ())), preferred_element_type=F32)


def nn3(a, b):
    (ah, al), (bh, bl) = split(a), split(b)
    return nn(ah, bh) + nn(ah, bl) + nn(al, bh)


def nt3(a, b):
    (ah, al), (bh, bl) = split(a), split(b)
    return nt(ah, bh) + nt(ah, bl) + nt(al, bh)


def lane_mask():
    return lax.broadcasted_iota(jnp.int32, (1, 128), 1) < HW


def bcast(cols, at):
    return jnp.broadcast_to(cols[:, at : at + 1], (cols.shape[0], 128))


def expand(cols, base, pair):
    return jnp.where(
        lane_mask(), bcast(cols, base + 2 * pair), bcast(cols, base + 2 * pair + 1)
    )


def expand_all(cols, base, heads):
    return jnp.concatenate([expand(cols, base, p) for p in range(heads // 2)], axis=1)


def load_window(window, halo, block, first):
    @pl.when(first)
    def _():
        window[0:8] = halo[...]

    @pl.when(jnp.logical_not(first))
    def _():
        window[0:8] = window[QB : QB + 8]

    window[8 : QB + 8] = block[...].astype(F32)


def conv_pair(window, weight, t_weight):
    z = jnp.zeros((QB, window.shape[1]), F32)
    dz = jnp.zeros((QB, window.shape[1]), F32)
    for k in range(4):
        rows = window[5 + k : 5 + k + QB, :]
        z = z + weight[k : k + 1, :] * rows
        dz = dz + t_weight[k : k + 1, :] * rows
    sig = jax.nn.sigmoid(z)
    slope = sig * (1.0 + z * (1.0 - sig))
    return z * sig, slope * dz, slope


def first_kernel(
    pre_x, halo_x, pre_bc, halo_bc, dt, cx, tcx, cbc, tcbc, hpc,
    x_o, dx_o, gx_o, bc_o, dbc_o, gbc_o, row_o, col_o, st_o, dst_o, log_o, msg_o,
    wx, wbc, feat, state, d_state, logs,
):
    step = pl.program_id(0)
    heads = dt.shape[0]
    nst = cbc.shape[1] // 2

    @pl.when(step == 0)
    def _():
        state[...] = jnp.zeros_like(state)
        d_state[...] = jnp.zeros_like(d_state)
        logs[...] = jnp.zeros_like(logs)
        feat[...] = jnp.zeros_like(feat)

    load_window(wx, halo_x, pre_x, step == 0)
    load_window(wbc, halo_bc, pre_bc, step == 0)
    z = dt[...] + hpc[:, 0:1]
    rate = jnp.exp(hpc[:, 1:2])
    t_bias, t_lrate = hpc[:, 3:4], hpc[:, 4:5]
    size = jnp.maximum(z, 0.0) + jnp.log1p(jnp.exp(-jnp.abs(z)))
    sig = jax.nn.sigmoid(z)
    log_decay = -size * rate
    at_i = lax.broadcasted_iota(jnp.int32, (QB, QB), 1)
    at_j = lax.broadcasted_iota(jnp.int32, (QB, QB), 0)
    upper = jnp.where(at_j <= at_i, 1.0, 0.0).astype(F32)
    cumul = jnp.dot(log_decay, upper, precision=lax.Precision.HIGHEST, preferred_element_type=F32)
    sig_sum = jnp.dot(sig, upper, precision=lax.Precision.HIGHEST, preferred_element_type=F32)
    d_size = sig * t_bias
    d_cumul = cumul * t_lrate - rate * t_bias * sig_sum
    to_end = jnp.exp(cumul[:, QB - 1 : QB] - cumul)
    feat[S_ : S_ + heads] = size
    feat[DS_ : DS_ + heads] = d_size
    feat[C_ : C_ + heads] = cumul
    feat[DC_ : DC_ + heads] = d_cumul
    feat[CS_ : CS_ + heads] = sig_sum
    feat[SG_ : SG_ + heads] = sig
    feat[K_ : K_ + heads] = to_end * size
    feat[DK_ : DK_ + heads] = to_end * (
        d_size + size * (d_cumul[:, QB - 1 : QB] - d_cumul)
    )
    rows = feat[...]
    cols = rows.T
    row_o[...] = rows
    col_o[...] = cols

    bc, dbc, gbc = conv_pair(wbc, cbc, tcbc)
    bc_o[...] = bc
    dbc_o[...] = dbc
    gbc_o[...] = gbc
    x, dx, gx = conv_pair(wx, cx, tcx)
    x_o[...] = x
    dx_o[...] = dx
    gx_o[...] = gx

    last = cols[QB - 1 : QB, :]
    own = expand_all(last, C_, heads)
    d_own = expand_all(last, DC_, heads)
    sig_own = expand_all(last, CS_, heads)
    log_o[0, 0:1, :] = logs[0:1, :]
    log_o[0, 1:2, :] = logs[1:2, :]
    log_o[0, 2:3, :] = own
    log_o[0, 3:4, :] = d_own
    log_o[0, 4:5, :] = sig_own
    log_o[0, 5:8, :] = jnp.zeros((3, own.shape[1]), F32)
    logs[0:1, :] = logs[0:1, :] + own
    logs[1:2, :] = logs[1:2, :] + d_own

    st_o[0] = state[...]
    dst_o[0] = d_state[...]
    bt = bc[:, :nst].T
    dbt = dbc[:, :nst].T
    both = jnp.concatenate([bt, dbt], axis=1)
    both_h, both_l = split(both)
    for p in range(heads // 2):
        at = slice(128 * p, 128 * p + 128)
        k_x, dk_x = expand(cols, K_, p), expand(cols, DK_, p)
        ux = k_x * x[:, at]
        dux = k_x * dx[:, at] + dk_x * x[:, at]
        z_h, z_l = split(jnp.concatenate([dux, ux], axis=0))
        d_add = nn(both_h, z_h) + nn(both_h, z_l) + nn(both_l, z_h)
        b_h, b_l, u_h, u_l = both_h[:, :QB], both_l[:, :QB], z_h[QB:], z_l[QB:]
        add = nn(b_h, u_h) + nn(b_h, u_l) + nn(b_l, u_h)
        decay = jnp.exp(own[:, at])
        before = state[:, at]
        d_state[:, at] = decay * (d_state[:, at] + d_own[:, at] * before) + d_add
        state[:, at] = decay * before + add

    @pl.when(step == pl.num_programs(0) - 1)
    def _():
        parts = msg_o.shape[0]
        width = state.shape[1]
        msg_o[:, 0:8, :] = state[...].reshape(parts, 8, width)
        msg_o[:, 8:16, :] = d_state[...].reshape(parts, 8, width)
        msg_o[:, 16:24, :] = jnp.broadcast_to(logs[...][None], (parts, 8, width))


def first_call(pre_x, halo_x, pre_bc, halo_bc, dt, cx, tcx, cbc, tcbc, hpc, parts):
    length, width = pre_x.shape
    wide = pre_bc.shape[1]
    nst = wide // 2
    heads = dt.shape[0]
    count = length // QB
    whole = lambda a: pl.BlockSpec(a.shape, lambda i: (0,) * a.ndim)
    rows = lambda w: pl.BlockSpec((QB, w), lambda i: (i, 0))
    cube = lambda r: pl.BlockSpec((1, r, width), lambda i: (i, 0, 0))
    out = lambda *s: jax.ShapeDtypeStruct(s, F32)
    return pl.pallas_call(
        first_kernel,
        grid=(count,),
        in_specs=[
            rows(width), whole(halo_x), rows(wide), whole(halo_bc),
            pl.BlockSpec((heads, QB), lambda i: (0, i)),
            whole(cx), whole(tcx), whole(cbc), whole(tcbc), whole(hpc),
        ],
        out_specs=[rows(width)] * 3 + [rows(wide)] * 3 + [
            pl.BlockSpec((128, QB), lambda i: (0, i)),
            rows(128), cube(nst), cube(nst), cube(8),
            pl.BlockSpec((parts, 24, width), lambda i: (0, 0, 0)),
        ],
        out_shape=[out(length, width)] * 3 + [out(length, wide)] * 3 + [
            out(128, length), out(length, 128),
            out(count, nst, width), out(count, nst, width), out(count, 8, width),
            out(parts, 24, width),
        ],
        scratch_shapes=[
            pltpu.VMEM((QB + 8, width), F32), pltpu.VMEM((QB + 8, wide), F32),
            pltpu.VMEM((128, QB), F32), pltpu.VMEM((nst, width), F32),
            pltpu.VMEM((nst, width), F32), pltpu.VMEM((8, width), F32),
        ],
        compiler_params=pltpu.CompilerParams(vmem_limit_bytes=LIMIT),
        name="conv_and_states",
    )(pre_x, halo_x, pre_bc, halo_bc, dt, cx, tcx, cbc, tcbc, hpc)


def scan_kernel(count, forward, msg, result, landed, answer, send1, recv1, send2, recv2):
    me = lax.axis_index("seq")
    barrier = pltpu.get_barrier_semaphore()
    for k in range(1, count):
        pl.semaphore_signal(
            barrier, inc=1, device_id={"seq": lax.rem(me + k, count)}, device_id_type=MESH
        )
    pl.semaphore_wait(barrier, count - 1)
    first = []
    for k in range(1, count):
        to = lax.rem(me + k, count)
        copy = pltpu.make_async_remote_copy(
            src_ref=msg.at[to],
            dst_ref=landed.at[me],
            send_sem=send1.at[k],
            recv_sem=recv1.at[k],
            device_id={"seq": to},
            device_id_type=MESH,
        )
        copy.start()
        first.append(copy)
    landed[me] = msg[me]
    for copy in first:
        copy.wait()
    width = msg.shape[2]
    state = jnp.zeros((8, width), F32)
    d_state = jnp.zeros((8, width), F32)
    for i in range(count) if forward else range(count - 1, -1, -1):
        if forward:
            answer[i, 0:8] = state
            answer[i, 8:16] = d_state
            decay = jnp.exp(landed[i, 16:17])
            d_state = decay * (d_state + landed[i, 17:18] * state) + landed[i, 8:16]
        else:
            answer[i] = state
            decay = jnp.exp(landed[i, 8:9])
        state = decay * state + landed[i, 0:8]
    second = []
    for k in range(1, count):
        to = lax.rem(me + k, count)
        copy = pltpu.make_async_remote_copy(
            src_ref=answer.at[to],
            dst_ref=result.at[me],
            send_sem=send2.at[k],
            recv_sem=recv2.at[k],
            device_id={"seq": to},
            device_id_type=MESH,
        )
        copy.start()
        second.append(copy)
    result[me] = answer[me]
    for copy in second:
        copy.wait()


def scan_call(msg, forward, collective_id):
    parts, rows, width = msg.shape
    back = 16 if forward else 8
    vmem = pl.BlockSpec(memory_space=pltpu.VMEM)

    def kernel(*refs):
        scan_kernel(parts, forward, *refs)

    return pl.pallas_call(
        kernel,
        in_specs=[vmem],
        out_specs=vmem,
        out_shape=jax.ShapeDtypeStruct((parts, back, width), F32),
        scratch_shapes=[
            pltpu.VMEM((parts, rows, width), F32),
            pltpu.VMEM((parts, back, width), F32),
            pltpu.SemaphoreType.DMA((parts,)),
            pltpu.SemaphoreType.DMA((parts,)),
            pltpu.SemaphoreType.DMA((parts,)),
            pltpu.SemaphoreType.DMA((parts,)),
        ],
        compiler_params=pltpu.CompilerParams(
            collective_id=collective_id, has_side_effects=True, vmem_limit_bytes=LIMIT
        ),
        name="state_scan_forward" if forward else "state_scan_backward",
    )(msg)


def second_kernel(
    x, dx, bc, dbc, rowv, colv, st, dst, log, start, gate_z, dexp,
    gated_o, dgated_o, s0_o, sums_o,
):
    nst = bc.shape[1] // 2
    heads = x.shape[1] // HW
    b_mat, c_mat = bc[:, :nst], bc[:, nst:]
    db_mat, dc_mat = dbc[:, :nst], dbc[:, nst:]
    at_j = lax.broadcasted_iota(jnp.int32, (QB, QB), 1)
    at_i = lax.broadcasted_iota(jnp.int32, (QB, QB), 0)
    keep = at_i >= at_j
    inner = jnp.where(keep, nt3(c_mat, b_mat), 0.0)
    d_inner = jnp.where(
        keep,
        nt3(
            jnp.concatenate([dc_mat, c_mat], axis=1),
            jnp.concatenate([b_mat, db_mat], axis=1),
        ),
        0.0,
    )
    cols = colv[...]
    rows = rowv[...]
    mask = lane_mask()
    squares = jnp.zeros((QB, 128), F32)
    crossed = jnp.zeros((QB, 128), F32)
    for p in range(heads // 2):
        at = slice(128 * p, 128 * p + 128)
        reach = jnp.exp(log[0, 0:1, at])
        s_in = start[:, 0:8, at].reshape(nst, 128)
        ds_in = start[:, 8:16, at].reshape(nst, 128)
        s0 = st[0, :, at] + reach * s_in
        ds0 = dst[0, :, at] + reach * (ds_in + log[0, 1:2, at] * s_in)
        s0_o[0, :, at] = s0
        xp, dxp = x[:, at], dx[:, at]
        size, d_size = expand(cols, S_, p), expand(cols, DS_, p)
        u = size * xp
        du = size * dxp + d_size * xp
        z_h, z_l = split(jnp.concatenate([u, s0], axis=0))
        dz_h, dz_l = split(jnp.concatenate([du, ds0], axis=0))
        mats, d_mats = [], []
        for h in (2 * p, 2 * p + 1):
            c_col = bcast(cols, C_ + h)
            dc_col = bcast(cols, DC_ + h)
            c_row = rows[C_ + h : C_ + h + 1, :]
            dc_row = rows[DC_ + h : DC_ + h + 1, :]
            level = jnp.exp(jnp.minimum(c_col - c_row, 0.0))
            m = inner * level
            dm = d_inner * level + m * (dc_col - dc_row)
            lift = jnp.exp(c_col)
            e = lift * c_mat
            de = lift * dc_mat + dc_col * e
            mats.append(jnp.concatenate([m, e], axis=1))
            d_mats.append(jnp.concatenate([dm, de], axis=1))
        a_h, a_l = split(jnp.concatenate(mats, axis=0))
        da_h, da_l = split(jnp.concatenate(d_mats, axis=0))
        big = nn(a_h, jnp.concatenate([z_h, dz_h], axis=1))
        big = big + nn(a_h, jnp.concatenate([z_l, dz_l], axis=1))
        big = big + nn(a_l, jnp.concatenate([z_h, dz_h], axis=1))
        small = nn(da_h, jnp.concatenate([z_h, z_l], axis=1))
        low = nn(da_l, z_h)
        y2 = big[:, :128]
        dy2 = big[:, 128:] + small[:, :128] + small[:, 128:] + low
        skip, d_skip = dexp[0:1, at], dexp[1:2, at]
        y = jnp.where(mask, y2[:QB], y2[QB:]) + skip * xp
        dy = jnp.where(mask, dy2[:QB], dy2[QB:]) + skip * dxp + d_skip * xp
        gz = gate_z[:, at].astype(F32)
        gate = gz * jax.nn.sigmoid(gz)
        gated = y * gate
        dgated = dy * gate
        gated_o[:, at] = gated
        dgated_o[:, at] = dgated
        squares = squares + gated * gated
        crossed = crossed + 2.0 * gated * dgated
    sums_o[0:1, :] = jnp.sum(squares.T, axis=0, keepdims=True)
    sums_o[1:2, :] = jnp.sum(crossed.T, axis=0, keepdims=True)


def second_call(x, dx, bc, dbc, rowv, colv, st, dst, logs, start, gate_z, dexp):
    length, width = x.shape
    wide = bc.shape[1]
    nst = wide // 2
    count = length // QB
    whole = lambda a: pl.BlockSpec(a.shape, lambda i: (0,) * a.ndim)
    rows = lambda w: pl.BlockSpec((QB, w), lambda i: (i, 0))
    cube = lambda r: pl.BlockSpec((1, r, width), lambda i: (i, 0, 0))
    out = lambda *s: jax.ShapeDtypeStruct(s, F32)
    return pl.pallas_call(
        second_kernel,
        grid=(count,),
        in_specs=[
            rows(width), rows(width), rows(wide), rows(wide),
            pl.BlockSpec((128, QB), lambda i: (0, i)),
            rows(128), cube(nst), cube(nst), cube(8), whole(start), rows(width), whole(dexp),
        ],
        out_specs=[rows(width), rows(width), cube(nst), pl.BlockSpec((2, QB), lambda i: (0, i))],
        out_shape=[out(length, width), out(length, width), out(count, nst, width), out(2, length)],
        compiler_params=pltpu.CompilerParams(vmem_limit_bytes=LIMIT),
        name="outputs_and_tangents",
    )(x, dx, bc, dbc, rowv, colv, st, dst, logs, start, gate_z, dexp)


def third_kernel(by, bc, colv, log, lam_o, msg_o, state, total):
    step = pl.program_id(0)
    nst = bc.shape[1] // 2
    heads = by.shape[1] // HW

    @pl.when(step == 0)
    def _():
        state[...] = jnp.zeros_like(state)
        total[...] = jnp.zeros_like(total)

    lam_o[0] = state[...]
    cols = colv[...]
    ct_h, ct_l = split(bc[:, nst:].T)
    for p in range(heads // 2):
        at = slice(128 * p, 128 * p + 128)
        lifted = jnp.exp(expand(cols, C_, p)) * by[:, at]
        l_h, l_l = split(lifted)
        add = nn(ct_h, l_h) + nn(ct_h, l_l) + nn(ct_l, l_h)
        state[:, at] = jnp.exp(log[0, 2:3, at]) * state[:, at] + add
    total[0:1, :] = total[0:1, :] + log[0, 2:3, :]

    @pl.when(step == pl.num_programs(0) - 1)
    def _():
        parts = msg_o.shape[0]
        width = state.shape[1]
        msg_o[:, 0:8, :] = state[...].reshape(parts, 8, width)
        msg_o[:, 8:16, :] = jnp.broadcast_to(total[...][None], (parts, 8, width))


def third_call(by, bc, colv, logs, parts):
    length, width = by.shape
    wide = bc.shape[1]
    nst = wide // 2
    count = length // QB
    rows = lambda w: pl.BlockSpec((QB, w), lambda i: (count - 1 - i, 0))
    cube = lambda r: pl.BlockSpec((1, r, width), lambda i: (count - 1 - i, 0, 0))
    out = lambda *s: jax.ShapeDtypeStruct(s, F32)
    return pl.pallas_call(
        third_kernel,
        grid=(count,),
        in_specs=[rows(width), rows(wide), rows(128), cube(8)],
        out_specs=[cube(nst), pl.BlockSpec((parts, 16, width), lambda i: (0, 0, 0))],
        out_shape=[out(count, nst, width), out(parts, 16, width)],
        scratch_shapes=[pltpu.VMEM((nst, width), F32), pltpu.VMEM((8, width), F32)],
        compiler_params=pltpu.CompilerParams(vmem_limit_bytes=LIMIT),
        name="adjoint_states",
    )(by, bc, colv, logs)


def fold(a):
    return jnp.sum(a.reshape(a.shape[0] // 8, 8, a.shape[1]), axis=0)


def fourth_kernel(
    by, x, gx, pre_x, halo_x, bc, gbc, pre_bc, halo_bc, rowv, colv, s0_b, lam_b, log, last_log,
    s_end, dexp,
    gcx_o, gcbc_o, lane_o, head_o,
    wx, wbc,
):
    step = pl.program_id(0)
    nst = bc.shape[1] // 2
    heads = x.shape[1] // HW

    @pl.when(step == 0)
    def _():
        gcx_o[...] = jnp.zeros_like(gcx_o)
        gcbc_o[...] = jnp.zeros_like(gcbc_o)
        lane_o[...] = jnp.zeros_like(lane_o)
        head_o[...] = jnp.zeros_like(head_o)

    load_window(wx, halo_x, pre_x, step == 0)
    load_window(wbc, halo_bc, pre_bc, step == 0)
    b_mat, c_mat = bc[:, :nst], bc[:, nst:]
    at_i = lax.broadcasted_iota(jnp.int32, (QB, QB), 1)
    at_j = lax.broadcasted_iota(jnp.int32, (QB, QB), 0)
    keep = at_i >= at_j
    inner_t = jnp.where(keep, nt3(b_mat, c_mat), 0.0)
    cols = colv[...]
    rows = rowv[...]
    mask = lane_mask()
    back_inner_t = jnp.zeros((QB, QB), F32)
    back_b = jnp.zeros((QB, nst), F32)
    back_c = jnp.zeros((QB, nst), F32)
    for p in range(heads // 2):
        at = slice(128 * p, 128 * p + 128)
        own, sig_own = log[0, 2:3, at], log[0, 4:5, at]
        reach = jnp.exp(last_log[0, 0:1, at] + last_log[0, 2:3, at] - log[0, 0:1, at] - own)
        s1 = lam_b[0, :, at] + reach * s_end[:, :, at].reshape(nst, 128)
        s0 = s0_b[0, :, at]
        byp, xp = by[:, at], x[:, at]
        size = expand(cols, S_, p)
        u = size * xp
        rhs_h, rhs_l = split(jnp.concatenate([byp, s1], axis=0))
        u_h, u_l = split(
            jnp.concatenate([jnp.where(mask, u, 0.0), jnp.where(mask, 0.0, u)], axis=0)
        )
        y_h, y_l = split(
            jnp.concatenate([jnp.where(mask, byp, 0.0), jnp.where(mask, 0.0, byp)], axis=0)
        )
        s0_h, s0_l = split(s0)
        mt_tt = nt(u_h, rhs_h) + nt(u_h, rhs_l) + nt(u_l, rhs_h)
        v_all = nt(y_h, s0_h) + nt(y_h, s0_l) + nt(y_l, s0_h)
        mats = []
        for s in range(2):
            h = 2 * p + s
            c_col, cs_col = bcast(cols, C_ + h), bcast(cols, CS_ + h)
            c_row = rows[C_ + h : C_ + h + 1, :]
            cs_row = rows[CS_ + h : CS_ + h + 1, :]
            c_end, cs_end = c_row[:, QB - 1 : QB], cs_row[:, QB - 1 : QB]
            back_mt = mt_tt[s * QB : s * QB + QB, :QB]
            tt = mt_tt[s * QB : s * QB + QB, QB:]
            v = v_all[s * QB : s * QB + QB]
            diff = jnp.minimum(c_row - c_col, 0.0)
            level = jnp.exp(diff)
            back_inner_t = back_inner_t + level * back_mt
            m_t = inner_t * level
            prod = m_t * back_mt
            lifted = jnp.exp(c_col) * v
            back_c = back_c + lifted
            lc = lifted * c_mat
            left = c_end - c_col
            to_end = jnp.exp(left)
            tb = to_end * tt
            back_b = back_b + tb
            tbb = tb * b_mat
            head_o[h, 0] = head_o[h, 0] + fold(prod * diff + lc * c_col + tbb * left)
            head_o[h, 1] = head_o[h, 1] + fold(
                prod * (cs_row - cs_col) + lc * cs_col + tbb * (cs_end - cs_col)
            )
            mats.append(jnp.concatenate([m_t, to_end * b_mat], axis=1))
        a_h, a_l = split(jnp.concatenate(mats, axis=0))
        wide = nn(a_h, jnp.concatenate([rhs_h, rhs_l], axis=1))
        back_u2 = wide[:, :128] + wide[:, 128:] + nn(a_l, rhs_h)
        back_u = jnp.where(mask, back_u2[:QB], back_u2[QB:])
        back_x = back_u * size + dexp[0:1, at] * byp
        carried = jnp.sum(s1 * s0, axis=0, keepdims=True) * jnp.exp(own)
        through = jnp.sum(expand(cols, SG_, p) * (back_u * xp), axis=0, keepdims=True)
        lane_o[0:1, at] = lane_o[0:1, at] + through
        lane_o[1:2, at] = lane_o[1:2, at] + carried * own
        lane_o[2:3, at] = lane_o[2:3, at] + carried * sig_own
        lane_o[3:4, at] = lane_o[3:4, at] + jnp.sum(byp * xp, axis=0, keepdims=True)
        back_z = back_x * gx[:, at]
        for k in range(4):
            gcx_o[k : k + 1, at] = gcx_o[k : k + 1, at] + jnp.sum(
                back_z * wx[5 + k : 5 + k + QB, at], axis=0, keepdims=True
            )
    back_inner_t = jnp.where(keep, back_inner_t, 0.0)
    back_b = back_b + nn3(back_inner_t, c_mat)
    back_c = back_c + nn3(back_inner_t.T, b_mat)
    back_zbc = jnp.concatenate([back_b, back_c], axis=1) * gbc[...]
    for k in range(4):
        gcbc_o[k : k + 1, :] = gcbc_o[k : k + 1, :] + jnp.sum(
            back_zbc * wbc[5 + k : 5 + k + QB, :], axis=0, keepdims=True
        )


def fourth_call(
    by, x, gx, pre_x, halo_x, bc, gbc, pre_bc, halo_bc, rowv, colv, s0, lam, logs, s_end, dexp
):
    length, width = by.shape
    wide = bc.shape[1]
    nst = wide // 2
    heads = width // HW
    count = length // QB
    whole = lambda a: pl.BlockSpec(a.shape, lambda i: (0,) * a.ndim)
    rows = lambda w: pl.BlockSpec((QB, w), lambda i: (i, 0))
    cube = lambda r: pl.BlockSpec((1, r, width), lambda i: (i, 0, 0))
    out = lambda *s: jax.ShapeDtypeStruct(s, F32)
    fixed = lambda *s: pl.BlockSpec(s, lambda i: (0,) * len(s))
    return pl.pallas_call(
        fourth_kernel,
        grid=(count,),
        in_specs=[
            rows(width), rows(width), rows(width), rows(width), whole(halo_x),
            rows(wide), rows(wide), rows(wide), whole(halo_bc),
            pl.BlockSpec((128, QB), lambda i: (0, i)), rows(128),
            cube(nst), cube(nst), cube(8),
            pl.BlockSpec((1, 8, width), lambda i: (count - 1, 0, 0)),
            whole(s_end), whole(dexp),
        ],
        out_specs=[fixed(8, width), fixed(8, wide), fixed(8, width), fixed(heads, 2, 8, 128)],
        out_shape=[out(8, width), out(8, wide), out(8, width), out(heads, 2, 8, 128)],
        scratch_shapes=[pltpu.VMEM((QB + 8, width), F32), pltpu.VMEM((QB + 8, wide), F32)],
        compiler_params=pltpu.CompilerParams(vmem_limit_bytes=LIMIT),
        name="adjoint_gradients",
    )(by, x, gx, pre_x, halo_x, bc, gbc, pre_bc, halo_bc, rowv, colv, s0, lam, logs, logs, s_end, dexp)


def on_device(
    pre_x, pre_bc, gate_z, dt_raw, conv_x, conv_bc, head_params, norm_gain, w_out,
    t_conv_x, t_conv_bc, t_heads, t_gain, t_wout,
):
    count = lax.axis_size("seq")
    width = pre_x.shape[1]
    heads = dt_raw.shape[0]
    channels = width * lax.axis_size("head") * 1.0
    tails = jnp.concatenate([pre_x[-8:], pre_bc[-8:]], axis=1)
    tails = lax.ppermute(tails, "seq", [(i, i + 1) for i in range(count - 1)]).astype(F32)
    halo_x, halo_bc = tails[:, :width], tails[:, width:]
    t_wout_all = lax.all_gather(t_wout, "seq", axis=1, tiled=True)
    hpc = jnp.concatenate([head_params, t_heads], axis=0).T
    dexp = jnp.repeat(jnp.stack([head_params[2], t_heads[2]]), HW, axis=1)
    x, dx, gx, bc, dbc, gbc, rowv, colv, st, dst, logs, msg = first_call(
        pre_x, halo_x, pre_bc, halo_bc, dt_raw, conv_x, t_conv_x, conv_bc, t_conv_bc, hpc, count
    )
    start = scan_call(msg, True, 1)
    gated, d_gated, s0, sums = second_call(
        x, dx, bc, dbc, rowv, colv, st, dst, logs, start, gate_z, dexp
    )
    sums = lax.psum(sums, "head")
    inv_rms = lax.rsqrt(sums[0] / channels + 1e-05)
    d_inv = -0.5 * inv_rms**3 * sums[1] / channels
    normed = (gated * inv_rms[:, None] * norm_gain).astype(BF16)
    d_normed = (
        (d_gated * inv_rms[:, None] + gated * d_inv[:, None]) * norm_gain
        + gated * inv_rms[:, None] * t_gain
    ).astype(BF16)
    partial_out = nn(d_normed, w_out) + nn(normed, t_wout_all)
    probe_part = lax.psum_scatter(partial_out, "head", scatter_dimension=0, tiled=True)
    probe_out = lax.all_gather(probe_part.astype(BF16), "head", axis=0, tiled=True)
    gn_wout = lax.psum_scatter(nn(normed.T, probe_out), "seq", scatter_dimension=1, tiled=True)
    back_normed = nt(probe_out, w_out)
    gain_part = jnp.sum(back_normed * gated * inv_rms[:, None], axis=0)
    weighted = back_normed * norm_gain
    mixed = lax.psum(jnp.sum(weighted * gated, axis=1), "head")
    gate = jax.nn.silu(gate_z.astype(F32))
    back_y = (weighted * inv_rms[:, None] - gated * (inv_rms**3 * mixed / channels)[:, None]) * gate
    lam, msg_back = third_call(back_y, bc, colv, logs, count)
    s_end = scan_call(msg_back, False, 2)
    gcx, gcbc, lanes, head_sums = fourth_call(
        back_y, x, gx, pre_x, halo_x, bc, gbc, pre_bc, halo_bc, rowv, colv, s0, lam, logs, s_end, dexp
    )
    per_head = jnp.sum(lanes[:4].reshape(4, heads, HW), axis=2)
    through_c = jnp.sum(head_sums, axis=(2, 3))
    log_rate = per_head[1] + through_c[:, 0]
    rate = jnp.exp(head_params[1])
    bias = per_head[0] - rate * (per_head[2] + through_c[:, 1])
    gn_heads = jnp.stack([bias, log_rate, per_head[3]])
    gn_conv_x, gn_heads, gn_gain = lax.psum((gcx[:4], gn_heads, gain_part), "seq")
    gn_conv_bc = lax.psum(gcbc[:4], ("seq", "head"))
    return (gn_conv_x, gn_conv_bc, gn_heads, gn_gain, gn_wout)


def solution(mesh):
    in_specs = (
        P("seq", "head"), P("seq", None), P("seq", "head"), P("head", "seq"), P(None, "head"),
        P(), P(None, "head"), P("head"), P("head", None), P(None, "head"), P(), P(None, "head"),
        P("head"), P("head", "seq"),
    )
    out_specs = (P(None, "head"), P(), P(None, "head"), P("head"), P("head", "seq"))
    return jax.shard_map(
        on_device, mesh=mesh, in_specs=in_specs, out_specs=out_specs, check_vma=False
    )
```

```python
import jax
import jax.numpy as jnp
from jax import lax
from jax.experimental import pallas as pl
from jax.experimental.pallas import tpu as pltpu
from jax.sharding import PartitionSpec as P

QB = 128
HW = 64
F32 = jnp.float32
BF16 = jnp.bfloat16
MESH = pl.DeviceIdType.MESH
S_, DS_, C_, DC_, CS_, SG_, K_, DK_ = (16 * i for i in range(8))
LIMIT = 50 * 1024 * 1024


def split(a):
    high = a.astype(BF16)
    return high, (a - high.astype(F32)).astype(BF16)


def nn(a, b):
    return jnp.dot(a, b, preferred_element_type=F32)


def nt(a, b):
    return lax.dot_general(a, b, (((1,), (1,)), ((), ())), preferred_element_type=F32)


def nn3(a, b):
    (ah, al), (bh, bl) = split(a), split(b)
    return nn(ah, bh) + nn(ah, bl) + nn(al, bh)


def nt3(a, b):
    (ah, al), (bh, bl) = split(a), split(b)
    return nt(ah, bh) + nt(ah, bl) + nt(al, bh)


def lane_mask():
    return lax.broadcasted_iota(jnp.int32, (1, 128), 1) < HW


def bcast(cols, at):
    return jnp.broadcast_to(cols[:, at : at + 1], (cols.shape[0], 128))


def expand(cols, base, pair):
    return jnp.where(
        lane_mask(), bcast(cols, base + 2 * pair), bcast(cols, base + 2 * pair + 1)
    )


def expand_all(cols, base, heads):
    return jnp.concatenate([expand(cols, base, p) for p in range(heads // 2)], axis=1)


def load_window(window, halo, block, first):
    @pl.when(first)
    def _():
        window[0:8] = halo[...]

    @pl.when(jnp.logical_not(first))
    def _():
        window[0:8] = window[QB : QB + 8]

    window[8 : QB + 8] = block[...].astype(F32)


def conv_pair(window, weight, t_weight):
    z = jnp.zeros((QB, window.shape[1]), F32)
    dz = jnp.zeros((QB, window.shape[1]), F32)
    for k in range(4):
        rows = window[5 + k : 5 + k + QB, :]
        z = z + weight[k : k + 1, :] * rows
        dz = dz + t_weight[k : k + 1, :] * rows
    sig = jax.nn.sigmoid(z)
    slope = sig * (1.0 + z * (1.0 - sig))
    return z * sig, slope * dz, slope


def first_kernel(
    pre_x, halo_x, pre_bc, halo_bc, dt, cx, tcx, cbc, tcbc, hpc,
    x_o, dx_o, gx_o, bc_o, dbc_o, gbc_o, row_o, col_o, st_o, dst_o, log_o, msg_o, tile_o,
    wx, wbc, feat, state, d_state, logs,
):
    step = pl.program_id(0)
    heads = dt.shape[0]
    nst = cbc.shape[1] // 2

    @pl.when(step == 0)
    def _():
        state[...] = jnp.zeros_like(state)
        d_state[...] = jnp.zeros_like(d_state)
        logs[...] = jnp.zeros_like(logs)
        feat[...] = jnp.zeros_like(feat)
        tile_o[...] = jnp.zeros_like(tile_o)

    load_window(wx, halo_x, pre_x, step == 0)
    load_window(wbc, halo_bc, pre_bc, step == 0)
    z = dt[...] + hpc[:, 0:1]
    rate = jnp.exp(hpc[:, 1:2])
    t_bias, t_lrate = hpc[:, 3:4], hpc[:, 4:5]
    size = jnp.maximum(z, 0.0) + jnp.log1p(jnp.exp(-jnp.abs(z)))
    sig = jax.nn.sigmoid(z)
    log_decay = -size * rate
    at_i = lax.broadcasted_iota(jnp.int32, (QB, QB), 1)
    at_j = lax.broadcasted_iota(jnp.int32, (QB, QB), 0)
    upper = jnp.where(at_j <= at_i, 1.0, 0.0).astype(F32)
    cumul = jnp.dot(log_decay, upper, precision=lax.Precision.HIGHEST, preferred_element_type=F32)
    sig_sum = jnp.dot(sig, upper, precision=lax.Precision.HIGHEST, preferred_element_type=F32)
    d_size = sig * t_bias
    d_cumul = cumul * t_lrate - rate * t_bias * sig_sum
    to_end = jnp.exp(cumul[:, QB - 1 : QB] - cumul)
    feat[S_ : S_ + heads] = size
    feat[DS_ : DS_ + heads] = d_size
    feat[C_ : C_ + heads] = cumul
    feat[DC_ : DC_ + heads] = d_cumul
    feat[CS_ : CS_ + heads] = sig_sum
    feat[SG_ : SG_ + heads] = sig
    feat[K_ : K_ + heads] = to_end * size
    feat[DK_ : DK_ + heads] = to_end * (
        d_size + size * (d_cumul[:, QB - 1 : QB] - d_cumul)
    )
    rows = feat[...]
    cols = rows.T
    row_o[...] = rows
    col_o[...] = cols

    bc, dbc, gbc = conv_pair(wbc, cbc, tcbc)
    bc_o[...] = bc
    dbc_o[...] = dbc
    gbc_o[...] = gbc
    x, dx, gx = conv_pair(wx, cx, tcx)
    x_o[...] = x
    dx_o[...] = dx
    gx_o[...] = gx

    last = cols[QB - 1 : QB, :]
    tile_o[0:1, :] = tile_o[0:1, :] + last
    own = expand_all(last, C_, heads)
    d_own = expand_all(last, DC_, heads)
    sig_own = expand_all(last, CS_, heads)
    log_o[0, 0:1, :] = logs[0:1, :]
    log_o[0, 1:2, :] = logs[1:2, :]
    log_o[0, 2:3, :] = own
    log_o[0, 3:4, :] = d_own
    log_o[0, 4:5, :] = sig_own
    log_o[0, 5:8, :] = jnp.zeros((3, own.shape[1]), F32)
    logs[0:1, :] = logs[0:1, :] + own
    logs[1:2, :] = logs[1:2, :] + d_own

    st_o[0] = state[...]
    dst_o[0] = d_state[...]
    bt = bc[:, :nst].T
    dbt = dbc[:, :nst].T
    both = jnp.concatenate([bt, dbt], axis=1)
    both_h, both_l = split(both)
    for p in range(heads // 2):
        at = slice(128 * p, 128 * p + 128)
        k_x, dk_x = expand(cols, K_, p), expand(cols, DK_, p)
        ux = k_x * x[:, at]
        dux = k_x * dx[:, at] + dk_x * x[:, at]
        z_h, z_l = split(jnp.concatenate([dux, ux], axis=0))
        d_add = nn(both_h, z_h) + nn(both_h, z_l) + nn(both_l, z_h)
        b_h, b_l, u_h, u_l = both_h[:, :QB], both_l[:, :QB], z_h[QB:], z_l[QB:]
        add = nn(b_h, u_h) + nn(b_h, u_l) + nn(b_l, u_h)
        decay = jnp.exp(own[:, at])
        before = state[:, at]
        d_state[:, at] = decay * (d_state[:, at] + d_own[:, at] * before) + d_add
        state[:, at] = decay * before + add

    @pl.when(step == pl.num_programs(0) - 1)
    def _():
        parts = msg_o.shape[0]
        width = state.shape[1]
        msg_o[:, 0:8, :] = state[...].reshape(parts, 8, width)
        msg_o[:, 8:16, :] = d_state[...].reshape(parts, 8, width)


def first_call(pre_x, halo_x, pre_bc, halo_bc, dt, cx, tcx, cbc, tcbc, hpc, parts):
    length, width = pre_x.shape
    wide = pre_bc.shape[1]
    nst = wide // 2
    heads = dt.shape[0]
    count = length // QB
    whole = lambda a: pl.BlockSpec(a.shape, lambda i: (0,) * a.ndim)
    rows = lambda w: pl.BlockSpec((QB, w), lambda i: (i, 0))
    cube = lambda r: pl.BlockSpec((1, r, width), lambda i: (i, 0, 0))
    out = lambda *s: jax.ShapeDtypeStruct(s, F32)
    return pl.pallas_call(
        first_kernel,
        grid=(count,),
        in_specs=[
            rows(width), whole(halo_x), rows(wide), whole(halo_bc),
            pl.BlockSpec((heads, QB), lambda i: (0, i)),
            whole(cx), whole(tcx), whole(cbc), whole(tcbc), whole(hpc),
        ],
        out_specs=[rows(width)] * 3 + [rows(wide)] * 3 + [
            pl.BlockSpec((128, QB), lambda i: (0, i)),
            rows(128), cube(nst), cube(nst), cube(8),
            pl.BlockSpec((parts, 16, width), lambda i: (0, 0, 0)),
            pl.BlockSpec((8, 128), lambda i: (0, 0)),
        ],
        out_shape=[out(length, width)] * 3 + [out(length, wide)] * 3 + [
            out(128, length), out(length, 128),
            out(count, nst, width), out(count, nst, width), out(count, 8, width),
            out(parts, 16, width), out(8, 128),
        ],
        scratch_shapes=[
            pltpu.VMEM((QB + 8, width), F32), pltpu.VMEM((QB + 8, wide), F32),
            pltpu.VMEM((128, QB), F32), pltpu.VMEM((nst, width), F32),
            pltpu.VMEM((nst, width), F32), pltpu.VMEM((8, width), F32),
        ],
        compiler_params=pltpu.CompilerParams(vmem_limit_bytes=LIMIT),
        name="conv_and_states",
    )(pre_x, halo_x, pre_bc, halo_bc, dt, cx, tcx, cbc, tcbc, hpc)


def greet(peers):
    barrier = pltpu.get_barrier_semaphore()
    for peer in peers:
        pl.semaphore_signal(barrier, inc=1, device_id=peer, device_id_type=MESH)
    pl.semaphore_wait(barrier, len(peers))


def others(axis, count):
    me = lax.axis_index(axis)
    return [lax.rem(me + k, count) for k in range(1, count)]


def send(src, dst, send_sem, recv_sem, device):
    copy = pltpu.make_async_remote_copy(
        src_ref=src, dst_ref=dst, send_sem=send_sem, recv_sem=recv_sem,
        device_id=device, device_id_type=MESH,
    )
    copy.start()
    return copy


def scan_forward_kernel(
    msg, tile, result, decay_o, landed, tiles, answer, send0, recv0, send1, recv1, send2, recv2
):
    count = msg.shape[0]
    width = msg.shape[2]
    heads = width // HW
    me = lax.axis_index("seq")
    peers = others("seq", count)
    greet([{"seq": to} for to in peers])
    copies = []
    for k, to in enumerate(peers):
        at = {"seq": to}
        copies.append(send(tile, tiles.at[me], send0.at[k], recv0.at[k], at))
        copies.append(send(msg.at[to], landed.at[me], send1.at[k], recv1.at[k], at))
    landed[me] = msg[me]
    tiles[me] = tile[...]
    for copy in copies:
        copy.wait()
    state = jnp.zeros((8, width), F32)
    d_state = jnp.zeros((8, width), F32)
    for i in range(count):
        answer[i, 0:8] = state
        answer[i, 8:16] = d_state
        features = tiles[i, 0:1, :]
        decay = jnp.exp(expand_all(features, C_, heads))
        decay_o[i : i + 1, :] = decay
        d_state = decay * (d_state + expand_all(features, DC_, heads) * state)
        d_state = d_state + landed[i, 8:16]
        state = decay * state + landed[i, 0:8]
    copies = []
    for k, to in enumerate(peers):
        copies.append(
            send(answer.at[to], result.at[me], send2.at[k], recv2.at[k], {"seq": to})
        )
    result[me] = answer[me]
    for copy in copies:
        copy.wait()


def scan_backward_kernel(msg, decays, result, landed, answer, send1, recv1, send2, recv2):
    count = msg.shape[0]
    width = msg.shape[2]
    me = lax.axis_index("seq")
    peers = others("seq", count)
    greet([{"seq": to} for to in peers])
    copies = []
    for k, to in enumerate(peers):
        copies.append(send(msg.at[to], landed.at[me], send1.at[k], recv1.at[k], {"seq": to}))
    landed[me] = msg[me]
    for copy in copies:
        copy.wait()
    state = jnp.zeros((8, width), F32)
    for i in range(count - 1, -1, -1):
        answer[i] = state
        state = decays[i : i + 1, :] * state + landed[i]
    copies = []
    for k, to in enumerate(peers):
        copies.append(
            send(answer.at[to], result.at[me], send2.at[k], recv2.at[k], {"seq": to})
        )
    result[me] = answer[me]
    for copy in copies:
        copy.wait()


VMEM = pl.BlockSpec(memory_space=pltpu.VMEM)


def scan_forward(msg, tile):
    parts, rows, width = msg.shape
    sems = [pltpu.SemaphoreType.DMA((parts,))] * 6
    return pl.pallas_call(
        scan_forward_kernel,
        in_specs=[VMEM] * 2,
        out_specs=[VMEM] * 2,
        out_shape=[
            jax.ShapeDtypeStruct((parts, rows, width), F32),
            jax.ShapeDtypeStruct((parts, width), F32),
        ],
        scratch_shapes=[
            pltpu.VMEM((parts, rows, width), F32),
            pltpu.VMEM((parts, 8, 128), F32),
            pltpu.VMEM((parts, rows, width), F32),
        ]
        + sems,
        compiler_params=pltpu.CompilerParams(
            collective_id=1, has_side_effects=True, vmem_limit_bytes=LIMIT
        ),
        name="state_scan_forward",
    )(msg, tile)


def scan_backward(msg, decays):
    parts, rows, width = msg.shape
    sems = [pltpu.SemaphoreType.DMA((parts,))] * 4
    return pl.pallas_call(
        scan_backward_kernel,
        in_specs=[VMEM] * 2,
        out_specs=VMEM,
        out_shape=jax.ShapeDtypeStruct((parts, rows, width), F32),
        scratch_shapes=[pltpu.VMEM((parts, rows, width), F32)] * 2 + sems,
        compiler_params=pltpu.CompilerParams(
            collective_id=2, has_side_effects=True, vmem_limit_bytes=LIMIT
        ),
        name="state_scan_backward",
    )(msg, decays)


def middle_kernel(
    gated, dgated, sums, gate_z, w, tw, gain, tgain,
    by_o, gnw_o, gain_o,
    got, scal, both, part, sib, far_src, far_dst, out_src, out_dst, probe, back, mix, mix_got,
    sums_s, sums_r, sib_s, sib_r, far_s, far_r, out_s, out_r, ag_s, ag_r, mix_s, mix_r,
):
    length, width = gated.shape
    cols = w.shape[1]
    half = cols // 2
    groups = width // 128
    channels = width * 8.0
    head = lax.axis_index("head")
    mine = head // 2
    core = lax.rem(head, 2)
    right, left, far = (lax.rem(mine + k, 4) for k in (1, 3, 2))
    device = lambda chip, c: {"head": chip * 2 + c}
    to_right, to_left, to_sib = device(right, core), device(left, core), device(mine, 1 - core)
    peers = others("head", 8)
    greet([{"head": to} for to in peers])
    copies = []
    for k, to in enumerate(peers):
        copies.append(send(sums, got.at[head], sums_s.at[k], sums_r.at[k], {"head": to}))
    got[head] = sums[...]
    gain_o[...] = jnp.zeros_like(gain_o)
    for copy in copies:
        copy.wait()
    total = got[0]
    for i in range(1, 8):
        total = total + got[i]
    inv = lax.rsqrt(total[0:1] / channels + 1e-05)
    scal[0:1] = inv
    scal[1:2] = -0.5 * inv * inv * inv * total[1:2] / channels

    def column(row, start):
        at = pl.ds(pl.multiple_of(start, 128), 128)
        return jnp.broadcast_to(scal[row : row + 1, at], (128, 128)).T

    def compute(index, chip):
        slot = index % 2
        for c in range(2):
            start = pl.multiple_of(chip * 256 + c * 128, 128)
            rows = pl.ds(start, 128)
            inv_c, d_inv_c = column(0, start), column(1, start)
            for g in range(groups):
                at = slice(128 * g, 128 * g + 128)
                gt, dgt = gated[rows, at], dgated[rows, at]
                ga = gain[:, at]
                scaled = gt * inv_c
                normed = scaled * ga
                d_normed = (dgt * inv_c + gt * d_inv_c) * ga + scaled * tgain[:, at]
                both[rows, at] = d_normed.astype(BF16)
                both[rows, width + 128 * g : width + 128 * g + 128] = normed.astype(BF16)
        rows = pl.ds(pl.multiple_of(chip * 256, 256), 256)

        def tile(i, carry):
            at = pl.ds(pl.multiple_of(i * 512, 512), 512)
            res = nn(both[rows, 0:width], w[:, at]) + nn(both[rows, width:], tw[:, at])
            part[slot, 0, :, at] = res[:128]
            part[slot, 1, :, at] = res[128:]
            return carry

        lax.fori_loop(0, cols // 512, tile, 0)
        return send(
            part.at[slot, 1 - core], sib.at[index], sib_s.at[index], sib_r.at[index], to_sib
        )

    def pair(index, h):
        at = slice(half * h, half * h + half)
        return part[index % 2, core, :, at] + sib[index, :, at]

    first = compute(0, far)
    second = compute(1, right)
    first.wait()
    far_src[0] = pair(0, 0).astype(BF16)
    far_src[1] = pair(0, 1).astype(BF16)
    far_l = send(far_src.at[0], far_dst.at[0], far_s.at[0], far_r.at[0], to_right)
    far_rt = send(far_src.at[1], far_dst.at[1], far_s.at[1], far_r.at[1], to_left)
    third = compute(2, left)
    second.wait()
    out_src[0, 1] = pair(1, 1).astype(BF16)
    out_rr = send(out_src.at[0, 1], out_dst.at[0, 1], out_s.at[0], out_r.at[0], to_right)
    far_l.wait()
    out_src[0, 0] = (pair(1, 0) + far_dst[0].astype(F32)).astype(BF16)
    out_rl = send(out_src.at[0, 0], out_dst.at[0, 0], out_s.at[1], out_r.at[1], to_right)
    fourth = compute(3, mine)
    third.wait()
    out_src[1, 0] = pair(2, 0).astype(BF16)
    out_ll = send(out_src.at[1, 0], out_dst.at[1, 0], out_s.at[2], out_r.at[2], to_left)
    far_rt.wait()
    out_src[1, 1] = (pair(2, 1) + far_dst[1].astype(F32)).astype(BF16)
    out_lr = send(out_src.at[1, 1], out_dst.at[1, 1], out_s.at[3], out_r.at[3], to_left)
    fourth.wait()
    for copy in (out_rr, out_rl, out_ll, out_lr):
        copy.wait()

    def chunk(chip, c):
        return pl.ds(pl.multiple_of(chip * 256 + c * 128, 128), 128)

    own = chunk(mine, core)
    for h in range(2):
        res = pair(3, h) + out_dst[0, h].astype(F32) + out_dst[1, h].astype(F32)
        probe[own, half * h : half * h + half] = res.astype(BF16)

    def pass_on(slot, chip, h, device):
        if h is None:
            ref = probe.at[chunk(chip, core), :]
        else:
            ref = probe.at[chunk(chip, core), half * h : half * h + half]
        return send(ref, ref, ag_s.at[slot], ag_r.at[slot], device)

    go_right = pass_on(0, mine, None, to_right)
    go_left = pass_on(1, mine, None, to_left)
    sib_own = pass_on(2, mine, None, to_sib)

    def back_product(chip):
        rows = pl.ds(pl.multiple_of(chip * 256, 256), 256)
        for lo, hi in ((0, 256), (256, 512), (512, 640)):
            back[rows, lo:hi] = nt(probe[rows, :], w[lo:hi, :])

        def tile(i, carry):
            at = pl.ds(pl.multiple_of(i * 512, 512), 512)
            gnw_o[:, at] = carry + lax.dot_general(
                both[rows, width:],
                probe[rows, at],
                (((0,), (0,)), ((), ())),
                preferred_element_type=F32,
            )
            return carry

        def tile_add(i, carry):
            at = pl.ds(pl.multiple_of(i * 512, 512), 512)
            gnw_o[:, at] = gnw_o[:, at] + lax.dot_general(
                both[rows, width:],
                probe[rows, at],
                (((0,), (0,)), ((), ())),
                preferred_element_type=F32,
            )
            return carry

        lax.fori_loop(0, cols // 512, tile if chip is mine else tile_add, 0.0 if chip is mine else 0)
        for c in range(2):
            start = pl.multiple_of(chip * 256 + c * 128, 128)
            rows = pl.ds(start, 128)
            inv_c = column(0, start)
            mixed = jnp.zeros((128, 128), F32)
            for g in range(groups):
                at = slice(128 * g, 128 * g + 128)
                prod = back[rows, at] * gated[rows, at]
                gain_o[:, at] = gain_o[:, at] + fold(prod * inv_c)
                mixed = mixed + prod * gain[:, at]
            mix[pl.ds(chip * 2 + c, 1), :] = jnp.sum(mixed.T, axis=0, keepdims=True)

    sib_own.wait()
    back_product(mine)
    go_right.wait()
    fwd_l = pass_on(3, left, 0, to_right)
    sib_left = pass_on(4, left, None, to_sib)
    go_left.wait()
    fwd_r = pass_on(5, right, 1, to_left)
    sib_right = pass_on(6, right, None, to_sib)
    sib_left.wait()
    back_product(left)
    fwd_l.wait()
    sib_far_l = pass_on(7, far, 0, to_sib)
    fwd_r.wait()
    sib_far_r = pass_on(8, far, 1, to_sib)
    sib_right.wait()
    back_product(right)
    sib_far_l.wait()
    sib_far_r.wait()
    back_product(far)
    copies = []
    for k, to in enumerate(peers):
        copies.append(send(mix, mix_got.at[head], mix_s.at[k], mix_r.at[k], {"head": to}))
    mix_got[head] = mix[...]
    for copy in copies:
        copy.wait()
    total = mix_got[0]
    for i in range(1, 8):
        total = total + mix_got[i]
    mix[...] = total / channels

    def finish(i, carry):
        start = pl.multiple_of(i * 128, 128)
        rows = pl.ds(start, 128)
        inv_c = column(0, start)
        mixed_c = jnp.broadcast_to(mix[pl.ds(i, 1), :], (128, 128)).T * (inv_c * inv_c * inv_c)
        for g in range(groups):
            at = slice(128 * g, 128 * g + 128)
            gz = gate_z[rows, at].astype(F32)
            gate = gz * jax.nn.sigmoid(gz)
            by_o[rows, at] = (
                back[rows, at] * gain[:, at] * inv_c - gated[rows, at] * mixed_c
            ) * gate
        return carry

    lax.fori_loop(0, length // 128, finish, 0)


def middle_call(gated, dgated, sums, gate_z, w, tw, gain, tgain):
    length, width = gated.shape
    cols = w.shape[1]
    half = cols // 2
    out = lambda *s: jax.ShapeDtypeStruct(s, F32)
    dma = pltpu.SemaphoreType.DMA
    return pl.pallas_call(
        middle_kernel,
        in_specs=[VMEM] * 8,
        out_specs=[VMEM] * 3,
        out_shape=[out(length, width), out(width, cols), out(8, width)],
        scratch_shapes=[
            pltpu.VMEM((8, 2, length), F32),
            pltpu.VMEM((8, length), F32),
            pltpu.VMEM((length, 2 * width), BF16),
            pltpu.VMEM((2, 2, 128, cols), F32),
            pltpu.VMEM((4, 128, cols), F32),
            pltpu.VMEM((2, 128, half), BF16),
            pltpu.VMEM((2, 128, half), BF16),
            pltpu.VMEM((2, 2, 128, half), BF16),
            pltpu.VMEM((2, 2, 128, half), BF16),
            pltpu.VMEM((length, cols), BF16),
            pltpu.VMEM((length, width), F32),
            pltpu.VMEM((8, 128), F32),
            pltpu.VMEM((8, 8, 128), F32),
            dma((8,)), dma((8,)), dma((4,)), dma((4,)), dma((2,)), dma((2,)),
            dma((4,)), dma((4,)), dma((9,)), dma((9,)), dma((8,)), dma((8,)),
        ],
        compiler_params=pltpu.CompilerParams(
            collective_id=3, has_side_effects=True, vmem_limit_bytes=60 * 1024 * 1024
        ),
        name="probe_and_back",
    )(gated, dgated, sums, gate_z, w, tw, gain, tgain)


def final_kernel(
    pack, hp, gcx_o, gcbc_o, heads_o, gain_o, landed, part, landed2, send1, recv1, send2, recv2
):
    count, n_head = landed.shape[0], landed2.shape[0]
    width = pack.shape[1]
    heads = hp.shape[1]
    me, head = lax.axis_index("seq"), lax.axis_index("head")
    seq_peers, head_peers = others("seq", count), others("head", n_head)
    greet([{"seq": to} for to in seq_peers] + [{"head": to} for to in head_peers])
    copies = []
    for k, to in enumerate(seq_peers):
        copies.append(send(pack, landed.at[me], send1.at[k], recv1.at[k], {"seq": to}))
    landed[me] = pack[...]
    for copy in copies:
        copy.wait()
    total = landed[0]
    for i in range(1, count):
        total = total + landed[i]
    part[...] = total[8:16, 0:256]
    copies = []
    for k, to in enumerate(head_peers):
        copies.append(send(part, landed2.at[head], send2.at[k], recv2.at[k], {"head": to}))
    landed2[head] = part[...]
    gcx_o[...] = total[0:4]
    gain_o[...] = total[8:9]
    at = lax.broadcasted_iota(jnp.int32, (width, 128), 0)
    to = lax.broadcasted_iota(jnp.int32, (width, 128), 1) * HW
    pick = jnp.where((at >= to) & (at < to + HW), 1.0, 0.0).astype(F32)
    sums = jnp.dot(
        total, pick, precision=lax.Precision.HIGHEST, preferred_element_type=F32
    )[:, :heads]
    heads_o[0:1] = sums[4:5] - jnp.exp(hp[1:2]) * sums[6:7]
    heads_o[1:2] = sums[5:6]
    heads_o[2:3] = sums[7:8]
    for copy in copies:
        copy.wait()
    total2 = landed2[0]
    for i in range(1, n_head):
        total2 = total2 + landed2[i]
    gcbc_o[...] = total2[1:5]


def final_call(pack, head_params, count, n_head):
    width = pack.shape[1]
    heads = head_params.shape[1]
    out = lambda *s: jax.ShapeDtypeStruct(s, F32)
    dma = pltpu.SemaphoreType.DMA
    return pl.pallas_call(
        final_kernel,
        in_specs=[VMEM] * 2,
        out_specs=[VMEM] * 4,
        out_shape=[out(4, width), out(4, 256), out(3, heads), out(1, width)],
        scratch_shapes=[
            pltpu.VMEM((count, 16, width), F32),
            pltpu.VMEM((8, 256), F32),
            pltpu.VMEM((n_head, 8, 256), F32),
            dma((count,)), dma((count,)), dma((n_head,)), dma((n_head,)),
        ],
        compiler_params=pltpu.CompilerParams(
            collective_id=4, has_side_effects=True, vmem_limit_bytes=LIMIT
        ),
        name="final_sums",
    )(pack, head_params)


def second_kernel(
    x, dx, bc, dbc, rowv, colv, st, dst, log, start, gate_z, dexp,
    gated_o, dgated_o, s0_o, sums_o,
):
    nst = bc.shape[1] // 2
    heads = x.shape[1] // HW
    b_mat, c_mat = bc[:, :nst], bc[:, nst:]
    db_mat, dc_mat = dbc[:, :nst], dbc[:, nst:]
    at_j = lax.broadcasted_iota(jnp.int32, (QB, QB), 1)
    at_i = lax.broadcasted_iota(jnp.int32, (QB, QB), 0)
    keep = at_i >= at_j
    inner = jnp.where(keep, nt3(c_mat, b_mat), 0.0)
    d_inner = jnp.where(
        keep,
        nt3(
            jnp.concatenate([dc_mat, c_mat], axis=1),
            jnp.concatenate([b_mat, db_mat], axis=1),
        ),
        0.0,
    )
    cols = colv[...]
    rows = rowv[...]
    mask = lane_mask()
    squares = jnp.zeros((QB, 128), F32)
    crossed = jnp.zeros((QB, 128), F32)
    for p in range(heads // 2):
        at = slice(128 * p, 128 * p + 128)
        reach = jnp.exp(log[0, 0:1, at])
        s_in = start[:, 0:8, at].reshape(nst, 128)
        ds_in = start[:, 8:16, at].reshape(nst, 128)
        s0 = st[0, :, at] + reach * s_in
        ds0 = dst[0, :, at] + reach * (ds_in + log[0, 1:2, at] * s_in)
        s0_o[0, :, at] = s0
        xp, dxp = x[:, at], dx[:, at]
        size, d_size = expand(cols, S_, p), expand(cols, DS_, p)
        u = size * xp
        du = size * dxp + d_size * xp
        z_h, z_l = split(jnp.concatenate([u, s0], axis=0))
        dz_h, dz_l = split(jnp.concatenate([du, ds0], axis=0))
        mats, d_mats = [], []
        for h in (2 * p, 2 * p + 1):
            c_col = bcast(cols, C_ + h)
            dc_col = bcast(cols, DC_ + h)
            c_row = rows[C_ + h : C_ + h + 1, :]
            dc_row = rows[DC_ + h : DC_ + h + 1, :]
            level = jnp.exp(jnp.minimum(c_col - c_row, 0.0))
            m = inner * level
            dm = d_inner * level + m * (dc_col - dc_row)
            lift = jnp.exp(c_col)
            e = lift * c_mat
            de = lift * dc_mat + dc_col * e
            mats.append(jnp.concatenate([m, e], axis=1))
            d_mats.append(jnp.concatenate([dm, de], axis=1))
        a_h, a_l = split(jnp.concatenate(mats, axis=0))
        da_h, da_l = split(jnp.concatenate(d_mats, axis=0))
        big = nn(a_h, jnp.concatenate([z_h, dz_h], axis=1))
        big = big + nn(a_h, jnp.concatenate([z_l, dz_l], axis=1))
        big = big + nn(a_l, jnp.concatenate([z_h, dz_h], axis=1))
        small = nn(da_h, jnp.concatenate([z_h, z_l], axis=1))
        low = nn(da_l, z_h)
        y2 = big[:, :128]
        dy2 = big[:, 128:] + small[:, :128] + small[:, 128:] + low
        skip, d_skip = dexp[0:1, at], dexp[1:2, at]
        y = jnp.where(mask, y2[:QB], y2[QB:]) + skip * xp
        dy = jnp.where(mask, dy2[:QB], dy2[QB:]) + skip * dxp + d_skip * xp
        gz = gate_z[:, at].astype(F32)
        gate = gz * jax.nn.sigmoid(gz)
        gated = y * gate
        dgated = dy * gate
        gated_o[:, at] = gated
        dgated_o[:, at] = dgated
        squares = squares + gated * gated
        crossed = crossed + 2.0 * gated * dgated
    sums_o[0:1, :] = jnp.sum(squares.T, axis=0, keepdims=True)
    sums_o[1:2, :] = jnp.sum(crossed.T, axis=0, keepdims=True)


def second_call(x, dx, bc, dbc, rowv, colv, st, dst, logs, start, gate_z, dexp):
    length, width = x.shape
    wide = bc.shape[1]
    nst = wide // 2
    count = length // QB
    whole = lambda a: pl.BlockSpec(a.shape, lambda i: (0,) * a.ndim)
    rows = lambda w: pl.BlockSpec((QB, w), lambda i: (i, 0))
    cube = lambda r: pl.BlockSpec((1, r, width), lambda i: (i, 0, 0))
    out = lambda *s: jax.ShapeDtypeStruct(s, F32)
    return pl.pallas_call(
        second_kernel,
        grid=(count,),
        in_specs=[
            rows(width), rows(width), rows(wide), rows(wide),
            pl.BlockSpec((128, QB), lambda i: (0, i)),
            rows(128), cube(nst), cube(nst), cube(8), whole(start), rows(width), whole(dexp),
        ],
        out_specs=[rows(width), rows(width), cube(nst), pl.BlockSpec((2, QB), lambda i: (0, i))],
        out_shape=[out(length, width), out(length, width), out(count, nst, width), out(2, length)],
        compiler_params=pltpu.CompilerParams(vmem_limit_bytes=LIMIT),
        name="outputs_and_tangents",
    )(x, dx, bc, dbc, rowv, colv, st, dst, logs, start, gate_z, dexp)


def third_kernel(by, bc, colv, log, lam_o, msg_o, state):
    step = pl.program_id(0)
    nst = bc.shape[1] // 2
    heads = by.shape[1] // HW

    @pl.when(step == 0)
    def _():
        state[...] = jnp.zeros_like(state)

    lam_o[0] = state[...]
    cols = colv[...]
    ct_h, ct_l = split(bc[:, nst:].T)
    for p in range(heads // 2):
        at = slice(128 * p, 128 * p + 128)
        lifted = jnp.exp(expand(cols, C_, p)) * by[:, at]
        l_h, l_l = split(lifted)
        add = nn(ct_h, l_h) + nn(ct_h, l_l) + nn(ct_l, l_h)
        state[:, at] = jnp.exp(log[0, 2:3, at]) * state[:, at] + add

    @pl.when(step == pl.num_programs(0) - 1)
    def _():
        parts = msg_o.shape[0]
        width = state.shape[1]
        msg_o[...] = state[...].reshape(parts, 8, width)


def third_call(by, bc, colv, logs, parts):
    length, width = by.shape
    wide = bc.shape[1]
    nst = wide // 2
    count = length // QB
    rows = lambda w: pl.BlockSpec((QB, w), lambda i: (count - 1 - i, 0))
    cube = lambda r: pl.BlockSpec((1, r, width), lambda i: (count - 1 - i, 0, 0))
    out = lambda *s: jax.ShapeDtypeStruct(s, F32)
    return pl.pallas_call(
        third_kernel,
        grid=(count,),
        in_specs=[rows(width), rows(wide), rows(128), cube(8)],
        out_specs=[cube(nst), pl.BlockSpec((parts, 8, width), lambda i: (0, 0, 0))],
        out_shape=[out(count, nst, width), out(parts, 8, width)],
        scratch_shapes=[pltpu.VMEM((nst, width), F32)],
        compiler_params=pltpu.CompilerParams(vmem_limit_bytes=LIMIT),
        name="adjoint_states",
    )(by, bc, colv, logs)


def fold(a):
    return jnp.sum(a.reshape(a.shape[0] // 8, 8, a.shape[1]), axis=0)


def fourth_kernel(
    by, x, gx, pre_x, halo_x, bc, gbc, pre_bc, halo_bc, rowv, colv, s0_b, lam_b, log, last_log,
    s_end, dexp, gain,
    pack_o,
    wx, wbc, head_o,
):
    step = pl.program_id(0)
    nst = bc.shape[1] // 2
    heads = x.shape[1] // HW

    @pl.when(step == 0)
    def _():
        pack_o[...] = jnp.zeros_like(pack_o)
        pack_o[8:9, :] = jnp.sum(gain[...], axis=0, keepdims=True)
        head_o[...] = jnp.zeros_like(head_o)

    load_window(wx, halo_x, pre_x, step == 0)
    load_window(wbc, halo_bc, pre_bc, step == 0)
    b_mat, c_mat = bc[:, :nst], bc[:, nst:]
    at_i = lax.broadcasted_iota(jnp.int32, (QB, QB), 1)
    at_j = lax.broadcasted_iota(jnp.int32, (QB, QB), 0)
    keep = at_i >= at_j
    inner_t = jnp.where(keep, nt3(b_mat, c_mat), 0.0)
    cols = colv[...]
    rows = rowv[...]
    mask = lane_mask()
    back_inner_t = jnp.zeros((QB, QB), F32)
    back_b = jnp.zeros((QB, nst), F32)
    back_c = jnp.zeros((QB, nst), F32)
    for p in range(heads // 2):
        at = slice(128 * p, 128 * p + 128)
        own, sig_own = log[0, 2:3, at], log[0, 4:5, at]
        reach = jnp.exp(last_log[0, 0:1, at] + last_log[0, 2:3, at] - log[0, 0:1, at] - own)
        s1 = lam_b[0, :, at] + reach * s_end[:, :, at].reshape(nst, 128)
        s0 = s0_b[0, :, at]
        byp, xp = by[:, at], x[:, at]
        size = expand(cols, S_, p)
        u = size * xp
        rhs_h, rhs_l = split(jnp.concatenate([byp, s1], axis=0))
        u_h, u_l = split(
            jnp.concatenate([jnp.where(mask, u, 0.0), jnp.where(mask, 0.0, u)], axis=0)
        )
        y_h, y_l = split(
            jnp.concatenate([jnp.where(mask, byp, 0.0), jnp.where(mask, 0.0, byp)], axis=0)
        )
        s0_h, s0_l = split(s0)
        mt_tt = nt(u_h, rhs_h) + nt(u_h, rhs_l) + nt(u_l, rhs_h)
        v_all = nt(y_h, s0_h) + nt(y_h, s0_l) + nt(y_l, s0_h)
        mats = []
        for s in range(2):
            h = 2 * p + s
            c_col, cs_col = bcast(cols, C_ + h), bcast(cols, CS_ + h)
            c_row = rows[C_ + h : C_ + h + 1, :]
            cs_row = rows[CS_ + h : CS_ + h + 1, :]
            c_end, cs_end = c_row[:, QB - 1 : QB], cs_row[:, QB - 1 : QB]
            back_mt = mt_tt[s * QB : s * QB + QB, :QB]
            tt = mt_tt[s * QB : s * QB + QB, QB:]
            v = v_all[s * QB : s * QB + QB]
            diff = jnp.minimum(c_row - c_col, 0.0)
            level = jnp.exp(diff)
            back_inner_t = back_inner_t + level * back_mt
            m_t = inner_t * level
            prod = m_t * back_mt
            lifted = jnp.exp(c_col) * v
            back_c = back_c + lifted
            lc = lifted * c_mat
            left = c_end - c_col
            to_end = jnp.exp(left)
            tb = to_end * tt
            back_b = back_b + tb
            tbb = tb * b_mat
            head_o[h, 0] = head_o[h, 0] + fold(prod * diff + lc * c_col + tbb * left)
            head_o[h, 1] = head_o[h, 1] + fold(
                prod * (cs_row - cs_col) + lc * cs_col + tbb * (cs_end - cs_col)
            )
            mats.append(jnp.concatenate([m_t, to_end * b_mat], axis=1))
        a_h, a_l = split(jnp.concatenate(mats, axis=0))
        wide = nn(a_h, jnp.concatenate([rhs_h, rhs_l], axis=1))
        back_u2 = wide[:, :128] + wide[:, 128:] + nn(a_l, rhs_h)
        back_u = jnp.where(mask, back_u2[:QB], back_u2[QB:])
        back_x = back_u * size + dexp[0:1, at] * byp
        carried = jnp.sum(s1 * s0, axis=0, keepdims=True) * jnp.exp(own)
        through = jnp.sum(expand(cols, SG_, p) * (back_u * xp), axis=0, keepdims=True)
        pack_o[4:5, at] = pack_o[4:5, at] + through
        pack_o[5:6, at] = pack_o[5:6, at] + carried * own
        pack_o[6:7, at] = pack_o[6:7, at] + carried * sig_own
        pack_o[7:8, at] = pack_o[7:8, at] + jnp.sum(byp * xp, axis=0, keepdims=True)
        back_z = back_x * gx[:, at]
        for k in range(4):
            pack_o[k : k + 1, at] = pack_o[k : k + 1, at] + jnp.sum(
                back_z * wx[5 + k : 5 + k + QB, at], axis=0, keepdims=True
            )
    back_inner_t = jnp.where(keep, back_inner_t, 0.0)
    back_b = back_b + nn3(back_inner_t, c_mat)
    back_c = back_c + nn3(back_inner_t.T, b_mat)
    back_zbc = jnp.concatenate([back_b, back_c], axis=1) * gbc[...]
    for k in range(4):
        pack_o[9 + k : 10 + k, 0 : 2 * nst] = pack_o[9 + k : 10 + k, 0 : 2 * nst] + jnp.sum(
            back_zbc * wbc[5 + k : 5 + k + QB, :], axis=0, keepdims=True
        )

    @pl.when(step == pl.num_programs(0) - 1)
    def _():
        for p in range(heads // 2):
            at = slice(128 * p, 128 * p + 128)
            for kind in range(2):
                even, odd = head_o[2 * p, kind], head_o[2 * p + 1, kind]
                even = even + pltpu.roll(even, HW, 1)
                odd = odd + pltpu.roll(odd, HW, 1)
                both = jnp.sum(jnp.where(mask, even, odd), axis=0, keepdims=True)
                pack_o[5 + kind : 6 + kind, at] = pack_o[5 + kind : 6 + kind, at] + both


def fourth_call(
    by, x, gx, pre_x, halo_x, bc, gbc, pre_bc, halo_bc, rowv, colv, s0, lam, logs, s_end, dexp,
    gain,
):
    length, width = by.shape
    wide = bc.shape[1]
    nst = wide // 2
    heads = width // HW
    count = length // QB
    whole = lambda a: pl.BlockSpec(a.shape, lambda i: (0,) * a.ndim)
    rows = lambda w: pl.BlockSpec((QB, w), lambda i: (i, 0))
    cube = lambda r: pl.BlockSpec((1, r, width), lambda i: (i, 0, 0))
    out = lambda *s: jax.ShapeDtypeStruct(s, F32)
    fixed = lambda *s: pl.BlockSpec(s, lambda i: (0,) * len(s))
    return pl.pallas_call(
        fourth_kernel,
        grid=(count,),
        in_specs=[
            rows(width), rows(width), rows(width), rows(width), whole(halo_x),
            rows(wide), rows(wide), rows(wide), whole(halo_bc),
            pl.BlockSpec((128, QB), lambda i: (0, i)), rows(128),
            cube(nst), cube(nst), cube(8),
            pl.BlockSpec((1, 8, width), lambda i: (count - 1, 0, 0)),
            whole(s_end), whole(dexp), whole(gain),
        ],
        out_specs=fixed(16, width),
        out_shape=out(16, width),
        scratch_shapes=[
            pltpu.VMEM((QB + 8, width), F32), pltpu.VMEM((QB + 8, wide), F32),
            pltpu.VMEM((heads, 2, 8, 128), F32),
        ],
        compiler_params=pltpu.CompilerParams(vmem_limit_bytes=LIMIT),
        name="adjoint_gradients",
    )(by, x, gx, pre_x, halo_x, bc, gbc, pre_bc, halo_bc, rowv, colv, s0, lam, logs, logs, s_end, dexp, gain)


def on_device(
    pre_x, pre_bc, gate_z, dt_raw, conv_x, conv_bc, head_params, norm_gain, w_out,
    t_conv_x, t_conv_bc, t_heads, t_gain, t_wout,
):
    count = lax.axis_size("seq")
    width = pre_x.shape[1]
    heads = dt_raw.shape[0]
    channels = width * lax.axis_size("head") * 1.0
    tails = jnp.concatenate([pre_x[-8:], pre_bc[-8:]], axis=1)
    tails = lax.ppermute(tails, "seq", [(i, i + 1) for i in range(count - 1)]).astype(F32)
    halo_x, halo_bc = tails[:, :width], tails[:, width:]
    t_wout_all = lax.all_gather(t_wout, "seq", axis=1, tiled=True)
    hpc = jnp.concatenate([head_params, t_heads], axis=0).T
    dexp = jnp.repeat(jnp.stack([head_params[2], t_heads[2]]), HW, axis=1)
    x, dx, gx, bc, dbc, gbc, rowv, colv, st, dst, logs, msg, tile = first_call(
        pre_x, halo_x, pre_bc, halo_bc, dt_raw, conv_x, t_conv_x, conv_bc, t_conv_bc, hpc, count
    )
    start, decays = scan_forward(msg, tile)
    gated, d_gated, s0, sums = second_call(
        x, dx, bc, dbc, rowv, colv, st, dst, logs, start, gate_z, dexp
    )
    back_y, gnw, gain_part = middle_call(
        gated, d_gated, sums, gate_z, w_out, t_wout_all, norm_gain[None], t_gain[None]
    )
    gn_wout = lax.psum_scatter(gnw, "seq", scatter_dimension=1, tiled=True)
    lam, msg_back = third_call(back_y, bc, colv, logs, count)
    s_end = scan_backward(msg_back, decays)
    pack = fourth_call(
        back_y, x, gx, pre_x, halo_x, bc, gbc, pre_bc, halo_bc, rowv, colv, s0, lam, logs, s_end, dexp,
        gain_part,
    )
    gn_conv_x, gn_conv_bc, gn_heads, gn_gain = final_call(
        pack, head_params, count, lax.axis_size("head")
    )
    return (gn_conv_x, gn_conv_bc, gn_heads, gn_gain[0], gn_wout)


def solution(mesh):
    in_specs = (
        P("seq", "head"), P("seq", None), P("seq", "head"), P("head", "seq"), P(None, "head"),
        P(), P(None, "head"), P("head"), P("head", None), P(None, "head"), P(), P(None, "head"),
        P("head"), P("head", "seq"),
    )
    out_specs = (P(None, "head"), P(), P(None, "head"), P("head"), P("head", "seq"))
    return jax.shard_map(
        on_device, mesh=mesh, in_specs=in_specs, out_specs=out_specs, check_vma=False
    )
```

```python
import jax
import jax.numpy as jnp
from jax import lax
from jax.experimental import pallas as pl
from jax.experimental.pallas import tpu as pltpu
from jax.sharding import PartitionSpec as P

QB = 128
HW = 64
F32 = jnp.float32
BF16 = jnp.bfloat16
MESH = pl.DeviceIdType.MESH
S_, DS_, C_, DC_, CS_, SG_, K_, DK_ = (16 * i for i in range(8))
LIMIT = 50 * 1024 * 1024


def split(a):
    high = a.astype(BF16)
    return high, (a - high.astype(F32)).astype(BF16)


def nn(a, b):
    return jnp.dot(a, b, preferred_element_type=F32)


def nt(a, b):
    return lax.dot_general(a, b, (((1,), (1,)), ((), ())), preferred_element_type=F32)


def nn3(a, b):
    (ah, al), (bh, bl) = split(a), split(b)
    return nn(ah, bh) + nn(ah, bl) + nn(al, bh)


def nt3(a, b):
    (ah, al), (bh, bl) = split(a), split(b)
    return nt(ah, bh) + nt(ah, bl) + nt(al, bh)


def lane_mask():
    return lax.broadcasted_iota(jnp.int32, (1, 128), 1) < HW


def bcast(cols, at):
    return jnp.broadcast_to(cols[:, at : at + 1], (cols.shape[0], 128))


def expand(cols, base, pair):
    return jnp.where(
        lane_mask(), bcast(cols, base + 2 * pair), bcast(cols, base + 2 * pair + 1)
    )


def expand_all(cols, base, heads):
    return jnp.concatenate([expand(cols, base, p) for p in range(heads // 2)], axis=1)


def load_window(window, halo, block, first):
    @pl.when(first)
    def _():
        window[0:8] = halo[...]

    @pl.when(jnp.logical_not(first))
    def _():
        window[0:8] = window[QB : QB + 8]

    window[8 : QB + 8] = block[...].astype(F32)


def conv_pair(window, weight, t_weight):
    z = jnp.zeros((QB, window.shape[1]), F32)
    dz = jnp.zeros((QB, window.shape[1]), F32)
    for k in range(4):
        rows = window[5 + k : 5 + k + QB, :]
        z = z + weight[k : k + 1, :] * rows
        dz = dz + t_weight[k : k + 1, :] * rows
    sig = jax.nn.sigmoid(z)
    slope = sig * (1.0 + z * (1.0 - sig))
    return z * sig, slope * dz, slope


def first_kernel(
    pre_x, halo_x, pre_bc, halo_bc, dt, cx, tcx, cbc, tcbc, hpc,
    x_o, dx_o, gx_o, bc_o, dbc_o, gbc_o, row_o, col_o, st_o, dst_o, log_o, msg_o, tile_o,
    wx, wbc, feat, state, d_state, logs,
):
    step = pl.program_id(0)
    heads = dt.shape[0]
    nst = cbc.shape[1] // 2

    @pl.when(step == 0)
    def _():
        state[...] = jnp.zeros_like(state)
        d_state[...] = jnp.zeros_like(d_state)
        logs[...] = jnp.zeros_like(logs)
        feat[...] = jnp.zeros_like(feat)
        tile_o[...] = jnp.zeros_like(tile_o)

    load_window(wx, halo_x, pre_x, step == 0)
    load_window(wbc, halo_bc, pre_bc, step == 0)
    z = dt[...] + hpc[:, 0:1]
    rate = jnp.exp(hpc[:, 1:2])
    t_bias, t_lrate = hpc[:, 3:4], hpc[:, 4:5]
    size = jnp.maximum(z, 0.0) + jnp.log1p(jnp.exp(-jnp.abs(z)))
    sig = jax.nn.sigmoid(z)
    log_decay = -size * rate
    at_i = lax.broadcasted_iota(jnp.int32, (QB, QB), 1)
    at_j = lax.broadcasted_iota(jnp.int32, (QB, QB), 0)
    upper = jnp.where(at_j <= at_i, 1.0, 0.0).astype(F32)
    cumul = jnp.dot(log_decay, upper, precision=lax.Precision.HIGHEST, preferred_element_type=F32)
    sig_sum = jnp.dot(sig, upper, precision=lax.Precision.HIGHEST, preferred_element_type=F32)
    d_size = sig * t_bias
    d_cumul = cumul * t_lrate - rate * t_bias * sig_sum
    to_end = jnp.exp(cumul[:, QB - 1 : QB] - cumul)
    feat[S_ : S_ + heads] = size
    feat[DS_ : DS_ + heads] = d_size
    feat[C_ : C_ + heads] = cumul
    feat[DC_ : DC_ + heads] = d_cumul
    feat[CS_ : CS_ + heads] = sig_sum
    feat[SG_ : SG_ + heads] = sig
    feat[K_ : K_ + heads] = to_end * size
    feat[DK_ : DK_ + heads] = to_end * (
        d_size + size * (d_cumul[:, QB - 1 : QB] - d_cumul)
    )
    rows = feat[...]
    cols = rows.T
    row_o[...] = rows
    col_o[...] = cols

    bc, dbc, gbc = conv_pair(wbc, cbc, tcbc)
    bc_o[...] = bc
    dbc_o[...] = dbc
    gbc_o[...] = gbc
    x, dx, gx = conv_pair(wx, cx, tcx)
    x_o[...] = x
    dx_o[...] = dx
    gx_o[...] = gx

    last = cols[QB - 1 : QB, :]
    tile_o[0:1, :] = tile_o[0:1, :] + last
    own = expand_all(last, C_, heads)
    d_own = expand_all(last, DC_, heads)
    sig_own = expand_all(last, CS_, heads)
    log_o[0, 0:1, :] = logs[0:1, :]
    log_o[0, 1:2, :] = logs[1:2, :]
    log_o[0, 2:3, :] = own
    log_o[0, 3:4, :] = d_own
    log_o[0, 4:5, :] = sig_own
    log_o[0, 5:8, :] = jnp.zeros((3, own.shape[1]), F32)
    logs[0:1, :] = logs[0:1, :] + own
    logs[1:2, :] = logs[1:2, :] + d_own

    st_o[0] = state[...]
    dst_o[0] = d_state[...]
    bt = bc[:, :nst].T
    dbt = dbc[:, :nst].T
    both = jnp.concatenate([bt, dbt], axis=1)
    both_h, both_l = split(both)
    for p in range(heads // 2):
        at = slice(128 * p, 128 * p + 128)
        k_x, dk_x = expand(cols, K_, p), expand(cols, DK_, p)
        ux = k_x * x[:, at]
        dux = k_x * dx[:, at] + dk_x * x[:, at]
        z_h, z_l = split(jnp.concatenate([dux, ux], axis=0))
        d_add = nn(both_h, z_h) + nn(both_h, z_l) + nn(both_l, z_h)
        b_h, b_l, u_h, u_l = both_h[:, :QB], both_l[:, :QB], z_h[QB:], z_l[QB:]
        add = nn(b_h, u_h) + nn(b_h, u_l) + nn(b_l, u_h)
        decay = jnp.exp(own[:, at])
        before = state[:, at]
        d_state[:, at] = decay * (d_state[:, at] + d_own[:, at] * before) + d_add
        state[:, at] = decay * before + add

    @pl.when(step == pl.num_programs(0) - 1)
    def _():
        parts = msg_o.shape[0]
        width = state.shape[1]
        msg_o[:, 0:8, :] = state[...].reshape(parts, 8, width)
        msg_o[:, 8:16, :] = d_state[...].reshape(parts, 8, width)


def first_call(pre_x, halo_x, pre_bc, halo_bc, dt, cx, tcx, cbc, tcbc, hpc, parts):
    length, width = pre_x.shape
    wide = pre_bc.shape[1]
    nst = wide // 2
    heads = dt.shape[0]
    count = length // QB
    whole = lambda a: pl.BlockSpec(a.shape, lambda i: (0,) * a.ndim)
    rows = lambda w: pl.BlockSpec((QB, w), lambda i: (i, 0))
    cube = lambda r: pl.BlockSpec((1, r, width), lambda i: (i, 0, 0))
    out = lambda *s: jax.ShapeDtypeStruct(s, F32)
    return pl.pallas_call(
        first_kernel,
        grid=(count,),
        in_specs=[
            rows(width), whole(halo_x), rows(wide), whole(halo_bc),
            pl.BlockSpec((heads, QB), lambda i: (0, i)),
            whole(cx), whole(tcx), whole(cbc), whole(tcbc), whole(hpc),
        ],
        out_specs=[rows(width)] * 3 + [rows(wide)] * 3 + [
            pl.BlockSpec((128, QB), lambda i: (0, i)),
            rows(128), cube(nst), cube(nst), cube(8),
            pl.BlockSpec((parts, 16, width), lambda i: (0, 0, 0)),
            pl.BlockSpec((8, 128), lambda i: (0, 0)),
        ],
        out_shape=[out(length, width)] * 3 + [out(length, wide)] * 3 + [
            out(128, length), out(length, 128),
            out(count, nst, width), out(count, nst, width), out(count, 8, width),
            out(parts, 16, width), out(8, 128),
        ],
        scratch_shapes=[
            pltpu.VMEM((QB + 8, width), F32), pltpu.VMEM((QB + 8, wide), F32),
            pltpu.VMEM((128, QB), F32), pltpu.VMEM((nst, width), F32),
            pltpu.VMEM((nst, width), F32), pltpu.VMEM((8, width), F32),
        ],
        compiler_params=pltpu.CompilerParams(vmem_limit_bytes=LIMIT),
        name="conv_and_states",
    )(pre_x, halo_x, pre_bc, halo_bc, dt, cx, tcx, cbc, tcbc, hpc)


def greet(peers):
    barrier = pltpu.get_barrier_semaphore()
    for peer in peers:
        pl.semaphore_signal(barrier, inc=1, device_id=peer, device_id_type=MESH)
    pl.semaphore_wait(barrier, len(peers))


def others(axis, count):
    me = lax.axis_index(axis)
    return [lax.rem(me + k, count) for k in range(1, count)]


def link(src, dst, send_sem, recv_sem, device):
    return pltpu.make_async_remote_copy(
        src_ref=src, dst_ref=dst, send_sem=send_sem, recv_sem=recv_sem,
        device_id=device, device_id_type=MESH,
    )


def send(*what):
    copy = link(*what)
    copy.start()
    return copy


def scan_forward_kernel(
    msg, tile, result, decay_o, landed, tiles, answer, send0, recv0, send1, recv1, send2, recv2
):
    count = msg.shape[0]
    width = msg.shape[2]
    heads = width // HW
    me = lax.axis_index("seq")
    peers = others("seq", count)
    greet([{"seq": to} for to in peers])
    copies = []
    for k, to in enumerate(peers):
        at = {"seq": to}
        copies.append(send(tile, tiles.at[me], send0.at[k], recv0.at[k], at))
        copies.append(send(msg.at[to], landed.at[me], send1.at[k], recv1.at[k], at))
    landed[me] = msg[me]
    tiles[me] = tile[...]
    for copy in copies:
        copy.wait()
    state = jnp.zeros((8, width), F32)
    d_state = jnp.zeros((8, width), F32)
    for i in range(count):
        answer[i, 0:8] = state
        answer[i, 8:16] = d_state
        features = tiles[i, 0:1, :]
        decay = jnp.exp(expand_all(features, C_, heads))
        decay_o[i : i + 1, :] = decay
        d_state = decay * (d_state + expand_all(features, DC_, heads) * state)
        d_state = d_state + landed[i, 8:16]
        state = decay * state + landed[i, 0:8]
    copies = []
    for k, to in enumerate(peers):
        copies.append(
            send(answer.at[to], result.at[me], send2.at[k], recv2.at[k], {"seq": to})
        )
    result[me] = answer[me]
    for copy in copies:
        copy.wait()


VMEM = pl.BlockSpec(memory_space=pltpu.VMEM)


def scan_forward(msg, tile):
    parts, rows, width = msg.shape
    sems = [pltpu.SemaphoreType.DMA((parts,))] * 6
    return pl.pallas_call(
        scan_forward_kernel,
        in_specs=[VMEM] * 2,
        out_specs=[VMEM] * 2,
        out_shape=[
            jax.ShapeDtypeStruct((parts, rows, width), F32),
            jax.ShapeDtypeStruct((parts, width), F32),
        ],
        scratch_shapes=[
            pltpu.VMEM((parts, rows, width), F32),
            pltpu.VMEM((parts, 8, 128), F32),
            pltpu.VMEM((parts, rows, width), F32),
        ]
        + sems,
        compiler_params=pltpu.CompilerParams(
            collective_id=1, has_side_effects=True, vmem_limit_bytes=LIMIT
        ),
        name="state_scan_forward",
    )(msg, tile)


def middle_kernel(
    gated, dgated, sums, gate_z, w, tw, gain, tgain,
    by_o, gain_o, sum_z_o, sum_y_o,
    got, scal, both, part, sib, far_src, far_dst, out_src, out_dst, probe, back, gnw, got_z, got_y,
    mix, mix_got,
    sums_s, sums_r, sib_s, sib_r, far_s, far_r, out_s, out_r, ag_s, ag_r, mix_s, mix_r,
    az_s, az_r, ay_s, ay_r,
):
    length, width = gated.shape
    blocks, _, blk = probe.shape
    groups = width // 128
    channels = width * 8.0
    head = lax.axis_index("head")
    me = lax.axis_index("seq")
    my_y, my_z = me // 4, lax.rem(me, 4)
    mine = head // 2
    core = lax.rem(head, 2)
    right, left, far = (lax.rem(mine + k, 4) for k in (1, 3, 2))
    device = lambda chip, c: {"head": chip * 2 + c}
    to_right, to_left, to_sib = device(right, core), device(left, core), device(mine, 1 - core)
    y_peers = [{"seq": lax.rem(my_y + k, 4) * 4 + my_z} for k in range(1, 4)]
    z_peers = [{"seq": my_y * 4 + lax.rem(my_z + k, 4)} for k in range(1, 4)]
    peers = others("head", 8)
    greet([{"head": to} for to in peers] + y_peers + z_peers)
    copies = []
    for k, to in enumerate(peers):
        copies.append(send(sums, got.at[head], sums_s.at[k], sums_r.at[k], {"head": to}))
    got[head] = sums[...]
    gain_o[...] = jnp.zeros_like(gain_o)
    for copy in copies:
        copy.wait()
    total = got[0]
    for i in range(1, 8):
        total = total + got[i]
    inv = lax.rsqrt(total[0:1] / channels + 1e-05)
    scal[0:1] = inv
    scal[1:2] = -0.5 * inv * inv * inv * total[1:2] / channels

    def column(row, start):
        at = pl.ds(pl.multiple_of(start, 128), 128)
        return jnp.broadcast_to(scal[row : row + 1, at], (128, 128)).T

    def norm(i, carry):
        start = pl.multiple_of(i * 128, 128)
        rows = pl.ds(start, 128)
        inv_c, d_inv_c = column(0, start), column(1, start)
        for g in range(groups):
            at = slice(128 * g, 128 * g + 128)
            gt, dgt = gated[rows, at], dgated[rows, at]
            ga = gain[:, at]
            scaled = gt * inv_c
            normed = scaled * ga
            d_normed = (dgt * inv_c + gt * d_inv_c) * ga + scaled * tgain[:, at]
            both[rows, at] = d_normed.astype(BF16)
            both[rows, width + 128 * g : width + 128 * g + 128] = normed.astype(BF16)
        return carry

    lax.fori_loop(0, length // 128, norm, 0)

    def columns(i):
        return pl.ds(pl.multiple_of(lax.rem(my_y + 1 + i, 4) * blk, 128), blk)

    def compute(i):
        slot, at = i % 2, columns(i)

        res = nn(both[:, 0:width], w[:, at]) + nt(both[:, width:], tw[at, :])
        part[slot] = res.reshape(4, 2, 128, blk)
        return send(part.at[slot, :, 1 - core], sib.at[i], sib_s.at[i], sib_r.at[i], to_sib)

    def pairs(i, copy):
        copy.wait()
        for chip in range(4):
            sib[i, chip] = sib[i, chip] + part[i % 2, chip, core]
        way, near = (to_right, to_left) if i % 2 == 0 else (to_left, to_right)
        near_chip = left if i % 2 == 0 else right
        far_src[i] = sib[i, far].astype(BF16)
        transit = send(far_src.at[i], far_dst.at[i], far_s.at[i], far_r.at[i], way)
        out_src[i, 0] = sib[i, near_chip].astype(BF16)
        direct = send(out_src.at[i, 0], out_dst.at[i, 0], out_s.at[i, 0], out_r.at[i, 0], near)
        return transit, direct

    def through(i, transit):
        transit.wait()
        way, chip = (to_right, right) if i % 2 == 0 else (to_left, left)
        out_src[i, 1] = (sib[i, chip] + far_dst[i].astype(F32)).astype(BF16)
        return send(out_src.at[i, 1], out_dst.at[i, 1], out_s.at[i, 1], out_r.at[i, 1], way)

    def pass_on(i, slot, chip, to):
        ref = probe.at[i, pl.ds(pl.multiple_of(chip * 256 + core * 128, 128), 128), :]
        return send(ref, ref, ag_s.at[i, slot], ag_r.at[i, slot], to)

    def own(i, direct, joined):
        direct.wait()
        joined.wait()
        rows = pl.ds(pl.multiple_of(mine * 256 + core * 128, 128), 128)
        res = sib[i, mine] + out_dst[i, 0].astype(F32) + out_dst[i, 1].astype(F32)
        probe[i, rows, :] = res.astype(BF16)
        go_right = pass_on(i, 0, mine, to_right)
        go_left = pass_on(i, 1, mine, to_left)
        return go_right, go_left, pass_on(i, 2, mine, to_sib)

    def forward(i, go_right, go_left):
        if i % 2 == 0:
            go_right.wait()
            onward = pass_on(i, 3, left, to_right)
            go_left.wait()
        else:
            go_left.wait()
            onward = pass_on(i, 3, right, to_left)
            go_right.wait()
        return onward, pass_on(i, 4, left, to_sib), pass_on(i, 5, right, to_sib)

    def last_hop(i, onward):
        onward.wait()
        return pass_on(i, 6, far, to_sib)

    def back_block(i, waits):
        for copy in waits:
            copy.wait()
        at = columns(i)
        gnw[i] = lax.dot_general(
            probe[i], both[:, width:], (((0,), (0,)), ((), ())), preferred_element_type=F32
        ).reshape(4, blk // 4, width)
        half = blk // 8
        sent = []
        for k in (2, 1, 3):
            z = lax.rem(my_z + k, 4)
            sent.append(
                send(
                    gnw.at[i, z, 0:half, :], got_z.at[i, k - 1],
                    az_s.at[i, k], az_r.at[i, k], z_peers[k - 1],
                )
            )
        if i < 3:
            sent.append(
                send(
                    gnw.at[i, :, half : 2 * half, :], got_y.at[i],
                    ay_s.at[i], ay_r.at[i], y_peers[i],
                )
            )

        res = nt(probe[i], w[:, at])
        back[...] = res if i == 0 else back[...] + res
        return sent

    sib0 = compute(0)
    sib1 = compute(1)
    far0, dir0 = pairs(0, sib0)
    sib2 = compute(2)
    far1, dir1 = pairs(1, sib1)
    join0 = through(0, far0)
    sib3 = compute(3)
    far2, dir2 = pairs(2, sib2)
    join1 = through(1, far1)
    ag0 = own(0, dir0, join0)
    far3, dir3 = pairs(3, sib3)
    join2 = through(2, far2)
    ag1 = own(1, dir1, join1)
    fwd0 = forward(0, ag0[0], ag0[1])
    join3 = through(3, far3)
    ag2 = own(2, dir2, join2)
    fwd1 = forward(1, ag1[0], ag1[1])
    end0 = last_hop(0, fwd0[0])
    ag3 = own(3, dir3, join3)
    fwd2 = forward(2, ag2[0], ag2[1])
    end1 = last_hop(1, fwd1[0])
    sent = back_block(0, [ag0[2], fwd0[1], fwd0[2], end0])
    fwd3 = forward(3, ag3[0], ag3[1])
    end2 = last_hop(2, fwd2[0])
    sent = sent + back_block(1, [ag1[2], fwd1[1], fwd1[2], end1])
    end3 = last_hop(3, fwd3[0])
    sent = sent + back_block(2, [ag2[2], fwd2[1], fwd2[2], end2])
    sent = sent + back_block(3, [ag3[2], fwd3[1], fwd3[2], end3])

    def mixing(i, carry):
        start = pl.multiple_of(i * 128, 128)
        rows = pl.ds(start, 128)
        inv_c = column(0, start)
        mixed = jnp.zeros((128, 128), F32)
        for g in range(groups):
            at = slice(128 * g, 128 * g + 128)
            prod = back[rows, at] * gated[rows, at]
            gain_o[:, at] = gain_o[:, at] + fold(prod * inv_c)
            mixed = mixed + prod * gain[:, at]
        mix[pl.ds(i, 1), :] = jnp.sum(mixed.T, axis=0, keepdims=True)
        return carry

    lax.fori_loop(0, length // 128, mixing, 0)
    copies = []
    for k, to in enumerate(peers):
        copies.append(send(mix, mix_got.at[head], mix_s.at[k], mix_r.at[k], {"head": to}))
    mix_got[head] = mix[...]
    for copy in copies:
        copy.wait()
    total = mix_got[0]
    for i in range(1, 8):
        total = total + mix_got[i]
    mix[...] = total / channels

    def finish(i, carry):
        start = pl.multiple_of(i * 128, 128)
        rows = pl.ds(start, 128)
        inv_c = column(0, start)
        mixed_c = jnp.broadcast_to(mix[pl.ds(i, 1), :], (128, 128)).T * (inv_c * inv_c * inv_c)
        for g in range(groups):
            at = slice(128 * g, 128 * g + 128)
            gz = gate_z[rows, at].astype(F32)
            gate = gz * jax.nn.sigmoid(gz)
            by_o[rows, at] = (
                back[rows, at] * gain[:, at] * inv_c - gated[rows, at] * mixed_c
            ) * gate
        return carry

    lax.fori_loop(0, length // 128, finish, 0)
    for copy in sent:
        copy.wait()
    half = blk // 8
    for i in range(blocks):
        j = lax.rem(my_y + 1 + i, 4)
        sum_z_o[j] = gnw[i, my_z, 0:half, :] + got_z[i, 0] + got_z[i, 1] + got_z[i, 2]
    sum_y_o[...] = gnw[3, :, half : 2 * half, :] + got_y[0] + got_y[1] + got_y[2]


def middle_call(gated, dgated, sums, gate_z, w, tw, gain, tgain):
    length, width = gated.shape
    cols = w.shape[1]
    blk = cols // 4
    half = blk // 8
    out = lambda *s: jax.ShapeDtypeStruct(s, F32)
    dma = pltpu.SemaphoreType.DMA
    return pl.pallas_call(
        middle_kernel,
        in_specs=[VMEM] * 8,
        out_specs=[VMEM] * 4,
        out_shape=[out(length, width), out(8, width), out(4, half, width), out(4, half, width)],
        scratch_shapes=[
            pltpu.VMEM((8, 2, length), F32),
            pltpu.VMEM((8, length), F32),
            pltpu.VMEM((length, 2 * width), BF16),
            pltpu.VMEM((2, 4, 2, 128, blk), F32),
            pltpu.VMEM((4, 4, 128, blk), F32),
            pltpu.VMEM((4, 128, blk), BF16),
            pltpu.VMEM((4, 128, blk), BF16),
            pltpu.VMEM((4, 2, 128, blk), BF16),
            pltpu.VMEM((4, 2, 128, blk), BF16),
            pltpu.VMEM((4, length, blk), BF16),
            pltpu.VMEM((length, width), F32),
            pltpu.VMEM((4, 4, blk // 4, width), F32),
            pltpu.VMEM((4, 3, half, width), F32),
            pltpu.VMEM((3, 4, half, width), F32),
            pltpu.VMEM((8, 128), F32),
            pltpu.VMEM((8, 8, 128), F32),
            dma((8,)), dma((8,)), dma((4,)), dma((4,)), dma((4,)), dma((4,)),
            dma((4, 2)), dma((4, 2)), dma((4, 7)), dma((4, 7)), dma((8,)), dma((8,)),
            dma((4, 4)), dma((4, 4)), dma((3,)), dma((3,)),
        ],
        compiler_params=pltpu.CompilerParams(
            collective_id=3, has_side_effects=True, vmem_limit_bytes=61 * 1024 * 1024
        ),
        name="probe_and_back",
    )(gated, dgated, sums, gate_z, w, tw, gain, tgain)


def second_kernel(
    x, dx, bc, dbc, rowv, colv, st, dst, log, start, gate_z, dexp,
    gated_o, dgated_o, s0_o, sums_o,
):
    nst = bc.shape[1] // 2
    heads = x.shape[1] // HW
    b_mat, c_mat = bc[:, :nst], bc[:, nst:]
    db_mat, dc_mat = dbc[:, :nst], dbc[:, nst:]
    at_j = lax.broadcasted_iota(jnp.int32, (QB, QB), 1)
    at_i = lax.broadcasted_iota(jnp.int32, (QB, QB), 0)
    keep = at_i >= at_j
    inner = jnp.where(keep, nt3(c_mat, b_mat), 0.0)
    d_inner = jnp.where(
        keep,
        nt3(
            jnp.concatenate([dc_mat, c_mat], axis=1),
            jnp.concatenate([b_mat, db_mat], axis=1),
        ),
        0.0,
    )
    cols = colv[...]
    rows = rowv[...]
    mask = lane_mask()
    squares = jnp.zeros((QB, 128), F32)
    crossed = jnp.zeros((QB, 128), F32)
    for p in range(heads // 2):
        at = slice(128 * p, 128 * p + 128)
        reach = jnp.exp(log[0, 0:1, at])
        s_in = start[:, 0:8, at].reshape(nst, 128)
        ds_in = start[:, 8:16, at].reshape(nst, 128)
        s0 = st[0, :, at] + reach * s_in
        ds0 = dst[0, :, at] + reach * (ds_in + log[0, 1:2, at] * s_in)
        s0_o[0, :, at] = s0
        xp, dxp = x[:, at], dx[:, at]
        size, d_size = expand(cols, S_, p), expand(cols, DS_, p)
        u = size * xp
        du = size * dxp + d_size * xp
        z_h, z_l = split(jnp.concatenate([u, s0], axis=0))
        dz_h, dz_l = split(jnp.concatenate([du, ds0], axis=0))
        mats, d_mats = [], []
        for h in (2 * p, 2 * p + 1):
            c_col = bcast(cols, C_ + h)
            dc_col = bcast(cols, DC_ + h)
            c_row = rows[C_ + h : C_ + h + 1, :]
            dc_row = rows[DC_ + h : DC_ + h + 1, :]
            level = jnp.exp(jnp.minimum(c_col - c_row, 0.0))
            m = inner * level
            dm = d_inner * level + m * (dc_col - dc_row)
            lift = jnp.exp(c_col)
            e = lift * c_mat
            de = lift * dc_mat + dc_col * e
            mats.append(jnp.concatenate([m, e], axis=1))
            d_mats.append(jnp.concatenate([dm, de], axis=1))
        a_h, a_l = split(jnp.concatenate(mats, axis=0))
        da_h, da_l = split(jnp.concatenate(d_mats, axis=0))
        big = nn(a_h, jnp.concatenate([z_h, dz_h], axis=1))
        big = big + nn(a_h, jnp.concatenate([z_l, dz_l], axis=1))
        big = big + nn(a_l, jnp.concatenate([z_h, dz_h], axis=1))
        small = nn(da_h, jnp.concatenate([z_h, z_l], axis=1))
        low = nn(da_l, z_h)
        y2 = big[:, :128]
        dy2 = big[:, 128:] + small[:, :128] + small[:, 128:] + low
        skip, d_skip = dexp[0:1, at], dexp[1:2, at]
        y = jnp.where(mask, y2[:QB], y2[QB:]) + skip * xp
        dy = jnp.where(mask, dy2[:QB], dy2[QB:]) + skip * dxp + d_skip * xp
        gz = gate_z[:, at].astype(F32)
        gate = gz * jax.nn.sigmoid(gz)
        gated = y * gate
        dgated = dy * gate
        gated_o[:, at] = gated
        dgated_o[:, at] = dgated
        squares = squares + gated * gated
        crossed = crossed + 2.0 * gated * dgated
    sums_o[0:1, :] = jnp.sum(squares.T, axis=0, keepdims=True)
    sums_o[1:2, :] = jnp.sum(crossed.T, axis=0, keepdims=True)


def second_call(x, dx, bc, dbc, rowv, colv, st, dst, logs, start, gate_z, dexp):
    length, width = x.shape
    wide = bc.shape[1]
    nst = wide // 2
    count = length // QB
    whole = lambda a: pl.BlockSpec(a.shape, lambda i: (0,) * a.ndim)
    rows = lambda w: pl.BlockSpec((QB, w), lambda i: (i, 0))
    cube = lambda r: pl.BlockSpec((1, r, width), lambda i: (i, 0, 0))
    out = lambda *s: jax.ShapeDtypeStruct(s, F32)
    return pl.pallas_call(
        second_kernel,
        grid=(count,),
        in_specs=[
            rows(width), rows(width), rows(wide), rows(wide),
            pl.BlockSpec((128, QB), lambda i: (0, i)),
            rows(128), cube(nst), cube(nst), cube(8), whole(start), rows(width), whole(dexp),
        ],
        out_specs=[rows(width), rows(width), cube(nst), pl.BlockSpec((2, QB), lambda i: (0, i))],
        out_shape=[out(length, width), out(length, width), out(count, nst, width), out(2, length)],
        compiler_params=pltpu.CompilerParams(vmem_limit_bytes=LIMIT),
        name="outputs_and_tangents",
    )(x, dx, bc, dbc, rowv, colv, st, dst, logs, start, gate_z, dexp)


def fold(a):
    return jnp.sum(a.reshape(a.shape[0] // 8, 8, a.shape[1]), axis=0)


def adjoint_kernel(
    by, x, gx, pre_x, halo_x, bc, gbc, pre_bc, halo_bc, rowv, colv, s0_b, log, last_log,
    dexp, gain, decays, hp, own_z, own_y,
    piece_o, gcx_o, gcbc_o, heads_o, gain_o,
    wx, wbc, head_o, pack_o, lam, state, msg, landed, answer, s_end,
    end_z, end_y, pack_z, landed_z, landed_y, part, landed_q,
    bz_s, bz_r, by_s, by_r,
    s1_s, s1_r, s2_s, s2_r, f1_s, f1_r, f3_s, f3_r, f2_s, f2_r,
):
    step = pl.program_id(0)
    half = lam.shape[0]
    nst = bc.shape[1] // 2
    width = by.shape[1]
    heads = width // HW
    count, n_head = landed.shape[0], landed_q.shape[0]
    me, head = lax.axis_index("seq"), lax.axis_index("head")
    my_y, my_z = me // 4, lax.rem(me, 4)
    seq_peers, head_peers = others("seq", count), others("head", n_head)
    rows_half = own_z.shape[1]
    mask = lane_mask()

    y_peers = [{"seq": lax.rem(my_y + k, 4) * 4 + my_z} for k in range(1, 4)]
    z_peers = [{"seq": my_y * 4 + lax.rem(my_z + k, 4)} for k in range(1, 4)]

    def last_copies():
        copies = []
        for k in (2, 1, 3):
            z, y = lax.rem(my_z + k, 4), lax.rem(my_y + k, 4)
            copies.append(
                link(own_z.at[y], end_z.at[k - 1], bz_s.at[k], bz_r.at[k], {"seq": y * 4 + my_z})
            )
            copies.append(
                link(own_y.at[z], end_y.at[k - 1], by_s.at[k], by_r.at[k], {"seq": my_y * 4 + z})
            )
        return copies

    @pl.when(step == 0)
    def _():
        greet([{"seq": to} for to in seq_peers] + [{"head": to} for to in head_peers])
        for copy in last_copies():
            copy.start()
        state[...] = jnp.zeros_like(state)
        head_o[...] = jnp.zeros_like(head_o)
        pack_o[...] = jnp.zeros_like(pack_o)
        pack_o[8:9, :] = jnp.sum(gain[...], axis=0, keepdims=True)

    @pl.when(step < half)
    def _():
        lam[half - 1 - step] = state[...]
        cols = colv[...]
        ct_h, ct_l = split(bc[:, nst:].T)
        for p in range(heads // 2):
            at = slice(128 * p, 128 * p + 128)
            lifted = jnp.exp(expand(cols, C_, p)) * by[:, at]
            l_h, l_l = split(lifted)
            add = nn(ct_h, l_h) + nn(ct_h, l_l) + nn(ct_l, l_h)
            state[:, at] = jnp.exp(log[0, 2:3, at]) * state[:, at] + add

    @pl.when(step == half - 1)
    def _():
        msg[...] = state[...].reshape(count, 8, width)
        copies = []
        for k, to in enumerate(seq_peers):
            copies.append(send(msg.at[to], landed.at[me], s1_s.at[k], s1_r.at[k], {"seq": to}))
        landed[me] = msg[me]
        for copy in copies:
            copy.wait()
        adjoint = jnp.zeros((8, width), F32)
        for i in range(count - 1, -1, -1):
            answer[i] = adjoint
            adjoint = decays[i : i + 1, :] * adjoint + landed[i]
        copies = []
        for k, to in enumerate(seq_peers):
            copies.append(send(answer.at[to], s_end.at[me], s2_s.at[k], s2_r.at[k], {"seq": to}))
        s_end[me] = answer[me]
        for copy in copies:
            copy.wait()

    @pl.when(step >= half)
    def _():
        load_window(wx, halo_x, pre_x, step == half)
        load_window(wbc, halo_bc, pre_bc, step == half)
        b_mat, c_mat = bc[:, :nst], bc[:, nst:]
        at_i = lax.broadcasted_iota(jnp.int32, (QB, QB), 1)
        at_j = lax.broadcasted_iota(jnp.int32, (QB, QB), 0)
        keep = at_i >= at_j
        inner_t = jnp.where(keep, nt3(b_mat, c_mat), 0.0)
        cols = colv[...]
        rows = rowv[...]
        back_inner_t = jnp.zeros((QB, QB), F32)
        back_b = jnp.zeros((QB, nst), F32)
        back_c = jnp.zeros((QB, nst), F32)
        for p in range(heads // 2):
            at = slice(128 * p, 128 * p + 128)
            own, sig_own = log[0, 2:3, at], log[0, 4:5, at]
            reach = jnp.exp(last_log[0, 0:1, at] + last_log[0, 2:3, at] - log[0, 0:1, at] - own)
            s1 = lam[step - half, :, at] + reach * s_end[:, :, at].reshape(nst, 128)
            s0 = s0_b[0, :, at]
            byp, xp = by[:, at], x[:, at]
            size = expand(cols, S_, p)
            u = size * xp
            rhs_h, rhs_l = split(jnp.concatenate([byp, s1], axis=0))
            u_h, u_l = split(
                jnp.concatenate([jnp.where(mask, u, 0.0), jnp.where(mask, 0.0, u)], axis=0)
            )
            y_h, y_l = split(
                jnp.concatenate([jnp.where(mask, byp, 0.0), jnp.where(mask, 0.0, byp)], axis=0)
            )
            s0_h, s0_l = split(s0)
            mt_tt = nt(u_h, rhs_h) + nt(u_h, rhs_l) + nt(u_l, rhs_h)
            v_all = nt(y_h, s0_h) + nt(y_h, s0_l) + nt(y_l, s0_h)
            mats = []
            for s in range(2):
                h = 2 * p + s
                c_col, cs_col = bcast(cols, C_ + h), bcast(cols, CS_ + h)
                c_row = rows[C_ + h : C_ + h + 1, :]
                cs_row = rows[CS_ + h : CS_ + h + 1, :]
                c_end, cs_end = c_row[:, QB - 1 : QB], cs_row[:, QB - 1 : QB]
                back_mt = mt_tt[s * QB : s * QB + QB, :QB]
                tt = mt_tt[s * QB : s * QB + QB, QB:]
                v = v_all[s * QB : s * QB + QB]
                diff = jnp.minimum(c_row - c_col, 0.0)
                level = jnp.exp(diff)
                back_inner_t = back_inner_t + level * back_mt
                m_t = inner_t * level
                prod = m_t * back_mt
                lifted = jnp.exp(c_col) * v
                back_c = back_c + lifted
                lc = lifted * c_mat
                left = c_end - c_col
                to_end = jnp.exp(left)
                tb = to_end * tt
                back_b = back_b + tb
                tbb = tb * b_mat
                head_o[h, 0] = head_o[h, 0] + fold(prod * diff + lc * c_col + tbb * left)
                head_o[h, 1] = head_o[h, 1] + fold(
                    prod * (cs_row - cs_col) + lc * cs_col + tbb * (cs_end - cs_col)
                )
                mats.append(jnp.concatenate([m_t, to_end * b_mat], axis=1))
            a_h, a_l = split(jnp.concatenate(mats, axis=0))
            wide = nn(a_h, jnp.concatenate([rhs_h, rhs_l], axis=1))
            back_u2 = wide[:, :128] + wide[:, 128:] + nn(a_l, rhs_h)
            back_u = jnp.where(mask, back_u2[:QB], back_u2[QB:])
            back_x = back_u * size + dexp[0:1, at] * byp
            carried = jnp.sum(s1 * s0, axis=0, keepdims=True) * jnp.exp(own)
            through = jnp.sum(expand(cols, SG_, p) * (back_u * xp), axis=0, keepdims=True)
            pack_o[4:5, at] = pack_o[4:5, at] + through
            pack_o[5:6, at] = pack_o[5:6, at] + carried * own
            pack_o[6:7, at] = pack_o[6:7, at] + carried * sig_own
            pack_o[7:8, at] = pack_o[7:8, at] + jnp.sum(byp * xp, axis=0, keepdims=True)
            back_z = back_x * gx[:, at]
            for k in range(4):
                pack_o[k : k + 1, at] = pack_o[k : k + 1, at] + jnp.sum(
                    back_z * wx[5 + k : 5 + k + QB, at], axis=0, keepdims=True
                )
        back_inner_t = jnp.where(keep, back_inner_t, 0.0)
        back_b = back_b + nn3(back_inner_t, c_mat)
        back_c = back_c + nn3(back_inner_t.T, b_mat)
        back_zbc = jnp.concatenate([back_b, back_c], axis=1) * gbc[...]
        for k in range(4):
            pack_o[9 + k : 10 + k, 0 : 2 * nst] = pack_o[9 + k : 10 + k, 0 : 2 * nst] + jnp.sum(
                back_zbc * wbc[5 + k : 5 + k + QB, :], axis=0, keepdims=True
            )


    @pl.when(step == 2 * half - 1)
    def _():
        for p in range(heads // 2):
            at = slice(128 * p, 128 * p + 128)
            for kind in range(2):
                even, odd = head_o[2 * p, kind], head_o[2 * p + 1, kind]
                even = even + pltpu.roll(even, HW, 1)
                odd = odd + pltpu.roll(odd, HW, 1)
                both = jnp.sum(jnp.where(mask, even, odd), axis=0, keepdims=True)
                pack_o[5 + kind : 6 + kind, at] = pack_o[5 + kind : 6 + kind, at] + both
        for slots, group, sems, mine in (
            (landed_z, z_peers, (f1_s, f1_r), pack_o),
            (landed_y, y_peers, (f3_s, f3_r), pack_z),
        ):
            copies = []
            for k, to in enumerate(group):
                copies.append(send(mine, slots.at[k], sems[0].at[k], sems[1].at[k], to))
            for copy in copies:
                copy.wait()
            if slots is landed_z:
                for z in range(4):
                    k = lax.rem(my_z + 3 - z, 4)
                    term = jnp.where(z == my_z, pack_o[...], slots[jnp.minimum(k, 2)])
                    total = term if z == 0 else total + term
                pack_z[...] = total
            else:
                for y in range(4):
                    k = lax.rem(my_y + 3 - y, 4)
                    term = jnp.where(y == my_y, pack_z[...], slots[jnp.minimum(k, 2)])
                    total = term if y == 0 else total + term
        part[...] = total[8:16, 0 : 2 * nst]
        copies = []
        for k, to in enumerate(head_peers):
            copies.append(send(part, landed_q.at[head], f2_s.at[k], f2_r.at[k], {"head": to}))
        landed_q[head] = part[...]
        gcx_o[...] = total[0:4]
        gain_o[...] = total[8:9]
        at = lax.broadcasted_iota(jnp.int32, (width, 128), 0)
        to = lax.broadcasted_iota(jnp.int32, (width, 128), 1) * HW
        pick = jnp.where((at >= to) & (at < to + HW), 1.0, 0.0).astype(F32)
        sums = jnp.dot(
            total, pick, precision=lax.Precision.HIGHEST, preferred_element_type=F32
        )[:, :heads]
        heads_o[0:1] = sums[4:5] - jnp.exp(hp[1:2]) * sums[6:7]
        heads_o[1:2] = sums[5:6]
        heads_o[2:3] = sums[7:8]
        for copy in last_copies():
            copy.wait()
        piece_o[0:rows_half] = own_z[my_y] + end_z[0] + end_z[1] + end_z[2]
        piece_o[rows_half : 2 * rows_half] = own_y[my_z] + end_y[0] + end_y[1] + end_y[2]
        for copy in copies:
            copy.wait()
        total2 = landed_q[0]
        for i in range(1, n_head):
            total2 = total2 + landed_q[i]
        gcbc_o[...] = total2[1:5]


def adjoint_call(
    by, x, gx, pre_x, halo_x, bc, gbc, pre_bc, halo_bc, rowv, colv, s0, logs, dexp, gain, decays,
    hp, sum_z, sum_y, count, n_head,
):
    length, width = by.shape
    wide = bc.shape[1]
    nst = wide // 2
    heads = width // HW
    half = length // QB
    rows_half = sum_z.shape[1]
    piece = 2 * rows_half
    both = lambda i: jnp.maximum(half - 1 - i, i - half)
    late = lambda i: jnp.maximum(i - half, 0)
    whole = lambda a: pl.BlockSpec(a.shape, lambda i: (0,) * a.ndim)
    rows = lambda w, f: pl.BlockSpec((QB, w), lambda i: (f(i), 0))
    cube = lambda r, f: pl.BlockSpec((1, r, width), lambda i: (f(i), 0, 0))
    out = lambda *s: jax.ShapeDtypeStruct(s, F32)
    fixed = lambda *s: pl.BlockSpec(s, lambda i: (0,) * len(s))
    dma = pltpu.SemaphoreType.DMA
    return pl.pallas_call(
        adjoint_kernel,
        grid=(2 * half,),
        in_specs=[
            rows(width, both), rows(width, late), rows(width, late), rows(width, late),
            whole(halo_x), rows(wide, both), rows(wide, late), rows(wide, late), whole(halo_bc),
            pl.BlockSpec((128, QB), lambda i: (0, late(i))), rows(128, both),
            cube(nst, late), cube(8, both),
            pl.BlockSpec((1, 8, width), lambda i: (half - 1, 0, 0)),
            whole(dexp), whole(gain), whole(decays), whole(hp),
            whole(sum_z), whole(sum_y),
        ],
        out_specs=[
            fixed(piece, width), fixed(4, width), fixed(4, wide), fixed(3, heads), fixed(1, width),
        ],
        out_shape=[out(piece, width), out(4, width), out(4, wide), out(3, heads), out(1, width)],
        scratch_shapes=[
            pltpu.VMEM((QB + 8, width), F32), pltpu.VMEM((QB + 8, wide), F32),
            pltpu.VMEM((heads, 2, 8, 128), F32), pltpu.VMEM((16, width), F32),
            pltpu.VMEM((half, nst, width), F32), pltpu.VMEM((nst, width), F32),
            pltpu.VMEM((count, 8, width), F32), pltpu.VMEM((count, 8, width), F32),
            pltpu.VMEM((count, 8, width), F32), pltpu.VMEM((count, 8, width), F32),
            pltpu.VMEM((3, rows_half, width), F32), pltpu.VMEM((3, rows_half, width), F32),
            pltpu.VMEM((16, width), F32), pltpu.VMEM((3, 16, width), F32),
            pltpu.VMEM((3, 16, width), F32), pltpu.VMEM((8, wide), F32),
            pltpu.VMEM((n_head, 8, wide), F32),
            dma((4,)), dma((4,)), dma((4,)), dma((4,)),
            dma((count,)), dma((count,)), dma((count,)), dma((count,)),
            dma((3,)), dma((3,)), dma((3,)), dma((3,)), dma((n_head,)), dma((n_head,)),
        ],
        compiler_params=pltpu.CompilerParams(
            collective_id=2, has_side_effects=True, vmem_limit_bytes=LIMIT
        ),
        name="adjoint",
    )(
        by, x, gx, pre_x, halo_x, bc, gbc, pre_bc, halo_bc, rowv, colv, s0, logs, logs,
        dexp, gain, decays, hp, sum_z, sum_y,
    )


def on_device(
    pre_x, pre_bc, gate_z, dt_raw, conv_x, conv_bc, head_params, norm_gain, w_out,
    t_conv_x, t_conv_bc, t_heads, t_gain, t_wout,
):
    count = lax.axis_size("seq")
    width = pre_x.shape[1]
    heads = dt_raw.shape[0]
    channels = width * lax.axis_size("head") * 1.0
    tails = jnp.concatenate([pre_x[-8:], pre_bc[-8:]], axis=1)
    tails = lax.ppermute(tails, "seq", [(i, i + 1) for i in range(count - 1)]).astype(F32)
    halo_x, halo_bc = tails[:, :width], tails[:, width:]
    t_wout_all = lax.all_gather(t_wout.T, "seq", axis=0, tiled=True)
    hpc = jnp.concatenate([head_params, t_heads], axis=0).T
    dexp = jnp.repeat(jnp.stack([head_params[2], t_heads[2]]), HW, axis=1)
    x, dx, gx, bc, dbc, gbc, rowv, colv, st, dst, logs, msg, tile = first_call(
        pre_x, halo_x, pre_bc, halo_bc, dt_raw, conv_x, t_conv_x, conv_bc, t_conv_bc, hpc, count
    )
    start, decays = scan_forward(msg, tile)
    gated, d_gated, s0, sums = second_call(
        x, dx, bc, dbc, rowv, colv, st, dst, logs, start, gate_z, dexp
    )
    back_y, gain_part, sum_z, sum_y = middle_call(
        gated, d_gated, sums, gate_z, w_out, t_wout_all, norm_gain[None], t_gain[None]
    )
    gn_wout, gn_conv_x, gn_conv_bc, gn_heads, gn_gain = adjoint_call(
        back_y, x, gx, pre_x, halo_x, bc, gbc, pre_bc, halo_bc, rowv, colv, s0, logs, dexp,
        gain_part, decays, head_params, sum_z, sum_y, count, lax.axis_size("head"),
    )
    return (gn_conv_x, gn_conv_bc, gn_heads, gn_gain[0], gn_wout.T)


def solution(mesh):
    in_specs = (
        P("seq", "head"), P("seq", None), P("seq", "head"), P("head", "seq"), P(None, "head"),
        P(), P(None, "head"), P("head"), P("head", None), P(None, "head"), P(), P(None, "head"),
        P("head"), P("head", "seq"),
    )
    out_specs = (P(None, "head"), P(), P(None, "head"), P("head"), P("head", "seq"))
    return jax.shard_map(
        on_device, mesh=mesh, in_specs=in_specs, out_specs=out_specs, check_vma=False
    )
```

```python
import jax
import jax.numpy as jnp
from jax import lax
from jax.experimental import pallas as pl
from jax.experimental.pallas import tpu as pltpu
from jax.sharding import PartitionSpec as P

QB = 128
HW = 64
F32 = jnp.float32
BF16 = jnp.bfloat16
MESH = pl.DeviceIdType.MESH
S_, DS_, C_, DC_, CS_, SG_, K_, DK_ = (16 * i for i in range(8))
LIMIT = 56 * 1024 * 1024
SCAN_AT = 4
TURN = (1, 3, 2, 4)


def split(a):
    high = a.astype(BF16)
    return high, (a - high.astype(F32)).astype(BF16)


def nn(a, b):
    return jnp.dot(a, b, preferred_element_type=F32)


def nt(a, b):
    return lax.dot_general(a, b, (((1,), (1,)), ((), ())), preferred_element_type=F32)


def nn3(a, b):
    (ah, al), (bh, bl) = split(a), split(b)
    return nn(ah, bh) + nn(ah, bl) + nn(al, bh)


def nt3(a, b):
    (ah, al), (bh, bl) = split(a), split(b)
    return nt(ah, bh) + nt(ah, bl) + nt(al, bh)


def lane_mask():
    return lax.broadcasted_iota(jnp.int32, (1, 128), 1) < HW


def bcast(cols, at):
    return jnp.broadcast_to(cols[:, at : at + 1], (cols.shape[0], 128))


def expand(cols, base, pair):
    return jnp.where(
        lane_mask(), bcast(cols, base + 2 * pair), bcast(cols, base + 2 * pair + 1)
    )


def expand_all(cols, base, heads):
    return jnp.concatenate([expand(cols, base, p) for p in range(heads // 2)], axis=1)


def load_window(window, halo, block, first):
    @pl.when(first)
    def _():
        window[0:8] = halo[...]

    @pl.when(jnp.logical_not(first))
    def _():
        window[0:8] = window[QB : QB + 8]

    window[8 : QB + 8] = block[...].astype(F32)


def conv_pair(window, weight, t_weight):
    z = jnp.zeros((QB, window.shape[1]), F32)
    dz = jnp.zeros((QB, window.shape[1]), F32)
    for k in range(4):
        rows = window[5 + k : 5 + k + QB, :]
        z = z + weight[k : k + 1, :] * rows
        dz = dz + t_weight[k : k + 1, :] * rows
    sig = jax.nn.sigmoid(z)
    slope = sig * (1.0 + z * (1.0 - sig))
    return z * sig, slope * dz, slope


def greet(peers):
    barrier = pltpu.get_barrier_semaphore()
    for peer in peers:
        pl.semaphore_signal(barrier, inc=1, device_id=peer, device_id_type=MESH)
    pl.semaphore_wait(barrier, len(peers))


def others(axis, count):
    me = lax.axis_index(axis)
    return [lax.rem(me + k, count) for k in range(1, count)]


def link(src, dst, send_sem, recv_sem, device):
    return pltpu.make_async_remote_copy(
        src_ref=src, dst_ref=dst, send_sem=send_sem, recv_sem=recv_sem,
        device_id=device, device_id_type=MESH,
    )


def send(*what):
    copy = link(*what)
    copy.start()
    return copy


VMEM = pl.BlockSpec(memory_space=pltpu.VMEM)


def column_of(row):
    heads = row.shape[1]
    at_i = lax.broadcasted_iota(jnp.int32, (heads, heads), 0)
    at_j = lax.broadcasted_iota(jnp.int32, (heads, heads), 1)
    return jnp.sum(jnp.where(at_i == at_j, row, 0.0), axis=1, keepdims=True)


def forward_kernel(
    pre_x, tail_x, pre_bc, tail_bc, dt, gate_z, cx, tcx, cbc, tcbc, hp, th,
    x_o, gx_o, bc_o, gbc_o, row_o, col_o, log_o, s0_o, gated_o, dgated_o, sums_o, decay_o,
    halo_x_o, halo_bc_o,
    wx, wbc, feat, state, d_state, logs, x_a, dx_a, bc_a, dbc_a, row_a, col_a, st_a, dst_a,
    log_a, y_a, dy_a, tile, got_x, got_bc, msg, landed, tiles, answer, start,
    halo_s, halo_r, tile_s, tile_r, s1_s, s1_r, s2_s, s2_r,
):
    step = pl.program_id(0)
    blocks = st_a.shape[0]
    heads = dt.shape[0]
    width = pre_x.shape[1]
    nst = cbc.shape[1] // 2
    count = landed.shape[0]
    me = lax.axis_index("seq")
    peers = others("seq", count)
    mask = lane_mask()

    def place(block):
        return pl.ds(pl.multiple_of(block * QB, QB), QB)

    def scan_copies():
        copies = []
        for k, to in enumerate(peers):
            at = {"seq": to}
            copies.append(link(tile, tiles.at[me], tile_s.at[k], tile_r.at[k], at))
            copies.append(link(msg.at[to], landed.at[me], s1_s.at[k], s1_r.at[k], at))
        return copies

    def back_copies():
        return [
            link(answer.at[to], start.at[me], s2_s.at[k], s2_r.at[k], {"seq": to})
            for k, to in enumerate(peers)
        ]

    @pl.when(step == 0)
    def _():
        greet([{"seq": to} for to in peers])
        after = {"seq": lax.rem(me + 1, count)}
        tails = [
            send(tail_x, got_x, halo_s.at[0], halo_r.at[0], after),
            send(tail_bc, got_bc, halo_s.at[1], halo_r.at[1], after),
        ]
        state[...] = jnp.zeros_like(state)
        d_state[...] = jnp.zeros_like(d_state)
        logs[...] = jnp.zeros_like(logs)
        feat[...] = jnp.zeros_like(feat)
        tile[...] = jnp.zeros_like(tile)
        for copy in tails:
            copy.wait()
        halo_x_o[...] = jnp.where(me == 0, 0.0, got_x[...].astype(F32)[8:16])
        halo_bc_o[...] = jnp.where(me == 0, 0.0, got_bc[...].astype(F32)[8:16])

    @pl.when(step < blocks)
    def _():
        load_window(wx, halo_x_o, pre_x, step == 0)
        load_window(wbc, halo_bc_o, pre_bc, step == 0)
        z = dt[...] + column_of(hp[0:1, :])
        rate = jnp.exp(column_of(hp[1:2, :]))
        t_bias, t_lrate = column_of(th[0:1, :]), column_of(th[1:2, :])
        size = jnp.maximum(z, 0.0) + jnp.log1p(jnp.exp(-jnp.abs(z)))
        sig = jax.nn.sigmoid(z)
        log_decay = -size * rate
        at_i = lax.broadcasted_iota(jnp.int32, (QB, QB), 1)
        at_j = lax.broadcasted_iota(jnp.int32, (QB, QB), 0)
        upper = jnp.where(at_j <= at_i, 1.0, 0.0).astype(F32)
        exact = dict(precision=lax.Precision.HIGHEST, preferred_element_type=F32)
        cumul = jnp.dot(log_decay, upper, **exact)
        sig_sum = jnp.dot(sig, upper, **exact)
        d_size = sig * t_bias
        d_cumul = cumul * t_lrate - rate * t_bias * sig_sum
        to_end = jnp.exp(cumul[:, QB - 1 : QB] - cumul)
        feat[S_ : S_ + heads] = size
        feat[DS_ : DS_ + heads] = d_size
        feat[C_ : C_ + heads] = cumul
        feat[DC_ : DC_ + heads] = d_cumul
        feat[CS_ : CS_ + heads] = sig_sum
        feat[SG_ : SG_ + heads] = sig
        feat[K_ : K_ + heads] = to_end * size
        feat[DK_ : DK_ + heads] = to_end * (
            d_size + size * (d_cumul[:, QB - 1 : QB] - d_cumul)
        )
        rows = feat[...]
        cols = rows.T
        row_o[...] = rows
        col_o[...] = cols
        row_a[step] = rows
        col_a[step] = cols

        bc, dbc, gbc = conv_pair(wbc, cbc, tcbc)
        bc_o[...] = bc
        gbc_o[...] = gbc
        bc_a[step] = bc
        dbc_a[step] = dbc
        x, dx, gx = conv_pair(wx, cx, tcx)
        x_o[...] = x
        gx_o[...] = gx
        x_a[step] = x
        dx_a[step] = dx

        last = cols[QB - 1 : QB, :]
        tile[0:1, :] = tile[0:1, :] + last
        own = expand_all(last, C_, heads)
        d_own = expand_all(last, DC_, heads)
        log = jnp.concatenate(
            [logs[0:1, :], logs[1:2, :], own, d_own, expand_all(last, CS_, heads)]
            + [jnp.zeros((3, width), F32)],
            axis=0,
        )
        log_o[0] = log
        log_a[step] = log
        logs[0:1, :] = logs[0:1, :] + own
        logs[1:2, :] = logs[1:2, :] + d_own

        st_a[step] = state[...]
        dst_a[step] = d_state[...]
        bt = bc[:, :nst].T
        dbt = dbc[:, :nst].T
        both_h, both_l = split(jnp.concatenate([bt, dbt], axis=1))
        for p in range(heads // 2):
            at = slice(128 * p, 128 * p + 128)
            k_x, dk_x = expand(cols, K_, p), expand(cols, DK_, p)
            ux = k_x * x[:, at]
            dux = k_x * dx[:, at] + dk_x * x[:, at]
            z_h, z_l = split(jnp.concatenate([dux, ux], axis=0))
            d_add = nn(both_h, z_h) + nn(both_h, z_l) + nn(both_l, z_h)
            b_h, b_l, u_h, u_l = both_h[:, :QB], both_l[:, :QB], z_h[QB:], z_l[QB:]
            add = nn(b_h, u_h) + nn(b_h, u_l) + nn(b_l, u_h)
            decay = jnp.exp(own[:, at])
            before = state[:, at]
            d_state[:, at] = decay * (d_state[:, at] + d_own[:, at] * before) + d_add
            state[:, at] = decay * before + add

    @pl.when(step == blocks - 1)
    def _():
        msg[:, 0:8, :] = state[...].reshape(count, 8, width)
        msg[:, 8:16, :] = d_state[...].reshape(count, 8, width)
        for copy in scan_copies():
            copy.start()

    @pl.when(step == blocks + SCAN_AT)
    def _():
        landed[me] = msg[me]
        tiles[me] = tile[...]
        for copy in scan_copies():
            copy.wait()
        total = jnp.zeros((8, width), F32)
        d_total = jnp.zeros((8, width), F32)
        for i in range(count):
            answer[i, 0:8] = total
            answer[i, 8:16] = d_total
            features = tiles[i, 0:1, :]
            decay = jnp.exp(expand_all(features, C_, heads))
            decay_o[i : i + 1, :] = decay
            d_total = decay * (d_total + expand_all(features, DC_, heads) * total)
            d_total = d_total + landed[i, 8:16]
            total = decay * total + landed[i, 0:8]
        for copy in back_copies():
            copy.start()

    @pl.when((step >= blocks) & (step < 2 * blocks))
    def _():
        block = step - blocks
        bc, dbc = bc_a[block], dbc_a[block]
        b_mat, c_mat = bc[:, :nst], bc[:, nst:]
        db_mat, dc_mat = dbc[:, :nst], dbc[:, nst:]
        at_j = lax.broadcasted_iota(jnp.int32, (QB, QB), 1)
        at_i = lax.broadcasted_iota(jnp.int32, (QB, QB), 0)
        keep = at_i >= at_j
        inner = jnp.where(keep, nt3(c_mat, b_mat), 0.0)
        d_inner = jnp.where(
            keep,
            nt3(
                jnp.concatenate([dc_mat, c_mat], axis=1),
                jnp.concatenate([b_mat, db_mat], axis=1),
            ),
            0.0,
        )
        cols = col_a[block]
        rows = row_a[block]
        for p in range(heads // 2):
            at = slice(128 * p, 128 * p + 128)
            xp, dxp = x_a[block, :, at], dx_a[block, :, at]
            size, d_size = expand(cols, S_, p), expand(cols, DS_, p)
            z_h, z_l = split(size * xp)
            dz_h, dz_l = split(size * dxp + d_size * xp)
            mats, d_mats = [], []
            for h in (2 * p, 2 * p + 1):
                c_row = rows[C_ + h : C_ + h + 1, :]
                dc_row = rows[DC_ + h : DC_ + h + 1, :]
                level = jnp.exp(jnp.minimum(bcast(cols, C_ + h) - c_row, 0.0))
                m = inner * level
                mats.append(m)
                d_mats.append(d_inner * level + m * (bcast(cols, DC_ + h) - dc_row))
            a_h, a_l = split(jnp.concatenate(mats, axis=0))
            da_h, da_l = split(jnp.concatenate(d_mats, axis=0))
            zz_h = jnp.concatenate([z_h, dz_h], axis=1)
            big = nn(
                jnp.concatenate([a_h, a_l], axis=1), jnp.concatenate([zz_h, zz_h], axis=0)
            ) + nn(a_h, jnp.concatenate([z_l, dz_l], axis=1))
            small = nn(
                jnp.concatenate([da_h, da_l], axis=1), jnp.concatenate([z_h, z_h], axis=0)
            ) + nn(da_h, z_l)
            y2 = big[:, :128]
            dy2 = big[:, 128:] + small
            skip, d_skip = expand(hp[2:3, :], 0, p), expand(th[2:3, :], 0, p)
            y_a[block, :, at] = jnp.where(mask, y2[:QB], y2[QB:]) + skip * xp
            dy_a[block, :, at] = (
                jnp.where(mask, dy2[:QB], dy2[QB:]) + skip * dxp + d_skip * xp
            )

    @pl.when(step == 2 * blocks)
    def _():
        start[me] = answer[me]
        for copy in back_copies():
            copy.wait()

    @pl.when(step >= 2 * blocks)
    def _():
        block = step - 2 * blocks
        cols = col_a[block]
        c_h, c_l = split(bc_a[block][:, nst:])
        dc_h, dc_l = split(dbc_a[block][:, nst:])
        squares = jnp.zeros((QB, 128), F32)
        crossed = jnp.zeros((QB, 128), F32)
        for p in range(heads // 2):
            at = slice(128 * p, 128 * p + 128)
            reach = jnp.exp(log_a[block, 0:1, at])
            s_in = start[:, 0:8, at].reshape(nst, 128)
            ds_in = start[:, 8:16, at].reshape(nst, 128)
            s0 = st_a[block, :, at] + reach * s_in
            ds0 = dst_a[block, :, at] + reach * (ds_in + log_a[block, 1:2, at] * s_in)
            s0_o[0, :, at] = s0
            s_h, s_l = split(s0)
            ds_h, ds_l = split(ds0)
            big = (
                nn(c_h, jnp.concatenate([s_h, ds_h], axis=1))
                + nn(c_h, jnp.concatenate([s_l, ds_l], axis=1))
                + nn(c_l, jnp.concatenate([s_h, ds_h], axis=1))
            )
            low = nn(dc_h, s_h) + nn(dc_h, s_l) + nn(dc_l, s_h)
            lift = jnp.exp(expand(cols, C_, p))
            add = lift * big[:, :128]
            y = y_a[block, :, at] + add
            dy = (
                dy_a[block, :, at]
                + lift * (big[:, 128:] + low)
                + expand(cols, DC_, p) * add
            )
            gz = gate_z[:, at].astype(F32)
            gate = gz * jax.nn.sigmoid(gz)
            gated = y * gate
            dgated = dy * gate
            gated_o[:, at] = gated
            dgated_o[:, at] = dgated
            squares = squares + gated * gated
            crossed = crossed + 2.0 * gated * dgated
        sums_o[0:1, :] = jnp.sum(squares.T, axis=0, keepdims=True)
        sums_o[1:2, :] = jnp.sum(crossed.T, axis=0, keepdims=True)


def forward_call(pre_x, pre_bc, dt, gate_z, cx, tcx, cbc, tcbc, hp, th, parts):
    length, width = pre_x.shape
    wide = pre_bc.shape[1]
    nst = wide // 2
    heads = dt.shape[0]
    count = length // QB
    first = lambda i: jnp.minimum(i, count - 1)
    last = lambda i: jnp.maximum(i - 2 * count, 0)
    whole = lambda a: pl.BlockSpec(a.shape, lambda i: (0,) * a.ndim)
    fixed = lambda *s: pl.BlockSpec(s, lambda i: (0,) * len(s))
    rows = lambda w, f: pl.BlockSpec((QB, w), lambda i: (f(i), 0))
    cube = lambda r, f: pl.BlockSpec((1, r, width), lambda i: (f(i), 0, 0))
    tail = lambda w: pl.BlockSpec((16, w), lambda i: (length // 16 - 1, 0))
    lanes = lambda r, f: pl.BlockSpec((r, QB), lambda i: (0, f(i)))
    out = lambda *s: jax.ShapeDtypeStruct(s, F32)
    vmem = lambda *s: pltpu.VMEM(s, F32)
    dma = pltpu.SemaphoreType.DMA
    return pl.pallas_call(
        forward_kernel,
        grid=(3 * count,),
        in_specs=[
            rows(width, first), tail(width), rows(wide, first), tail(wide), lanes(heads, first),
            rows(width, last), whole(cx), whole(tcx), whole(cbc), whole(tcbc), whole(hp),
            whole(th),
        ],
        out_specs=[
            rows(width, first), rows(width, first), rows(wide, first), rows(wide, first),
            lanes(128, first), rows(128, first), cube(8, first), cube(nst, last),
            rows(width, last), rows(width, last), lanes(2, last), fixed(parts, width),
            fixed(8, width), fixed(8, wide),
        ],
        out_shape=[
            out(length, width), out(length, width), out(length, wide), out(length, wide),
            out(128, length), out(length, 128), out(count, 8, width), out(count, nst, width),
            out(length, width), out(length, width), out(2, length), out(parts, width),
            out(8, width), out(8, wide),
        ],
        scratch_shapes=[
            vmem(QB + 8, width), vmem(QB + 8, wide), vmem(128, QB), vmem(nst, width),
            vmem(nst, width), vmem(8, width), vmem(count, QB, width), vmem(count, QB, width),
            vmem(count, QB, wide), vmem(count, QB, wide), vmem(count, 128, QB),
            vmem(count, QB, 128), vmem(count, nst, width), vmem(count, nst, width),
            vmem(count, 8, width), vmem(count, QB, width), vmem(count, QB, width),
            vmem(8, 128), pltpu.VMEM((16, width), BF16), pltpu.VMEM((16, wide), BF16),
            vmem(parts, 16, width), vmem(parts, 16, width), vmem(parts, 8, 128),
            vmem(parts, 16, width), vmem(parts, 16, width),
            dma((2,)), dma((2,)), dma((parts,)), dma((parts,)), dma((parts,)), dma((parts,)),
            dma((parts,)), dma((parts,)),
        ],
        compiler_params=pltpu.CompilerParams(
            collective_id=1, has_side_effects=True, vmem_limit_bytes=LIMIT
        ),
        name="forward",
    )(pre_x, pre_x, pre_bc, pre_bc, dt, gate_z, cx, tcx, cbc, tcbc, hp, th)


def middle_kernel(
    gated, dgated, sums, gate_z, w, tw, gain_in, tgain_in,
    by_o, gain_o, sum_z_o, sum_y_o, late_o,
    got, scal, both, part, sib, far_src, far_dst, out_src, out_dst, probe, back, gnw, got_z, got_y,
    mix, mix_got, gains,
    sums_s, sums_r, sib_s, sib_r, far_s, far_r, out_s, out_r, ag_s, ag_r, mix_s, mix_r,
    az_s, az_r, ay_s, ay_r,
):
    length, width = gated.shape
    blocks, _, blk = probe.shape
    groups = width // 128
    channels = width * 8.0
    head = lax.axis_index("head")
    me = lax.axis_index("seq")
    my_y, my_z = me // 4, lax.rem(me, 4)
    mine = head // 2
    core = lax.rem(head, 2)
    right, left, far = (lax.rem(mine + k, 4) for k in (1, 3, 2))
    device = lambda chip, c: {"head": chip * 2 + c}
    to_right, to_left, to_sib = device(right, core), device(left, core), device(mine, 1 - core)
    y_peers = [{"seq": lax.rem(my_y + k, 4) * 4 + my_z} for k in range(1, 4)]
    z_peers = [{"seq": my_y * 4 + lax.rem(my_z + k, 4)} for k in range(1, 4)]
    peers = others("head", 8)
    greet([{"head": to} for to in peers] + y_peers + z_peers)
    copies = []
    for k, to in enumerate(peers):
        copies.append(send(sums, got.at[head], sums_s.at[k], sums_r.at[k], {"head": to}))
    got[head] = sums[...]
    gain_o[...] = jnp.zeros_like(gain_o)
    gains[0:1] = gain_in[...].reshape(1, width)
    gains[1:2] = tgain_in[...].reshape(1, width)
    gain, tgain = gains.at[0:1], gains.at[1:2]
    for copy in copies:
        copy.wait()
    total = got[0]
    for i in range(1, 8):
        total = total + got[i]
    inv = lax.rsqrt(total[0:1] / channels + 1e-05)
    scal[0:1] = inv
    scal[1:2] = -0.5 * inv * inv * inv * total[1:2] / channels

    def column(row, start):
        at = pl.ds(pl.multiple_of(start, 128), 128)
        return jnp.broadcast_to(scal[row : row + 1, at], (128, 128)).T

    def norm(i, carry):
        start = pl.multiple_of(i * 128, 128)
        rows = pl.ds(start, 128)
        inv_c, d_inv_c = column(0, start), column(1, start)
        for g in range(groups):
            at = slice(128 * g, 128 * g + 128)
            gt, dgt = gated[rows, at], dgated[rows, at]
            ga = gain[:, at]
            scaled = gt * inv_c
            normed = scaled * ga
            d_normed = (dgt * inv_c + gt * d_inv_c) * ga + scaled * tgain[:, at]
            both[rows, at] = d_normed.astype(BF16)
            both[rows, width + 128 * g : width + 128 * g + 128] = normed.astype(BF16)
        return carry

    lax.fori_loop(0, length // 128, norm, 0)

    def columns(i):
        return pl.ds(pl.multiple_of(lax.rem(my_y + TURN[i], 4) * blk, 128), blk)

    def compute(i):
        slot, at = i % 2, columns(i)

        res = nn(both[:, 0:width], w[:, at]) + nt(both[:, width:], tw[at, :])
        part[slot] = res.reshape(4, 2, 128, blk)
        return send(part.at[slot, :, 1 - core], sib.at[i], sib_s.at[i], sib_r.at[i], to_sib)

    def pairs(i, copy):
        copy.wait()
        for chip in range(4):
            sib[i, chip] = sib[i, chip] + part[i % 2, chip, core]
        way, near = (to_right, to_left) if i % 2 == 0 else (to_left, to_right)
        near_chip = left if i % 2 == 0 else right
        far_src[i] = sib[i, far].astype(BF16)
        transit = send(far_src.at[i], far_dst.at[i], far_s.at[i], far_r.at[i], way)
        out_src[i, 0] = sib[i, near_chip].astype(BF16)
        direct = send(out_src.at[i, 0], out_dst.at[i, 0], out_s.at[i, 0], out_r.at[i, 0], near)
        return transit, direct

    def through(i, transit):
        transit.wait()
        way, chip = (to_right, right) if i % 2 == 0 else (to_left, left)
        out_src[i, 1] = (sib[i, chip] + far_dst[i].astype(F32)).astype(BF16)
        return send(out_src.at[i, 1], out_dst.at[i, 1], out_s.at[i, 1], out_r.at[i, 1], way)

    def pass_on(i, slot, chip, to):
        ref = probe.at[i, pl.ds(pl.multiple_of(chip * 256 + core * 128, 128), 128), :]
        return send(ref, ref, ag_s.at[i, slot], ag_r.at[i, slot], to)

    def own(i, direct, joined):
        direct.wait()
        joined.wait()
        rows = pl.ds(pl.multiple_of(mine * 256 + core * 128, 128), 128)
        res = sib[i, mine] + out_dst[i, 0].astype(F32) + out_dst[i, 1].astype(F32)
        probe[i, rows, :] = res.astype(BF16)
        go_right = pass_on(i, 0, mine, to_right)
        go_left = pass_on(i, 1, mine, to_left)
        return go_right, go_left, pass_on(i, 2, mine, to_sib)

    def forward(i, go_right, go_left):
        if i % 2 == 0:
            go_right.wait()
            onward = pass_on(i, 3, left, to_right)
            go_left.wait()
        else:
            go_left.wait()
            onward = pass_on(i, 3, right, to_left)
            go_right.wait()
        return onward, pass_on(i, 4, left, to_sib), pass_on(i, 5, right, to_sib)

    def last_hop(i, onward):
        onward.wait()
        return pass_on(i, 6, far, to_sib)

    def back_block(i, waits):
        for copy in waits:
            copy.wait()
        at = columns(i)
        summed = lax.dot_general(
            probe[i], both[:, width:], (((0,), (0,)), ((), ())), preferred_element_type=F32
        ).reshape(4, blk // 4, width)
        half = blk // 8
        sent = []
        if i < 2:
            gnw[i] = summed
        else:
            late_o[i - 2] = summed
        for k in (2, 1, 3) if i < 2 else ():
            z = lax.rem(my_z + k, 4)
            sent.append(
                send(
                    gnw.at[i, z, 0:half, :], got_z.at[i, k - 1],
                    az_s.at[i, k], az_r.at[i, k], z_peers[k - 1],
                )
            )
        if i < 2:
            sent.append(
                send(
                    gnw.at[i, :, half : 2 * half, :], got_y.at[i],
                    ay_s.at[i], ay_r.at[i], y_peers[TURN[i] - 1],
                )
            )

        res = nt(probe[i], w[:, at])
        back[...] = res if i == 0 else back[...] + res
        return sent

    sib0 = compute(0)
    sib1 = compute(1)
    far0, dir0 = pairs(0, sib0)
    sib2 = compute(2)
    far1, dir1 = pairs(1, sib1)
    join0 = through(0, far0)
    sib3 = compute(3)
    far2, dir2 = pairs(2, sib2)
    join1 = through(1, far1)
    ag0 = own(0, dir0, join0)
    far3, dir3 = pairs(3, sib3)
    join2 = through(2, far2)
    ag1 = own(1, dir1, join1)
    fwd0 = forward(0, ag0[0], ag0[1])
    join3 = through(3, far3)
    ag2 = own(2, dir2, join2)
    fwd1 = forward(1, ag1[0], ag1[1])
    end0 = last_hop(0, fwd0[0])
    ag3 = own(3, dir3, join3)
    fwd2 = forward(2, ag2[0], ag2[1])
    end1 = last_hop(1, fwd1[0])
    sent = back_block(0, [ag0[2], fwd0[1], fwd0[2], end0])
    fwd3 = forward(3, ag3[0], ag3[1])
    end2 = last_hop(2, fwd2[0])
    sent = sent + back_block(1, [ag1[2], fwd1[1], fwd1[2], end1])
    end3 = last_hop(3, fwd3[0])
    sent = sent + back_block(2, [ag2[2], fwd2[1], fwd2[2], end2])
    sent = sent + back_block(3, [ag3[2], fwd3[1], fwd3[2], end3])

    def mixing(i, carry):
        start = pl.multiple_of(i * 128, 128)
        rows = pl.ds(start, 128)
        inv_c = column(0, start)
        mixed = jnp.zeros((128, 128), F32)
        for g in range(groups):
            at = slice(128 * g, 128 * g + 128)
            prod = back[rows, at] * gated[rows, at]
            gain_o[:, at] = gain_o[:, at] + fold(prod * inv_c)
            mixed = mixed + prod * gain[:, at]
        mix[pl.ds(i, 1), :] = jnp.sum(mixed.T, axis=0, keepdims=True)
        return carry

    lax.fori_loop(0, length // 128, mixing, 0)
    copies = []
    for k, to in enumerate(peers):
        copies.append(send(mix, mix_got.at[head], mix_s.at[k], mix_r.at[k], {"head": to}))
    mix_got[head] = mix[...]
    for copy in copies:
        copy.wait()
    total = mix_got[0]
    for i in range(1, 8):
        total = total + mix_got[i]
    mix[...] = total / channels

    def finish(i, carry):
        start = pl.multiple_of(i * 128, 128)
        rows = pl.ds(start, 128)
        inv_c = column(0, start)
        mixed_c = jnp.broadcast_to(mix[pl.ds(i, 1), :], (128, 128)).T * (inv_c * inv_c * inv_c)
        for g in range(groups):
            at = slice(128 * g, 128 * g + 128)
            gz = gate_z[rows, at].astype(F32)
            gate = gz * jax.nn.sigmoid(gz)
            by_o[rows, at] = (
                back[rows, at] * gain[:, at] * inv_c - gated[rows, at] * mixed_c
            ) * gate
        return carry

    lax.fori_loop(0, length // 128, finish, 0)
    for copy in sent:
        copy.wait()
    half = blk // 8
    for i in range(2):
        sum_z_o[i] = gnw[i, my_z, 0:half, :] + got_z[i, 0] + got_z[i, 1] + got_z[i, 2]
    sum_y_o[...] = late_o[1, :, half : 2 * half, :] + got_y[0] + got_y[1]


def middle_call(gated, dgated, sums, gate_z, w, tw, gain, tgain):
    length, width = gated.shape
    cols = w.shape[1]
    blk = cols // 4
    half = blk // 8
    out = lambda *s: jax.ShapeDtypeStruct(s, F32)
    dma = pltpu.SemaphoreType.DMA
    return pl.pallas_call(
        middle_kernel,
        in_specs=[VMEM] * 8,
        out_specs=[VMEM] * 5,
        out_shape=[
            out(length, width), out(8, width), out(2, half, width), out(4, half, width),
            out(2, 4, blk // 4, width),
        ],
        scratch_shapes=[
            pltpu.VMEM((8, 2, length), F32),
            pltpu.VMEM((8, length), F32),
            pltpu.VMEM((length, 2 * width), BF16),
            pltpu.VMEM((2, 4, 2, 128, blk), F32),
            pltpu.VMEM((4, 4, 128, blk), F32),
            pltpu.VMEM((4, 128, blk), BF16),
            pltpu.VMEM((4, 128, blk), BF16),
            pltpu.VMEM((4, 2, 128, blk), BF16),
            pltpu.VMEM((4, 2, 128, blk), BF16),
            pltpu.VMEM((4, length, blk), BF16),
            pltpu.VMEM((length, width), F32),
            pltpu.VMEM((2, 4, blk // 4, width), F32),
            pltpu.VMEM((2, 3, half, width), F32),
            pltpu.VMEM((2, 4, half, width), F32),
            pltpu.VMEM((8, 128), F32),
            pltpu.VMEM((8, 8, 128), F32),
            pltpu.VMEM((8, width), F32),
            dma((8,)), dma((8,)), dma((4,)), dma((4,)), dma((4,)), dma((4,)),
            dma((4, 2)), dma((4, 2)), dma((4, 7)), dma((4, 7)), dma((8,)), dma((8,)),
            dma((2, 4)), dma((2, 4)), dma((2,)), dma((2,)),
        ],
        compiler_params=pltpu.CompilerParams(
            collective_id=3, has_side_effects=True, vmem_limit_bytes=61 * 1024 * 1024
        ),
        name="probe_and_back",
    )(gated, dgated, sums, gate_z, w, tw, gain, tgain)


def fold(a):
    return jnp.sum(a.reshape(a.shape[0] // 8, 8, a.shape[1]), axis=0)


def adjoint_kernel(
    by, x, gx, pre_x, halo_x, bc, gbc, pre_bc, halo_bc, rowv, colv, s0_b, log, last_log,
    gain, decays, hp, sum_z, sum_y, late,
    result_o,
    wx, wbc, head_o, pack_o, lam, back_u_a, back_bc_a, state, msg, landed, answer, s_end,
    own_z, own_y, got_z, got_y, end_z, end_y, pack_z, landed_z, landed_y, part, landed_q,
    az_s, az_r, ay_s, ay_r, bz_s, bz_r, by_s, by_r,
    s1_s, s1_r, s2_s, s2_r, f1_s, f1_r, f3_s, f3_r, f2_s, f2_r,
):
    step = pl.program_id(0)
    half = lam.shape[0]
    nst = bc.shape[1] // 2
    width = by.shape[1]
    heads = width // HW
    count, n_head = landed.shape[0], landed_q.shape[0]
    me, head = lax.axis_index("seq"), lax.axis_index("head")
    my_y, my_z = me // 4, lax.rem(me, 4)
    seq_peers, head_peers = others("seq", count), others("head", n_head)
    rows_half = sum_z.shape[1]
    mask = lane_mask()

    y_peers = [{"seq": lax.rem(my_y + k, 4) * 4 + my_z} for k in range(1, 4)]
    z_peers = [{"seq": my_y * 4 + lax.rem(my_z + k, 4)} for k in range(1, 4)]

    def late_copies(part_at):
        copies = []
        for i, k in ((0, 1), (0, 3)) if part_at % 2 == 0 else ((0, 2),):
            i = i + part_at // 2
            copies.append(
                link(
                    late.at[i, lax.rem(my_z + k, 4), 0:rows_half, :], got_z.at[i, k - 1],
                    az_s.at[i, k], az_r.at[i, k], z_peers[k - 1],
                )
            )
        copies.append(
            link(
                late.at[0, part_at, rows_half : 2 * rows_half, :], got_y.at[part_at],
                ay_s.at[part_at], ay_r.at[part_at], y_peers[TURN[2] - 1],
            )
        )
        return copies

    def early_last():
        return [
            link(sum_z.at[i], end_z.at[i], bz_s.at[i], bz_r.at[i], y_peers[TURN[i] - 1])
            for i in range(2)
        ]

    def last_copies():
        copies = [link(own_z, end_z.at[2], bz_s.at[2], bz_r.at[2], y_peers[TURN[2] - 1])]
        for k in (2, 1, 3):
            z = lax.rem(my_z + k, 4)
            copies.append(
                link(own_y.at[z], end_y.at[k - 1], by_s.at[k], by_r.at[k], z_peers[k - 1])
            )
        return copies

    for part_at, when in enumerate((0, 3, half + SCAN_AT + 1, half + SCAN_AT + 2)):

        @pl.when(step == when)
        def _(part_at=part_at):
            if part_at == 0:
                greet([{"seq": to} for to in seq_peers] + [{"head": to} for to in head_peers])
            for copy in late_copies(part_at) + (early_last() if part_at == 3 else []):
                copy.start()

    @pl.when(step == 0)
    def _():
        state[...] = jnp.zeros_like(state)
        head_o[...] = jnp.zeros_like(head_o)
        pack_o[...] = jnp.zeros_like(pack_o)
        pack_o[8:9, :] = jnp.sum(gain[...], axis=0, keepdims=True)

    @pl.when(step < half)
    def _():
        lam[half - 1 - step] = state[...]
        cols = colv[...]
        ct_h, ct_l = split(bc[:, nst:].T)
        for p in range(heads // 2):
            at = slice(128 * p, 128 * p + 128)
            lifted = jnp.exp(expand(cols, C_, p)) * by[:, at]
            l_h, l_l = split(lifted)
            add = nn(ct_h, l_h) + nn(ct_h, l_l) + nn(ct_l, l_h)
            state[:, at] = jnp.exp(log[0, 2:3, at]) * state[:, at] + add

    def scan_copies():
        return [
            link(msg.at[to], landed.at[me], s1_s.at[k], s1_r.at[k], {"seq": to})
            for k, to in enumerate(seq_peers)
        ]

    def back_copies():
        return [
            link(answer.at[to], s_end.at[me], s2_s.at[k], s2_r.at[k], {"seq": to})
            for k, to in enumerate(seq_peers)
        ]

    @pl.when(step == half - 1)
    def _():
        msg[...] = state[...].reshape(count, 8, width)
        for copy in scan_copies():
            copy.start()

    @pl.when(step == half + SCAN_AT)
    def _():
        landed[me] = msg[me]
        for copy in scan_copies():
            copy.wait()
        adjoint = jnp.zeros((8, width), F32)
        for i in range(count - 1, -1, -1):
            answer[i] = adjoint
            adjoint = decays[i : i + 1, :] * adjoint + landed[i]
        for copy in back_copies():
            copy.start()

    @pl.when((step >= half) & (step < 2 * half))
    def _():
        block = step - half
        b_mat, c_mat = bc[:, :nst], bc[:, nst:]
        at_i = lax.broadcasted_iota(jnp.int32, (QB, QB), 1)
        at_j = lax.broadcasted_iota(jnp.int32, (QB, QB), 0)
        keep = at_i >= at_j
        inner_t = jnp.where(keep, nt3(b_mat, c_mat), 0.0)
        cols = colv[...]
        rows = rowv[...]
        back_inner_t = jnp.zeros((QB, QB), F32)
        for p in range(heads // 2):
            at = slice(128 * p, 128 * p + 128)
            byp = by[:, at]
            u = expand(cols, S_, p) * x[:, at]
            y_h, y_l = split(byp)
            u_h, u_l = split(
                jnp.concatenate([jnp.where(mask, u, 0.0), jnp.where(mask, 0.0, u)], axis=0)
            )
            back_mts = nt(
                jnp.concatenate([u_h, u_l], axis=1), jnp.concatenate([y_h, y_h], axis=1)
            ) + nt(u_h, y_l)
            mats = []
            for s in range(2):
                h = 2 * p + s
                c_row = rows[C_ + h : C_ + h + 1, :]
                cs_row = rows[CS_ + h : CS_ + h + 1, :]
                back_mt = back_mts[s * QB : s * QB + QB]
                diff = jnp.minimum(c_row - bcast(cols, C_ + h), 0.0)
                level = jnp.exp(diff)
                back_inner_t = back_inner_t + level * back_mt
                m_t = inner_t * level
                prod = m_t * back_mt
                head_o[h, 0] = head_o[h, 0] + fold(prod * diff)
                head_o[h, 1] = head_o[h, 1] + fold(prod * (cs_row - bcast(cols, CS_ + h)))
                mats.append(m_t)
            a_h, a_l = split(jnp.concatenate(mats, axis=0))
            back_u2 = nn(
                jnp.concatenate([a_h, a_l], axis=1), jnp.concatenate([y_h, y_h], axis=0)
            ) + nn(a_h, y_l)
            back_u_a[block, :, at] = jnp.where(mask, back_u2[:QB], back_u2[QB:])
        back_inner_t = jnp.where(keep, back_inner_t, 0.0)
        back_bc_a[block, :, 0:nst] = nn3(back_inner_t, c_mat)
        back_bc_a[block, :, nst:] = nn3(back_inner_t.T, b_mat)

    @pl.when(step == 2 * half)
    def _():
        s_end[me] = answer[me]
        for copy in back_copies():
            copy.wait()

    @pl.when(step >= 2 * half)
    def _():
        block = step - 2 * half
        load_window(wx, halo_x, pre_x, step == 2 * half)
        load_window(wbc, halo_bc, pre_bc, step == 2 * half)
        b_h, b_l = split(bc[:, :nst])
        c_h, c_l = split(bc[:, nst:])
        cols = colv[...]
        back_b = back_bc_a[block, :, 0:nst]
        back_c = back_bc_a[block, :, nst:]
        for p in range(heads // 2):
            at = slice(128 * p, 128 * p + 128)
            own, sig_own = log[0, 2:3, at], log[0, 4:5, at]
            reach = jnp.exp(last_log[0, 0:1, at] + last_log[0, 2:3, at] - log[0, 0:1, at] - own)
            s1 = lam[block, :, at] + reach * s_end[:, :, at].reshape(nst, 128)
            s0 = s0_b[0, :, at]
            byp, xp = by[:, at], x[:, at]
            size = expand(cols, S_, p)
            c_cols, cs_cols = expand(cols, C_, p), expand(cols, CS_, p)
            left = own - c_cols
            to_end = jnp.exp(left)
            u = size * xp
            lifted = jnp.exp(c_cols) * byp
            s0_h, s0_l = split(s0)
            s1_h, s1_l = split(s1)
            l_h, l_l = split(lifted)
            e_h, e_l = split(to_end * u)
            back_c = back_c + nt(
                jnp.concatenate([l_h, l_l], axis=1), jnp.concatenate([s0_h, s0_h], axis=1)
            ) + nt(l_h, s0_l)
            back_b = back_b + nt(
                jnp.concatenate([e_h, e_l], axis=1), jnp.concatenate([s1_h, s1_h], axis=1)
            ) + nt(e_h, s1_l)
            through_c = lifted * (nn(c_h, s0_h) + nn(c_h, s0_l) + nn(c_l, s0_h))
            from_end = to_end * (nn(b_h, s1_h) + nn(b_h, s1_l) + nn(b_l, s1_h))
            through_b = u * from_end
            back_u = back_u_a[block, :, at] + from_end
            back_x = back_u * size + expand(hp[2:3, :], 0, p) * byp
            carried = jnp.sum(s1 * s0, axis=0, keepdims=True) * jnp.exp(own)
            total = lambda a: jnp.sum(a, axis=0, keepdims=True)
            pack_o[4:5, at] = pack_o[4:5, at] + total(expand(cols, SG_, p) * (back_u * xp))
            pack_o[5:6, at] = (
                pack_o[5:6, at] + carried * own + total(through_c * c_cols + through_b * left)
            )
            pack_o[6:7, at] = (
                pack_o[6:7, at]
                + carried * sig_own
                + total(through_c * cs_cols + through_b * (sig_own - cs_cols))
            )
            pack_o[7:8, at] = pack_o[7:8, at] + total(byp * xp)
            back_z = back_x * gx[:, at]
            for k in range(4):
                pack_o[k : k + 1, at] = pack_o[k : k + 1, at] + total(
                    back_z * wx[5 + k : 5 + k + QB, at]
                )
        back_zbc = jnp.concatenate([back_b, back_c], axis=1) * gbc[...]
        for k in range(4):
            pack_o[9 + k : 10 + k, 0 : 2 * nst] = pack_o[
                9 + k : 10 + k, 0 : 2 * nst
            ] + jnp.sum(back_zbc * wbc[5 + k : 5 + k + QB, :], axis=0, keepdims=True)

    @pl.when(step == 3 * half - 5)
    def _():
        for part_at in range(4):
            for copy in late_copies(part_at):
                copy.wait()
        own_z[...] = late[0, my_z, 0:rows_half, :] + got_z[0, 0] + got_z[0, 1] + got_z[0, 2]
        own_y[...] = sum_y[...] + got_y[...]
        for copy in last_copies():
            copy.start()

    @pl.when(step == 3 * half - 1)
    def _():
        for p in range(heads // 2):
            at = slice(128 * p, 128 * p + 128)
            for kind in range(2):
                even, odd = head_o[2 * p, kind], head_o[2 * p + 1, kind]
                even = even + pltpu.roll(even, HW, 1)
                odd = odd + pltpu.roll(odd, HW, 1)
                both = jnp.sum(jnp.where(mask, even, odd), axis=0, keepdims=True)
                pack_o[5 + kind : 6 + kind, at] = pack_o[5 + kind : 6 + kind, at] + both
        for slots, group, sems, mine in (
            (landed_z, z_peers, (f1_s, f1_r), pack_o),
            (landed_y, y_peers, (f3_s, f3_r), pack_z),
        ):
            copies = []
            for k, to in enumerate(group):
                copies.append(send(mine, slots.at[k], sems[0].at[k], sems[1].at[k], to))
            for copy in copies:
                copy.wait()
            if slots is landed_z:
                for z in range(4):
                    k = lax.rem(my_z + 3 - z, 4)
                    term = jnp.where(z == my_z, pack_o[...], slots[jnp.minimum(k, 2)])
                    total = term if z == 0 else total + term
                pack_z[...] = total
            else:
                for y in range(4):
                    k = lax.rem(my_y + 3 - y, 4)
                    term = jnp.where(y == my_y, pack_z[...], slots[jnp.minimum(k, 2)])
                    total = term if y == 0 else total + term
        part[...] = total[8:16, 0 : 2 * nst]
        copies = []
        for k, to in enumerate(head_peers):
            copies.append(send(part, landed_q.at[head], f2_s.at[k], f2_r.at[k], {"head": to}))
        landed_q[head] = part[...]
        result_o[2 * rows_half : 2 * rows_half + 16] = total
        at = lax.broadcasted_iota(jnp.int32, (width, 128), 0)
        to = lax.broadcasted_iota(jnp.int32, (width, 128), 1) * HW
        pick = jnp.where((at >= to) & (at < to + HW), 1.0, 0.0).astype(F32)
        sums = jnp.dot(
            total, pick, precision=lax.Precision.HIGHEST, preferred_element_type=F32
        )[:, :heads]
        at = 2 * rows_half + 24
        result_o[at : at + 1, 0:heads] = sums[4:5] - jnp.exp(hp[1:2]) * sums[6:7]
        result_o[at + 1 : at + 2, 0:heads] = sums[5:6]
        result_o[at + 2 : at + 3, 0:heads] = sums[7:8]
        for copy in early_last() + last_copies():
            copy.wait()
        total = late[1, my_z, 0:rows_half, :] + got_z[1, 0] + got_z[1, 1] + got_z[1, 2]
        result_o[0:rows_half] = total + end_z[0] + end_z[1] + end_z[2]
        result_o[rows_half : 2 * rows_half] = own_y[my_z] + end_y[0] + end_y[1] + end_y[2]
        for copy in copies:
            copy.wait()
        total2 = landed_q[0]
        for i in range(1, n_head):
            total2 = total2 + landed_q[i]
        result_o[2 * rows_half + 16 : 2 * rows_half + 24, 0 : 2 * nst] = total2


def adjoint_call(
    by, x, gx, pre_x, halo_x, bc, gbc, pre_bc, halo_bc, rowv, colv, s0, logs, gain, decays,
    hp, sum_z, sum_y, late_sums, count, n_head,
):
    length, width = by.shape
    wide = bc.shape[1]
    nst = wide // 2
    heads = width // HW
    half = length // QB
    rows_half = sum_z.shape[1]
    piece = 2 * rows_half
    every = lambda i: jnp.where(i < half, half - 1 - i, lax.rem(i, half))
    mid = lambda i: jnp.where(i < half, 0, lax.rem(i, half))
    late = lambda i: jnp.maximum(i - 2 * half, 0)
    whole = lambda a: pl.BlockSpec(a.shape, lambda i: (0,) * a.ndim)
    rows = lambda w, f: pl.BlockSpec((QB, w), lambda i: (f(i), 0))
    cube = lambda r, f: pl.BlockSpec((1, r, width), lambda i: (f(i), 0, 0))
    out = lambda *s: jax.ShapeDtypeStruct(s, F32)
    fixed = lambda *s: pl.BlockSpec(s, lambda i: (0,) * len(s))
    dma = pltpu.SemaphoreType.DMA
    return pl.pallas_call(
        adjoint_kernel,
        grid=(3 * half,),
        in_specs=[
            rows(width, every), rows(width, mid), rows(width, late), rows(width, late),
            whole(halo_x), rows(wide, every), rows(wide, late), rows(wide, late), whole(halo_bc),
            pl.BlockSpec((128, QB), lambda i: (0, mid(i))), rows(128, every),
            cube(nst, late), cube(8, every),
            pl.BlockSpec((1, 8, width), lambda i: (half - 1, 0, 0)),
            whole(gain), whole(decays), whole(hp),
            whole(sum_z), whole(sum_y), VMEM,
        ],
        out_specs=fixed(256, width),
        out_shape=out(256, width),
        scratch_shapes=[
            pltpu.VMEM((QB + 8, width), F32), pltpu.VMEM((QB + 8, wide), F32),
            pltpu.VMEM((heads, 2, 8, 128), F32), pltpu.VMEM((16, width), F32),
            pltpu.VMEM((half, nst, width), F32), pltpu.VMEM((half, QB, width), F32),
            pltpu.VMEM((half, QB, wide), F32), pltpu.VMEM((nst, width), F32),
            pltpu.VMEM((count, 8, width), F32), pltpu.VMEM((count, 8, width), F32),
            pltpu.VMEM((count, 8, width), F32), pltpu.VMEM((count, 8, width), F32),
            pltpu.VMEM((rows_half, width), F32), pltpu.VMEM((4, rows_half, width), F32),
            pltpu.VMEM((2, 3, rows_half, width), F32), pltpu.VMEM((4, rows_half, width), F32),
            pltpu.VMEM((3, rows_half, width), F32), pltpu.VMEM((3, rows_half, width), F32),
            pltpu.VMEM((16, width), F32), pltpu.VMEM((3, 16, width), F32),
            pltpu.VMEM((3, 16, width), F32), pltpu.VMEM((8, wide), F32),
            pltpu.VMEM((n_head, 8, wide), F32),
            dma((2, 4)), dma((2, 4)), dma((4,)), dma((4,)),
            dma((4,)), dma((4,)), dma((4,)), dma((4,)),
            dma((count,)), dma((count,)), dma((count,)), dma((count,)),
            dma((3,)), dma((3,)), dma((3,)), dma((3,)), dma((n_head,)), dma((n_head,)),
        ],
        compiler_params=pltpu.CompilerParams(
            collective_id=2, has_side_effects=True, vmem_limit_bytes=LIMIT
        ),
        name="adjoint",
    )(
        by, x, gx, pre_x, halo_x, bc, gbc, pre_bc, halo_bc, rowv, colv, s0, logs, logs,
        gain, decays, hp, sum_z, sum_y, late_sums,
    )


def outputs_kernel(result, gcx_o, gcbc_o, heads_o, gain_o, gnw_o):
    piece, heads, wide = gnw_o.shape[0], heads_o.shape[1], gcbc_o.shape[1]
    width = result.shape[1]
    gcx_o[...] = result[piece : piece + 4]
    gain_o[...] = result[piece + 8 : piece + 9].reshape(width)
    gcbc_o[...] = result[piece + 17 : piece + 21, 0:wide]
    heads_o[...] = result[piece + 24 : piece + 27, 0:heads]
    gnw_o[...] = result[0:piece]


def outputs_call(result, piece, bc_shape, heads_shape):
    width = result.shape[1]
    out = lambda *s: jax.ShapeDtypeStruct(s, F32)
    return pl.pallas_call(
        outputs_kernel,
        in_specs=[VMEM],
        out_specs=[VMEM] * 5,
        out_shape=[
            out(4, width), out(*bc_shape), out(*heads_shape), out(width), out(piece, width),
        ],
        name="outputs",
    )(result)


def on_device(
    pre_x, pre_bc, gate_z, dt_raw, conv_x, conv_bc, head_params, norm_gain, w_out,
    t_conv_x, t_conv_bc, t_heads, t_gain, t_wout,
):
    count = lax.axis_size("seq")
    t_wout_all = lax.all_gather(t_wout.T, "seq", axis=0, tiled=True)
    x, gx, bc, gbc, rowv, colv, logs, s0, gated, d_gated, sums, decays, halo_x, halo_bc = forward_call(
        pre_x, pre_bc, dt_raw, gate_z, conv_x, t_conv_x, conv_bc, t_conv_bc, head_params, t_heads,
        count,
    )
    back_y, gain_part, sum_z, sum_y, late_sums = middle_call(
        gated, d_gated, sums, gate_z, w_out, t_wout_all, norm_gain, t_gain
    )
    result = adjoint_call(
        back_y, x, gx, pre_x, halo_x, bc, gbc, pre_bc, halo_bc, rowv, colv, s0, logs,
        gain_part, decays, head_params, sum_z, sum_y, late_sums, count, lax.axis_size("head"),
    )
    gn_conv_x, gn_conv_bc, gn_heads, gn_gain, gn_wout = outputs_call(
        result, t_wout.shape[1], conv_bc.shape, head_params.shape
    )
    return gn_conv_x, gn_conv_bc, gn_heads, gn_gain, gn_wout.T


def solution(mesh):
    in_specs = (
        P("seq", "head"), P("seq", None), P("seq", "head"), P("head", "seq"), P(None, "head"),
        P(), P(None, "head"), P("head"), P("head", None), P(None, "head"), P(), P(None, "head"),
        P("head"), P("head", "seq"),
    )
    out_specs = (P(None, "head"), P(), P(None, "head"), P("head"), P("head", "seq"))
    return jax.shard_map(
        on_device, mesh=mesh, in_specs=in_specs, out_specs=out_specs, check_vma=False
    )
```

```python
import jax
import jax.numpy as jnp
from jax import lax
from jax.experimental import pallas as pl
from jax.experimental.pallas import tpu as pltpu
from jax.sharding import PartitionSpec as P

QB = 128
HW = 64
F32 = jnp.float32
BF16 = jnp.bfloat16
MESH = pl.DeviceIdType.MESH
S_, DS_, C_, DC_, CS_, SG_, K_, DK_ = (16 * i for i in range(8))
LIMIT = 56 * 1024 * 1024
SCAN_AT = 4
TURN = (1, 3, 2, 4)


def split(a):
    high = a.astype(BF16)
    return high, (a - high.astype(F32)).astype(BF16)


def nn(a, b):
    return jnp.dot(a, b, preferred_element_type=F32)


def nt(a, b):
    return lax.dot_general(a, b, (((1,), (1,)), ((), ())), preferred_element_type=F32)


def nn3(a, b):
    (ah, al), (bh, bl) = split(a), split(b)
    return nn(ah, bh) + nn(ah, bl) + nn(al, bh)


def nt3(a, b):
    (ah, al), (bh, bl) = split(a), split(b)
    return nt(ah, bh) + nt(ah, bl) + nt(al, bh)


def lane_mask():
    return lax.broadcasted_iota(jnp.int32, (1, 128), 1) < HW


def bcast(cols, at):
    return jnp.broadcast_to(cols[:, at : at + 1], (cols.shape[0], 128))


def expand(cols, base, pair):
    return jnp.where(
        lane_mask(), bcast(cols, base + 2 * pair), bcast(cols, base + 2 * pair + 1)
    )


def expand_all(cols, base, heads):
    return jnp.concatenate([expand(cols, base, p) for p in range(heads // 2)], axis=1)


def load_window(window, halo, block, first):
    @pl.when(first)
    def _():
        window[0:8] = halo[...]

    @pl.when(jnp.logical_not(first))
    def _():
        window[0:8] = window[QB : QB + 8]

    window[8 : QB + 8] = block[...].astype(F32)


def conv_pair(window, weight, t_weight):
    z = jnp.zeros((QB, window.shape[1]), F32)
    dz = jnp.zeros((QB, window.shape[1]), F32)
    for k in range(4):
        rows = window[5 + k : 5 + k + QB, :]
        z = z + weight[k : k + 1, :] * rows
        dz = dz + t_weight[k : k + 1, :] * rows
    sig = jax.nn.sigmoid(z)
    slope = sig * (1.0 + z * (1.0 - sig))
    return z * sig, slope * dz, slope


def greet(peers):
    barrier = pltpu.get_barrier_semaphore()
    for peer in peers:
        pl.semaphore_signal(barrier, inc=1, device_id=peer, device_id_type=MESH)
    pl.semaphore_wait(barrier, len(peers))


def others(axis, count):
    me = lax.axis_index(axis)
    return [lax.rem(me + k, count) for k in range(1, count)]


def link(src, dst, send_sem, recv_sem, device):
    return pltpu.make_async_remote_copy(
        src_ref=src, dst_ref=dst, send_sem=send_sem, recv_sem=recv_sem,
        device_id=device, device_id_type=MESH,
    )


def send(*what):
    copy = link(*what)
    copy.start()
    return copy


VMEM = pl.BlockSpec(memory_space=pltpu.VMEM)


def column_of(row):
    heads = row.shape[1]
    at_i = lax.broadcasted_iota(jnp.int32, (heads, heads), 0)
    at_j = lax.broadcasted_iota(jnp.int32, (heads, heads), 1)
    return jnp.sum(jnp.where(at_i == at_j, row, 0.0), axis=1, keepdims=True)


def forward_kernel(
    pre_x, tail_x, pre_bc, tail_bc, dt, gate_z, cx, tcx, cbc, tcbc, hp, th, tw_in,
    x_o, gx_o, bc_o, gbc_o, row_o, col_o, log_o, s0_o, gated_o, dgated_o, sums_o, decay_o,
    halo_x_o, halo_bc_o, tw_o,
    wx, wbc, feat, state, d_state, logs, x_a, dx_a, bc_a, dbc_a, row_a, col_a, st_a, dst_a,
    log_a, y_a, dy_a, tile, got_x, got_bc, msg, landed, tiles, answer, start,
    halo_s, halo_r, tile_s, tile_r, s1_s, s1_r, s2_s, s2_r,
    own_m, gz_s, gz_r, gy_s, gy_r, hz_s, hz_r, hy_s, hy_r,
):
    step = pl.program_id(0)
    blocks = st_a.shape[0]
    heads = dt.shape[0]
    width = pre_x.shape[1]
    nst = cbc.shape[1] // 2
    count = landed.shape[0]
    me = lax.axis_index("seq")
    peers = others("seq", count)
    mask = lane_mask()

    my_y, my_z = me // 4, lax.rem(me, 4)
    y_peers = [{"seq": lax.rem(my_y + k, 4) * 4 + my_z} for k in range(1, 4)]
    z_peers = [{"seq": my_y * 4 + lax.rem(my_z + k, 4)} for k in range(1, 4)]
    piece = tw_in.shape[0]
    upper_rows, lower_rows = slice(0, piece // 2), slice(piece // 2, piece)

    def own_copy():
        return pltpu.make_async_copy(tw_in, tw_o.at[my_y, my_z], own_m.at[0])

    def gather_first():
        copies = []
        for k in (2, 1, 3):
            copies.append(
                link(
                    tw_in.at[upper_rows, :], tw_o.at[my_y, my_z, upper_rows, :],
                    gz_s.at[k], gz_r.at[k], z_peers[k - 1],
                )
            )
            copies.append(
                link(
                    tw_in.at[lower_rows, :], tw_o.at[my_y, my_z, lower_rows, :],
                    gy_s.at[k], gy_r.at[k], y_peers[k - 1],
                )
            )
        return copies

    def gather_second(k):
        along_y = tw_o.at[my_y, :, upper_rows, :]
        along_z = tw_o.at[:, my_z, lower_rows, :]
        return [
            link(along_y, along_y, hz_s.at[k], hz_r.at[k], y_peers[k - 1]),
            link(along_z, along_z, hy_s.at[k], hy_r.at[k], z_peers[k - 1]),
        ]

    def scan_copies():
        copies = []
        for k, to in enumerate(peers):
            at = {"seq": to}
            copies.append(link(tile, tiles.at[me], tile_s.at[k], tile_r.at[k], at))
            copies.append(link(msg.at[to], landed.at[me], s1_s.at[k], s1_r.at[k], at))
        return copies

    def back_copies():
        return [
            link(answer.at[to], start.at[me], s2_s.at[k], s2_r.at[k], {"seq": to})
            for k, to in enumerate(peers)
        ]

    @pl.when(step == 0)
    def _():
        greet([{"seq": to} for to in peers])
        after = {"seq": lax.rem(me + 1, count)}
        tails = [
            send(tail_x, got_x, halo_s.at[0], halo_r.at[0], after),
            send(tail_bc, got_bc, halo_s.at[1], halo_r.at[1], after),
        ]
        state[...] = jnp.zeros_like(state)
        d_state[...] = jnp.zeros_like(d_state)
        logs[...] = jnp.zeros_like(logs)
        feat[...] = jnp.zeros_like(feat)
        tile[...] = jnp.zeros_like(tile)
        for copy in tails:
            copy.wait()
        halo_x_o[...] = jnp.where(me == 0, 0.0, got_x[...].astype(F32)[8:16])
        halo_bc_o[...] = jnp.where(me == 0, 0.0, got_bc[...].astype(F32)[8:16])
        own_copy().start()
        for copy in gather_first():
            copy.start()

    @pl.when(step == 3)
    def _():
        own_copy().wait()
        for copy in gather_first():
            copy.wait()
        for copy in gather_second(1) + gather_second(3):
            copy.start()

    @pl.when(step == blocks + SCAN_AT + 1)
    def _():
        for copy in gather_second(2):
            copy.start()

    @pl.when(step == 3 * blocks - 1)
    def _():
        for k in (1, 3, 2):
            for copy in gather_second(k):
                copy.wait()

    @pl.when(step < blocks)
    def _():
        load_window(wx, halo_x_o, pre_x, step == 0)
        load_window(wbc, halo_bc_o, pre_bc, step == 0)
        z = dt[...] + column_of(hp[0:1, :])
        rate = jnp.exp(column_of(hp[1:2, :]))
        t_bias, t_lrate = column_of(th[0:1, :]), column_of(th[1:2, :])
        size = jnp.maximum(z, 0.0) + jnp.log1p(jnp.exp(-jnp.abs(z)))
        sig = jax.nn.sigmoid(z)
        log_decay = -size * rate
        at_i = lax.broadcasted_iota(jnp.int32, (QB, QB), 1)
        at_j = lax.broadcasted_iota(jnp.int32, (QB, QB), 0)
        upper = jnp.where(at_j <= at_i, 1.0, 0.0).astype(F32)
        exact = dict(precision=lax.Precision.HIGHEST, preferred_element_type=F32)
        cumul = jnp.dot(log_decay, upper, **exact)
        sig_sum = jnp.dot(sig, upper, **exact)
        d_size = sig * t_bias
        d_cumul = cumul * t_lrate - rate * t_bias * sig_sum
        to_end = jnp.exp(cumul[:, QB - 1 : QB] - cumul)
        feat[S_ : S_ + heads] = size
        feat[DS_ : DS_ + heads] = d_size
        feat[C_ : C_ + heads] = cumul
        feat[DC_ : DC_ + heads] = d_cumul
        feat[CS_ : CS_ + heads] = sig_sum
        feat[SG_ : SG_ + heads] = sig
        feat[K_ : K_ + heads] = to_end * size
        feat[DK_ : DK_ + heads] = to_end * (
            d_size + size * (d_cumul[:, QB - 1 : QB] - d_cumul)
        )
        rows = feat[...]
        cols = rows.T
        row_o[...] = rows
        col_o[...] = cols
        row_a[step] = rows
        col_a[step] = cols

        bc, dbc, gbc = conv_pair(wbc, cbc, tcbc)
        bc_o[...] = bc
        gbc_o[...] = gbc
        bc_a[step] = bc
        dbc_a[step] = dbc
        x, dx, gx = conv_pair(wx, cx, tcx)
        x_o[...] = x
        gx_o[...] = gx
        x_a[step] = x
        dx_a[step] = dx

        last = cols[QB - 1 : QB, :]
        tile[0:1, :] = tile[0:1, :] + last
        own = expand_all(last, C_, heads)
        d_own = expand_all(last, DC_, heads)
        log = jnp.concatenate(
            [logs[0:1, :], logs[1:2, :], own, d_own, expand_all(last, CS_, heads)]
            + [jnp.zeros((3, width), F32)],
            axis=0,
        )
        log_o[0] = log
        log_a[step] = log
        logs[0:1, :] = logs[0:1, :] + own
        logs[1:2, :] = logs[1:2, :] + d_own

        st_a[step] = state[...]
        dst_a[step] = d_state[...]
        bt = bc[:, :nst].T
        dbt = dbc[:, :nst].T
        both_h, both_l = split(jnp.concatenate([bt, dbt], axis=1))
        for p in range(heads // 2):
            at = slice(128 * p, 128 * p + 128)
            k_x, dk_x = expand(cols, K_, p), expand(cols, DK_, p)
            ux = k_x * x[:, at]
            dux = k_x * dx[:, at] + dk_x * x[:, at]
            z_h, z_l = split(jnp.concatenate([dux, ux], axis=0))
            d_add = nn(both_h, z_h) + nn(both_h, z_l) + nn(both_l, z_h)
            b_h, b_l, u_h, u_l = both_h[:, :QB], both_l[:, :QB], z_h[QB:], z_l[QB:]
            add = nn(b_h, u_h) + nn(b_h, u_l) + nn(b_l, u_h)
            decay = jnp.exp(own[:, at])
            before = state[:, at]
            d_state[:, at] = decay * (d_state[:, at] + d_own[:, at] * before) + d_add
            state[:, at] = decay * before + add

    @pl.when(step == blocks - 1)
    def _():
        msg[:, 0:8, :] = state[...].reshape(count, 8, width)
        msg[:, 8:16, :] = d_state[...].reshape(count, 8, width)
        for copy in scan_copies():
            copy.start()

    @pl.when(step == blocks + SCAN_AT)
    def _():
        landed[me] = msg[me]
        tiles[me] = tile[...]
        for copy in scan_copies():
            copy.wait()
        total = jnp.zeros((8, width), F32)
        d_total = jnp.zeros((8, width), F32)
        features = tiles[...][:, 0, :]
        decays = jnp.exp(expand_all(features, C_, heads))
        d_logs = expand_all(features, DC_, heads)
        decay_o[...] = decays
        for i in range(count):
            answer[i, 0:8] = total
            answer[i, 8:16] = d_total
            decay = decays[i : i + 1]
            d_total = decay * (d_total + d_logs[i : i + 1] * total)
            d_total = d_total + landed[i, 8:16]
            total = decay * total + landed[i, 0:8]
        for copy in back_copies():
            copy.start()

    @pl.when((step >= blocks) & (step < 2 * blocks))
    def _():
        block = step - blocks
        bc, dbc = bc_a[block], dbc_a[block]
        b_mat, c_mat = bc[:, :nst], bc[:, nst:]
        db_mat, dc_mat = dbc[:, :nst], dbc[:, nst:]
        at_j = lax.broadcasted_iota(jnp.int32, (QB, QB), 1)
        at_i = lax.broadcasted_iota(jnp.int32, (QB, QB), 0)
        keep = at_i >= at_j
        inner = jnp.where(keep, nt3(c_mat, b_mat), 0.0)
        d_inner = jnp.where(
            keep,
            nt3(
                jnp.concatenate([dc_mat, c_mat], axis=1),
                jnp.concatenate([b_mat, db_mat], axis=1),
            ),
            0.0,
        )
        cols = col_a[block]
        rows = row_a[block]
        for p in range(heads // 2):
            at = slice(128 * p, 128 * p + 128)
            xp, dxp = x_a[block, :, at], dx_a[block, :, at]
            size, d_size = expand(cols, S_, p), expand(cols, DS_, p)
            z_h, z_l = split(size * xp)
            dz_h, dz_l = split(size * dxp + d_size * xp)
            mats, d_mats = [], []
            for h in (2 * p, 2 * p + 1):
                c_row = rows[C_ + h : C_ + h + 1, :]
                dc_row = rows[DC_ + h : DC_ + h + 1, :]
                level = jnp.exp(jnp.minimum(bcast(cols, C_ + h) - c_row, 0.0))
                m = inner * level
                mats.append(m)
                d_mats.append(d_inner * level + m * (bcast(cols, DC_ + h) - dc_row))
            a_h, a_l = split(jnp.concatenate(mats, axis=0))
            da_h, da_l = split(jnp.concatenate(d_mats, axis=0))
            zz_h = jnp.concatenate([z_h, dz_h], axis=1)
            big = nn(
                jnp.concatenate([a_h, a_l], axis=1), jnp.concatenate([zz_h, zz_h], axis=0)
            ) + nn(a_h, jnp.concatenate([z_l, dz_l], axis=1))
            small = nn(
                jnp.concatenate([da_h, da_l], axis=1), jnp.concatenate([z_h, z_h], axis=0)
            ) + nn(da_h, z_l)
            y2 = big[:, :128]
            dy2 = big[:, 128:] + small
            skip, d_skip = expand(hp[2:3, :], 0, p), expand(th[2:3, :], 0, p)
            y_a[block, :, at] = jnp.where(mask, y2[:QB], y2[QB:]) + skip * xp
            dy_a[block, :, at] = (
                jnp.where(mask, dy2[:QB], dy2[QB:]) + skip * dxp + d_skip * xp
            )

    @pl.when(step == 2 * blocks)
    def _():
        start[me] = answer[me]
        for copy in back_copies():
            copy.wait()

    @pl.when(step >= 2 * blocks)
    def _():
        block = step - 2 * blocks
        cols = col_a[block]
        c_h, c_l = split(bc_a[block][:, nst:])
        dc_h, dc_l = split(dbc_a[block][:, nst:])
        squares = jnp.zeros((QB, 128), F32)
        crossed = jnp.zeros((QB, 128), F32)
        for p in range(heads // 2):
            at = slice(128 * p, 128 * p + 128)
            reach = jnp.exp(log_a[block, 0:1, at])
            s_in = start[:, 0:8, at].reshape(nst, 128)
            ds_in = start[:, 8:16, at].reshape(nst, 128)
            s0 = st_a[block, :, at] + reach * s_in
            ds0 = dst_a[block, :, at] + reach * (ds_in + log_a[block, 1:2, at] * s_in)
            s0_o[0, :, at] = s0
            s_h, s_l = split(s0)
            ds_h, ds_l = split(ds0)
            big = (
                nn(c_h, jnp.concatenate([s_h, ds_h], axis=1))
                + nn(c_h, jnp.concatenate([s_l, ds_l], axis=1))
                + nn(c_l, jnp.concatenate([s_h, ds_h], axis=1))
            )
            low = nn(dc_h, s_h) + nn(dc_h, s_l) + nn(dc_l, s_h)
            lift = jnp.exp(expand(cols, C_, p))
            add = lift * big[:, :128]
            y = y_a[block, :, at] + add
            dy = (
                dy_a[block, :, at]
                + lift * (big[:, 128:] + low)
                + expand(cols, DC_, p) * add
            )
            gz = gate_z[:, at].astype(F32)
            gate = gz * jax.nn.sigmoid(gz)
            gated = y * gate
            dgated = dy * gate
            gated_o[:, at] = gated
            dgated_o[:, at] = dgated
            squares = squares + gated * gated
            crossed = crossed + 2.0 * gated * dgated
        sums_o[0:1, :] = jnp.sum(squares.T, axis=0, keepdims=True)
        sums_o[1:2, :] = jnp.sum(crossed.T, axis=0, keepdims=True)


def forward_call(pre_x, pre_bc, dt, gate_z, cx, tcx, cbc, tcbc, hp, th, tw, parts):
    length, width = pre_x.shape
    wide = pre_bc.shape[1]
    nst = wide // 2
    heads = dt.shape[0]
    count = length // QB
    first = lambda i: jnp.minimum(i, count - 1)
    last = lambda i: jnp.maximum(i - 2 * count, 0)
    whole = lambda a: pl.BlockSpec(a.shape, lambda i: (0,) * a.ndim)
    fixed = lambda *s: pl.BlockSpec(s, lambda i: (0,) * len(s))
    rows = lambda w, f: pl.BlockSpec((QB, w), lambda i: (f(i), 0))
    cube = lambda r, f: pl.BlockSpec((1, r, width), lambda i: (f(i), 0, 0))
    tail = lambda w: pl.BlockSpec((16, w), lambda i: (length // 16 - 1, 0))
    lanes = lambda r, f: pl.BlockSpec((r, QB), lambda i: (0, f(i)))
    out = lambda *s: jax.ShapeDtypeStruct(s, F32)
    vmem = lambda *s: pltpu.VMEM(s, F32)
    dma = pltpu.SemaphoreType.DMA
    return pl.pallas_call(
        forward_kernel,
        grid=(3 * count,),
        in_specs=[
            rows(width, first), tail(width), rows(wide, first), tail(wide), lanes(heads, first),
            rows(width, last), whole(cx), whole(tcx), whole(cbc), whole(tcbc), whole(hp),
            whole(th), pl.BlockSpec(memory_space=pl.ANY),
        ],
        out_specs=[
            rows(width, first), rows(width, first), rows(wide, first), rows(wide, first),
            lanes(128, first), rows(128, first), cube(8, first), cube(nst, last),
            rows(width, last), rows(width, last), lanes(2, last), fixed(parts, width),
            fixed(8, width), fixed(8, wide), pl.BlockSpec(memory_space=pl.ANY),
        ],
        out_shape=[
            out(length, width), out(length, width), out(length, wide), out(length, wide),
            out(128, length), out(length, 128), out(count, 8, width), out(count, nst, width),
            out(length, width), out(length, width), out(2, length), out(parts, width),
            out(8, width), out(8, wide),
            jax.ShapeDtypeStruct((4, 4, *tw.shape), BF16),
        ],
        scratch_shapes=[
            vmem(QB + 8, width), vmem(QB + 8, wide), vmem(128, QB), vmem(nst, width),
            vmem(nst, width), vmem(8, width), vmem(count, QB, width), vmem(count, QB, width),
            vmem(count, QB, wide), vmem(count, QB, wide), vmem(count, 128, QB),
            vmem(count, QB, 128), vmem(count, nst, width), vmem(count, nst, width),
            vmem(count, 8, width), vmem(count, QB, width), vmem(count, QB, width),
            vmem(8, 128), pltpu.VMEM((16, width), BF16), pltpu.VMEM((16, wide), BF16),
            vmem(parts, 16, width), vmem(parts, 16, width), vmem(parts, 8, 128),
            vmem(parts, 16, width), vmem(parts, 16, width),
            dma((2,)), dma((2,)), dma((parts,)), dma((parts,)), dma((parts,)), dma((parts,)),
            dma((parts,)), dma((parts,)), dma((1,)), dma((4,)), dma((4,)), dma((4,)), dma((4,)),
            dma((4,)), dma((4,)), dma((4,)), dma((4,)),
        ],
        compiler_params=pltpu.CompilerParams(
            collective_id=1, has_side_effects=True, vmem_limit_bytes=LIMIT
        ),
        name="forward",
    )(pre_x, pre_x, pre_bc, pre_bc, dt, gate_z, cx, tcx, cbc, tcbc, hp, th, tw)


def middle_kernel(
    gated, dgated, sums, gate_in, w_in, tw_in, gain_in, tgain_in,
    by_o, gain_o, sum_z_o, sum_y_o, late_o,
    got, scal, both, part, sib, far_src, far_dst, out_src, out_dst, probe, back, gnw, got_z, got_y,
    mix, mix_got, gains, gate_z, w, tw, fetch_m,
    sums_s, sums_r, sib_s, sib_r, far_s, far_r, out_s, out_r, ag_s, ag_r, mix_s, mix_r,
    az_s, az_r, ay_s, ay_r,
):
    length, width = gated.shape
    blocks, _, blk = probe.shape
    fetches = [
        pltpu.make_async_copy(src, dst, fetch_m.at[i])
        for i, (src, dst) in enumerate(((w_in, w), (tw_in, tw), (gate_in, gate_z)))
    ]
    for copy in fetches:
        copy.start()
    groups = width // 128
    channels = width * 8.0
    head = lax.axis_index("head")
    me = lax.axis_index("seq")
    my_y, my_z = me // 4, lax.rem(me, 4)
    mine = head // 2
    core = lax.rem(head, 2)
    right, left, far = (lax.rem(mine + k, 4) for k in (1, 3, 2))
    device = lambda chip, c: {"head": chip * 2 + c}
    to_right, to_left, to_sib = device(right, core), device(left, core), device(mine, 1 - core)
    y_peers = [{"seq": lax.rem(my_y + k, 4) * 4 + my_z} for k in range(1, 4)]
    z_peers = [{"seq": my_y * 4 + lax.rem(my_z + k, 4)} for k in range(1, 4)]
    peers = others("head", 8)
    greet([{"head": to} for to in peers] + y_peers + z_peers)
    copies = []
    for k, to in enumerate(peers):
        copies.append(send(sums, got.at[head], sums_s.at[k], sums_r.at[k], {"head": to}))
    got[head] = sums[...]
    gain_o[...] = jnp.zeros_like(gain_o)
    gains[0:1] = gain_in[...].reshape(1, width)
    gains[1:2] = tgain_in[...].reshape(1, width)
    gain, tgain = gains.at[0:1], gains.at[1:2]
    for copy in copies:
        copy.wait()
    total = got[0]
    for i in range(1, 8):
        total = total + got[i]
    inv = lax.rsqrt(total[0:1] / channels + 1e-05)
    scal[0:1] = inv
    scal[1:2] = -0.5 * inv * inv * inv * total[1:2] / channels

    def column(row, start):
        at = pl.ds(pl.multiple_of(start, 128), 128)
        return jnp.broadcast_to(scal[row : row + 1, at], (128, 128)).T

    def norm(i, carry):
        start = pl.multiple_of(i * 128, 128)
        rows = pl.ds(start, 128)
        inv_c, d_inv_c = column(0, start), column(1, start)
        for g in range(groups):
            at = slice(128 * g, 128 * g + 128)
            gt, dgt = gated[rows, at], dgated[rows, at]
            ga = gain[:, at]
            scaled = gt * inv_c
            normed = scaled * ga
            d_normed = (dgt * inv_c + gt * d_inv_c) * ga + scaled * tgain[:, at]
            both[rows, at] = d_normed.astype(BF16)
            both[rows, width + 128 * g : width + 128 * g + 128] = normed.astype(BF16)
        return carry

    lax.fori_loop(0, length // 128, norm, 0)

    def columns(i):
        return pl.ds(pl.multiple_of(lax.rem(my_y + TURN[i], 4) * blk, 128), blk)

    def compute(i):
        slot, at = i % 2, columns(i)

        res = nn(both[:, 0:width], w[:, at]) + nt(both[:, width:], tw[at, :])
        part[slot] = res.reshape(4, 2, 128, blk)
        return send(part.at[slot, :, 1 - core], sib.at[i], sib_s.at[i], sib_r.at[i], to_sib)

    def pairs(i, copy):
        copy.wait()
        for chip in range(4):
            sib[i, chip] = sib[i, chip] + part[i % 2, chip, core]
        way, near = (to_right, to_left) if i % 2 == 0 else (to_left, to_right)
        near_chip = left if i % 2 == 0 else right
        far_src[i] = sib[i, far].astype(BF16)
        transit = send(far_src.at[i], far_dst.at[i], far_s.at[i], far_r.at[i], way)
        out_src[i, 0] = sib[i, near_chip].astype(BF16)
        direct = send(out_src.at[i, 0], out_dst.at[i, 0], out_s.at[i, 0], out_r.at[i, 0], near)
        return transit, direct

    def through(i, transit):
        transit.wait()
        way, chip = (to_right, right) if i % 2 == 0 else (to_left, left)
        out_src[i, 1] = (sib[i, chip] + far_dst[i].astype(F32)).astype(BF16)
        return send(out_src.at[i, 1], out_dst.at[i, 1], out_s.at[i, 1], out_r.at[i, 1], way)

    def pass_on(i, slot, chip, to):
        ref = probe.at[i, pl.ds(pl.multiple_of(chip * 256 + core * 128, 128), 128), :]
        return send(ref, ref, ag_s.at[i, slot], ag_r.at[i, slot], to)

    def own(i, direct, joined):
        direct.wait()
        joined.wait()
        rows = pl.ds(pl.multiple_of(mine * 256 + core * 128, 128), 128)
        res = sib[i, mine] + out_dst[i, 0].astype(F32) + out_dst[i, 1].astype(F32)
        probe[i, rows, :] = res.astype(BF16)
        go_right = pass_on(i, 0, mine, to_right)
        go_left = pass_on(i, 1, mine, to_left)
        return go_right, go_left, pass_on(i, 2, mine, to_sib)

    def forward(i, go_right, go_left):
        if i % 2 == 0:
            go_right.wait()
            onward = pass_on(i, 3, left, to_right)
            go_left.wait()
        else:
            go_left.wait()
            onward = pass_on(i, 3, right, to_left)
            go_right.wait()
        return onward, pass_on(i, 4, left, to_sib), pass_on(i, 5, right, to_sib)

    def last_hop(i, onward):
        onward.wait()
        return pass_on(i, 6, far, to_sib)

    def back_block(i, waits):
        for copy in waits:
            copy.wait()
        at = columns(i)
        summed = lax.dot_general(
            probe[i], both[:, width:], (((0,), (0,)), ((), ())), preferred_element_type=F32
        ).reshape(4, blk // 4, width)
        half = blk // 8
        sent = []
        if i < 2:
            gnw[i] = summed
        else:
            late_o[i - 2] = summed
        for k in (2, 1, 3) if i < 2 else ():
            z = lax.rem(my_z + k, 4)
            sent.append(
                send(
                    gnw.at[i, z, 0:half, :], got_z.at[i, k - 1],
                    az_s.at[i, k], az_r.at[i, k], z_peers[k - 1],
                )
            )
        if i < 2:
            sent.append(
                send(
                    gnw.at[i, :, half : 2 * half, :], got_y.at[i],
                    ay_s.at[i], ay_r.at[i], y_peers[TURN[i] - 1],
                )
            )

        res = nt(probe[i], w[:, at])
        back[...] = res if i == 0 else back[...] + res
        return sent

    fetches[0].wait()
    fetches[1].wait()
    sib0 = compute(0)
    sib1 = compute(1)
    far0, dir0 = pairs(0, sib0)
    sib2 = compute(2)
    far1, dir1 = pairs(1, sib1)
    join0 = through(0, far0)
    far2, dir2 = pairs(2, sib2)
    join1 = through(1, far1)
    sib3 = compute(3)
    ag0 = own(0, dir0, join0)
    ag1 = own(1, dir1, join1)
    fwd0 = forward(0, ag0[0], ag0[1])
    join2 = through(2, far2)
    far3, dir3 = pairs(3, sib3)
    fwd1 = forward(1, ag1[0], ag1[1])
    end0 = last_hop(0, fwd0[0])
    join3 = through(3, far3)
    sent = back_block(0, [ag0[2], fwd0[1], fwd0[2], end0])
    end1 = last_hop(1, fwd1[0])
    ag2 = own(2, dir2, join2)
    ag3 = own(3, dir3, join3)
    fwd2 = forward(2, ag2[0], ag2[1])
    sent = sent + back_block(1, [ag1[2], fwd1[1], fwd1[2], end1])
    fwd3 = forward(3, ag3[0], ag3[1])
    end2 = last_hop(2, fwd2[0])
    end3 = last_hop(3, fwd3[0])
    sent = sent + back_block(2, [ag2[2], fwd2[1], fwd2[2], end2])
    sent = sent + back_block(3, [ag3[2], fwd3[1], fwd3[2], end3])

    def mixing(i, carry):
        start = pl.multiple_of(i * 128, 128)
        rows = pl.ds(start, 128)
        inv_c = column(0, start)
        mixed = jnp.zeros((128, 128), F32)
        for g in range(groups):
            at = slice(128 * g, 128 * g + 128)
            prod = back[rows, at] * gated[rows, at]
            gain_o[:, at] = gain_o[:, at] + fold(prod * inv_c)
            mixed = mixed + prod * gain[:, at]
        mix[pl.ds(i, 1), :] = jnp.sum(mixed.T, axis=0, keepdims=True)
        return carry

    lax.fori_loop(0, length // 128, mixing, 0)
    copies = []
    for k, to in enumerate(peers):
        copies.append(send(mix, mix_got.at[head], mix_s.at[k], mix_r.at[k], {"head": to}))
    mix_got[head] = mix[...]
    for copy in copies:
        copy.wait()
    total = mix_got[0]
    for i in range(1, 8):
        total = total + mix_got[i]
    mix[...] = total / channels

    def finish(i, carry):
        start = pl.multiple_of(i * 128, 128)
        rows = pl.ds(start, 128)
        inv_c = column(0, start)
        mixed_c = jnp.broadcast_to(mix[pl.ds(i, 1), :], (128, 128)).T * (inv_c * inv_c * inv_c)
        for g in range(groups):
            at = slice(128 * g, 128 * g + 128)
            gz = gate_z[rows, at].astype(F32)
            gate = gz * jax.nn.sigmoid(gz)
            by_o[rows, at] = (
                back[rows, at] * gain[:, at] * inv_c - gated[rows, at] * mixed_c
            ) * gate
        return carry

    fetches[2].wait()
    lax.fori_loop(0, length // 128, finish, 0)
    for copy in sent:
        copy.wait()
    half = blk // 8
    for i in range(2):
        sum_z_o[i] = gnw[i, my_z, 0:half, :] + got_z[i, 0] + got_z[i, 1] + got_z[i, 2]
    sum_y_o[...] = late_o[1, :, half : 2 * half, :] + got_y[0] + got_y[1]


def middle_call(gated, dgated, sums, gate_z, w, tw, gain, tgain):
    length, width = gated.shape
    cols = w.shape[1]
    blk = cols // 4
    half = blk // 8
    out = lambda *s: jax.ShapeDtypeStruct(s, F32)
    dma = pltpu.SemaphoreType.DMA
    return pl.pallas_call(
        middle_kernel,
        in_specs=[VMEM] * 3 + [pl.BlockSpec(memory_space=pl.ANY)] * 3 + [VMEM] * 2,
        out_specs=[VMEM] * 5,
        out_shape=[
            out(length, width), out(8, width), out(2, half, width), out(4, half, width),
            out(2, 4, blk // 4, width),
        ],
        scratch_shapes=[
            pltpu.VMEM((8, 2, length), F32),
            pltpu.VMEM((8, length), F32),
            pltpu.VMEM((length, 2 * width), BF16),
            pltpu.VMEM((2, 4, 2, 128, blk), F32),
            pltpu.VMEM((4, 4, 128, blk), F32),
            pltpu.VMEM((4, 128, blk), BF16),
            pltpu.VMEM((4, 128, blk), BF16),
            pltpu.VMEM((4, 2, 128, blk), BF16),
            pltpu.VMEM((4, 2, 128, blk), BF16),
            pltpu.VMEM((4, length, blk), BF16),
            pltpu.VMEM((length, width), F32),
            pltpu.VMEM((2, 4, blk // 4, width), F32),
            pltpu.VMEM((2, 3, half, width), F32),
            pltpu.VMEM((2, 4, half, width), F32),
            pltpu.VMEM((8, 128), F32),
            pltpu.VMEM((8, 8, 128), F32),
            pltpu.VMEM((8, width), F32),
            pltpu.VMEM(gate_z.shape, BF16), pltpu.VMEM(w.shape, BF16), pltpu.VMEM(tw.shape, BF16),
            dma((3,)),
            dma((8,)), dma((8,)), dma((4,)), dma((4,)), dma((4,)), dma((4,)),
            dma((4, 2)), dma((4, 2)), dma((4, 7)), dma((4, 7)), dma((8,)), dma((8,)),
            dma((2, 4)), dma((2, 4)), dma((2,)), dma((2,)),
        ],
        compiler_params=pltpu.CompilerParams(
            collective_id=3, has_side_effects=True, vmem_limit_bytes=61 * 1024 * 1024
        ),
        name="probe_and_back",
    )(gated, dgated, sums, gate_z, w, tw, gain, tgain)


def fold(a):
    return jnp.sum(a.reshape(a.shape[0] // 8, 8, a.shape[1]), axis=0)


def adjoint_kernel(
    by, x, gx, pre_x, halo_x, bc, gbc, pre_bc, halo_bc, rowv, colv, s0_b, log, last_log,
    gain, decays, hp, sum_z, sum_y, late,
    result_o,
    wx, wbc, head_o, pack_o, lam, back_u_a, back_bc_a, state, msg, landed, answer, s_end,
    own_z, own_y, got_z, got_y, end_z, end_y, pack_z, landed_z, landed_y, part, landed_q,
    az_s, az_r, ay_s, ay_r, bz_s, bz_r, by_s, by_r,
    s1_s, s1_r, s2_s, s2_r, f1_s, f1_r, f3_s, f3_r, f2_s, f2_r,
):
    step = pl.program_id(0)
    half = lam.shape[0]
    nst = bc.shape[1] // 2
    width = by.shape[1]
    heads = width // HW
    count, n_head = landed.shape[0], landed_q.shape[0]
    me, head = lax.axis_index("seq"), lax.axis_index("head")
    my_y, my_z = me // 4, lax.rem(me, 4)
    seq_peers, head_peers = others("seq", count), others("head", n_head)
    rows_half = sum_z.shape[1]
    mask = lane_mask()

    y_peers = [{"seq": lax.rem(my_y + k, 4) * 4 + my_z} for k in range(1, 4)]
    z_peers = [{"seq": my_y * 4 + lax.rem(my_z + k, 4)} for k in range(1, 4)]

    def late_copies(part_at):
        copies = []
        for i, k in ((0, 1), (0, 3)) if part_at % 2 == 0 else ((0, 2),):
            i = i + part_at // 2
            copies.append(
                link(
                    late.at[i, lax.rem(my_z + k, 4), 0:rows_half, :], got_z.at[i, k - 1],
                    az_s.at[i, k], az_r.at[i, k], z_peers[k - 1],
                )
            )
        copies.append(
            link(
                late.at[0, part_at, rows_half : 2 * rows_half, :], got_y.at[part_at],
                ay_s.at[part_at], ay_r.at[part_at], y_peers[TURN[2] - 1],
            )
        )
        return copies

    def early_last():
        return [
            link(sum_z.at[i], end_z.at[i], bz_s.at[i], bz_r.at[i], y_peers[TURN[i] - 1])
            for i in range(2)
        ]

    def last_copies():
        copies = [link(own_z, end_z.at[2], bz_s.at[2], bz_r.at[2], y_peers[TURN[2] - 1])]
        for k in (2, 1, 3):
            z = lax.rem(my_z + k, 4)
            copies.append(
                link(own_y.at[z], end_y.at[k - 1], by_s.at[k], by_r.at[k], z_peers[k - 1])
            )
        return copies

    for part_at, when in enumerate((0, 3, half + SCAN_AT + 1, half + SCAN_AT + 2)):

        @pl.when(step == when)
        def _(part_at=part_at):
            if part_at == 0:
                greet([{"seq": to} for to in seq_peers] + [{"head": to} for to in head_peers])
            for copy in late_copies(part_at) + (early_last() if part_at == 3 else []):
                copy.start()

    @pl.when(step == 0)
    def _():
        state[...] = jnp.zeros_like(state)
        head_o[...] = jnp.zeros_like(head_o)
        pack_o[...] = jnp.zeros_like(pack_o)
        pack_o[8:9, :] = jnp.sum(gain[...], axis=0, keepdims=True)

    @pl.when(step < half)
    def _():
        lam[half - 1 - step] = state[...]
        cols = colv[...]
        ct_h, ct_l = split(bc[:, nst:].T)
        for p in range(heads // 2):
            at = slice(128 * p, 128 * p + 128)
            lifted = jnp.exp(expand(cols, C_, p)) * by[:, at]
            l_h, l_l = split(lifted)
            add = nn(ct_h, l_h) + nn(ct_h, l_l) + nn(ct_l, l_h)
            state[:, at] = jnp.exp(log[0, 2:3, at]) * state[:, at] + add

    def scan_copies():
        return [
            link(msg.at[to], landed.at[me], s1_s.at[k], s1_r.at[k], {"seq": to})
            for k, to in enumerate(seq_peers)
        ]

    def back_copies():
        return [
            link(answer.at[to], s_end.at[me], s2_s.at[k], s2_r.at[k], {"seq": to})
            for k, to in enumerate(seq_peers)
        ]

    @pl.when(step == half - 1)
    def _():
        msg[...] = state[...].reshape(count, 8, width)
        for copy in scan_copies():
            copy.start()

    @pl.when(step == half + SCAN_AT)
    def _():
        landed[me] = msg[me]
        for copy in scan_copies():
            copy.wait()
        adjoint = jnp.zeros((8, width), F32)
        for i in range(count - 1, -1, -1):
            answer[i] = adjoint
            adjoint = decays[i : i + 1, :] * adjoint + landed[i]
        for copy in back_copies():
            copy.start()

    @pl.when((step >= half) & (step < 2 * half))
    def _():
        block = step - half
        b_mat, c_mat = bc[:, :nst], bc[:, nst:]
        at_i = lax.broadcasted_iota(jnp.int32, (QB, QB), 1)
        at_j = lax.broadcasted_iota(jnp.int32, (QB, QB), 0)
        keep = at_i >= at_j
        inner_t = jnp.where(keep, nt3(b_mat, c_mat), 0.0)
        cols = colv[...]
        rows = rowv[...]
        back_inner_t = jnp.zeros((QB, QB), F32)
        for p in range(heads // 2):
            at = slice(128 * p, 128 * p + 128)
            byp = by[:, at]
            u = expand(cols, S_, p) * x[:, at]
            y_h, y_l = split(byp)
            u_h, u_l = split(
                jnp.concatenate([jnp.where(mask, u, 0.0), jnp.where(mask, 0.0, u)], axis=0)
            )
            back_mts = nt(
                jnp.concatenate([u_h, u_l], axis=1), jnp.concatenate([y_h, y_h], axis=1)
            ) + nt(u_h, y_l)
            mats = []
            for s in range(2):
                h = 2 * p + s
                c_row = rows[C_ + h : C_ + h + 1, :]
                cs_row = rows[CS_ + h : CS_ + h + 1, :]
                back_mt = back_mts[s * QB : s * QB + QB]
                diff = jnp.minimum(c_row - bcast(cols, C_ + h), 0.0)
                level = jnp.exp(diff)
                back_inner_t = back_inner_t + level * back_mt
                m_t = inner_t * level
                prod = m_t * back_mt
                head_o[h, 0] = head_o[h, 0] + fold(prod * diff)
                head_o[h, 1] = head_o[h, 1] + fold(prod * (cs_row - bcast(cols, CS_ + h)))
                mats.append(m_t)
            a_h, a_l = split(jnp.concatenate(mats, axis=0))
            back_u2 = nn(
                jnp.concatenate([a_h, a_l], axis=1), jnp.concatenate([y_h, y_h], axis=0)
            ) + nn(a_h, y_l)
            back_u_a[block, :, at] = jnp.where(mask, back_u2[:QB], back_u2[QB:])
        back_inner_t = jnp.where(keep, back_inner_t, 0.0)
        back_bc_a[block, :, 0:nst] = nn3(back_inner_t, c_mat)
        back_bc_a[block, :, nst:] = nn3(back_inner_t.T, b_mat)

    @pl.when(step == 2 * half)
    def _():
        s_end[me] = answer[me]
        for copy in back_copies():
            copy.wait()

    @pl.when(step >= 2 * half)
    def _():
        block = step - 2 * half
        load_window(wx, halo_x, pre_x, step == 2 * half)
        load_window(wbc, halo_bc, pre_bc, step == 2 * half)
        b_h, b_l = split(bc[:, :nst])
        c_h, c_l = split(bc[:, nst:])
        cols = colv[...]
        back_b = back_bc_a[block, :, 0:nst]
        back_c = back_bc_a[block, :, nst:]
        for p in range(heads // 2):
            at = slice(128 * p, 128 * p + 128)
            own, sig_own = log[0, 2:3, at], log[0, 4:5, at]
            reach = jnp.exp(last_log[0, 0:1, at] + last_log[0, 2:3, at] - log[0, 0:1, at] - own)
            s1 = lam[block, :, at] + reach * s_end[:, :, at].reshape(nst, 128)
            s0 = s0_b[0, :, at]
            byp, xp = by[:, at], x[:, at]
            size = expand(cols, S_, p)
            c_cols, cs_cols = expand(cols, C_, p), expand(cols, CS_, p)
            left = own - c_cols
            to_end = jnp.exp(left)
            u = size * xp
            lifted = jnp.exp(c_cols) * byp
            s0_h, s0_l = split(s0)
            s1_h, s1_l = split(s1)
            l_h, l_l = split(lifted)
            e_h, e_l = split(to_end * u)
            back_c = back_c + nt(
                jnp.concatenate([l_h, l_l], axis=1), jnp.concatenate([s0_h, s0_h], axis=1)
            ) + nt(l_h, s0_l)
            back_b = back_b + nt(
                jnp.concatenate([e_h, e_l], axis=1), jnp.concatenate([s1_h, s1_h], axis=1)
            ) + nt(e_h, s1_l)
            through_c = lifted * (nn(c_h, s0_h) + nn(c_h, s0_l) + nn(c_l, s0_h))
            from_end = to_end * (nn(b_h, s1_h) + nn(b_h, s1_l) + nn(b_l, s1_h))
            through_b = u * from_end
            back_u = back_u_a[block, :, at] + from_end
            back_x = back_u * size + expand(hp[2:3, :], 0, p) * byp
            carried = jnp.sum(s1 * s0, axis=0, keepdims=True) * jnp.exp(own)
            total = lambda a: jnp.sum(a, axis=0, keepdims=True)
            pack_o[4:5, at] = pack_o[4:5, at] + total(expand(cols, SG_, p) * (back_u * xp))
            pack_o[5:6, at] = (
                pack_o[5:6, at] + carried * own + total(through_c * c_cols + through_b * left)
            )
            pack_o[6:7, at] = (
                pack_o[6:7, at]
                + carried * sig_own
                + total(through_c * cs_cols + through_b * (sig_own - cs_cols))
            )
            pack_o[7:8, at] = pack_o[7:8, at] + total(byp * xp)
            back_z = back_x * gx[:, at]
            for k in range(4):
                pack_o[k : k + 1, at] = pack_o[k : k + 1, at] + total(
                    back_z * wx[5 + k : 5 + k + QB, at]
                )
        back_zbc = jnp.concatenate([back_b, back_c], axis=1) * gbc[...]
        for k in range(4):
            pack_o[9 + k : 10 + k, 0 : 2 * nst] = pack_o[
                9 + k : 10 + k, 0 : 2 * nst
            ] + jnp.sum(back_zbc * wbc[5 + k : 5 + k + QB, :], axis=0, keepdims=True)

    @pl.when(step == 3 * half - 5)
    def _():
        for part_at in range(4):
            for copy in late_copies(part_at):
                copy.wait()
        own_z[...] = late[0, my_z, 0:rows_half, :] + got_z[0, 0] + got_z[0, 1] + got_z[0, 2]
        own_y[...] = sum_y[...] + got_y[...]
        for copy in last_copies():
            copy.start()

    @pl.when(step == 3 * half - 1)
    def _():
        for p in range(heads // 2):
            at = slice(128 * p, 128 * p + 128)
            for kind in range(2):
                even, odd = head_o[2 * p, kind], head_o[2 * p + 1, kind]
                even = even + pltpu.roll(even, HW, 1)
                odd = odd + pltpu.roll(odd, HW, 1)
                both = jnp.sum(jnp.where(mask, even, odd), axis=0, keepdims=True)
                pack_o[5 + kind : 6 + kind, at] = pack_o[5 + kind : 6 + kind, at] + both
        for slots, group, sems, mine in (
            (landed_z, z_peers, (f1_s, f1_r), pack_o),
            (landed_y, y_peers, (f3_s, f3_r), pack_z),
        ):
            copies = []
            for k, to in enumerate(group):
                copies.append(send(mine, slots.at[k], sems[0].at[k], sems[1].at[k], to))
            for copy in copies:
                copy.wait()
            if slots is landed_z:
                for z in range(4):
                    k = lax.rem(my_z + 3 - z, 4)
                    term = jnp.where(z == my_z, pack_o[...], slots[jnp.minimum(k, 2)])
                    total = term if z == 0 else total + term
                pack_z[...] = total
            else:
                for y in range(4):
                    k = lax.rem(my_y + 3 - y, 4)
                    term = jnp.where(y == my_y, pack_z[...], slots[jnp.minimum(k, 2)])
                    total = term if y == 0 else total + term
        part[...] = total[8:16, 0 : 2 * nst]
        copies = []
        for k, to in enumerate(head_peers):
            copies.append(send(part, landed_q.at[head], f2_s.at[k], f2_r.at[k], {"head": to}))
        landed_q[head] = part[...]
        result_o[2 * rows_half : 2 * rows_half + 16] = total
        at = lax.broadcasted_iota(jnp.int32, (width, 128), 0)
        to = lax.broadcasted_iota(jnp.int32, (width, 128), 1) * HW
        pick = jnp.where((at >= to) & (at < to + HW), 1.0, 0.0).astype(F32)
        sums = jnp.dot(
            total, pick, precision=lax.Precision.HIGHEST, preferred_element_type=F32
        )[:, :heads]
        at = 2 * rows_half + 24
        result_o[at : at + 1, 0:heads] = sums[4:5] - jnp.exp(hp[1:2]) * sums[6:7]
        result_o[at + 1 : at + 2, 0:heads] = sums[5:6]
        result_o[at + 2 : at + 3, 0:heads] = sums[7:8]
        for copy in early_last() + last_copies():
            copy.wait()
        total = late[1, my_z, 0:rows_half, :] + got_z[1, 0] + got_z[1, 1] + got_z[1, 2]
        result_o[0:rows_half] = total + end_z[0] + end_z[1] + end_z[2]
        result_o[rows_half : 2 * rows_half] = own_y[my_z] + end_y[0] + end_y[1] + end_y[2]
        for copy in copies:
            copy.wait()
        total2 = landed_q[0]
        for i in range(1, n_head):
            total2 = total2 + landed_q[i]
        result_o[2 * rows_half + 16 : 2 * rows_half + 24, 0 : 2 * nst] = total2


def adjoint_call(
    by, x, gx, pre_x, halo_x, bc, gbc, pre_bc, halo_bc, rowv, colv, s0, logs, gain, decays,
    hp, sum_z, sum_y, late_sums, count, n_head,
):
    length, width = by.shape
    wide = bc.shape[1]
    nst = wide // 2
    heads = width // HW
    half = length // QB
    rows_half = sum_z.shape[1]
    piece = 2 * rows_half
    every = lambda i: jnp.where(i < half, half - 1 - i, lax.rem(i, half))
    mid = lambda i: jnp.where(i < half, 0, lax.rem(i, half))
    late = lambda i: jnp.maximum(i - 2 * half, 0)
    whole = lambda a: pl.BlockSpec(a.shape, lambda i: (0,) * a.ndim)
    rows = lambda w, f: pl.BlockSpec((QB, w), lambda i: (f(i), 0))
    cube = lambda r, f: pl.BlockSpec((1, r, width), lambda i: (f(i), 0, 0))
    out = lambda *s: jax.ShapeDtypeStruct(s, F32)
    fixed = lambda *s: pl.BlockSpec(s, lambda i: (0,) * len(s))
    dma = pltpu.SemaphoreType.DMA
    return pl.pallas_call(
        adjoint_kernel,
        grid=(3 * half,),
        in_specs=[
            rows(width, every), rows(width, mid), rows(width, late), rows(width, late),
            whole(halo_x), rows(wide, every), rows(wide, late), rows(wide, late), whole(halo_bc),
            pl.BlockSpec((128, QB), lambda i: (0, mid(i))), rows(128, every),
            cube(nst, late), cube(8, every),
            pl.BlockSpec((1, 8, width), lambda i: (half - 1, 0, 0)),
            whole(gain), whole(decays), whole(hp),
            whole(sum_z), whole(sum_y), VMEM,
        ],
        out_specs=fixed(256, width),
        out_shape=out(256, width),
        scratch_shapes=[
            pltpu.VMEM((QB + 8, width), F32), pltpu.VMEM((QB + 8, wide), F32),
            pltpu.VMEM((heads, 2, 8, 128), F32), pltpu.VMEM((16, width), F32),
            pltpu.VMEM((half, nst, width), F32), pltpu.VMEM((half, QB, width), F32),
            pltpu.VMEM((half, QB, wide), F32), pltpu.VMEM((nst, width), F32),
            pltpu.VMEM((count, 8, width), F32), pltpu.VMEM((count, 8, width), F32),
            pltpu.VMEM((count, 8, width), F32), pltpu.VMEM((count, 8, width), F32),
            pltpu.VMEM((rows_half, width), F32), pltpu.VMEM((4, rows_half, width), F32),
            pltpu.VMEM((2, 3, rows_half, width), F32), pltpu.VMEM((4, rows_half, width), F32),
            pltpu.VMEM((3, rows_half, width), F32), pltpu.VMEM((3, rows_half, width), F32),
            pltpu.VMEM((16, width), F32), pltpu.VMEM((3, 16, width), F32),
            pltpu.VMEM((3, 16, width), F32), pltpu.VMEM((8, wide), F32),
            pltpu.VMEM((n_head, 8, wide), F32),
            dma((2, 4)), dma((2, 4)), dma((4,)), dma((4,)),
            dma((4,)), dma((4,)), dma((4,)), dma((4,)),
            dma((count,)), dma((count,)), dma((count,)), dma((count,)),
            dma((3,)), dma((3,)), dma((3,)), dma((3,)), dma((n_head,)), dma((n_head,)),
        ],
        compiler_params=pltpu.CompilerParams(
            collective_id=2, has_side_effects=True, vmem_limit_bytes=LIMIT
        ),
        name="adjoint",
    )(
        by, x, gx, pre_x, halo_x, bc, gbc, pre_bc, halo_bc, rowv, colv, s0, logs, logs,
        gain, decays, hp, sum_z, sum_y, late_sums,
    )


def outputs_kernel(result, gcx_o, gcbc_o, heads_o, gain_o, gnw_o):
    piece, heads, wide = gnw_o.shape[0], heads_o.shape[1], gcbc_o.shape[1]
    width = result.shape[1]
    gcx_o[...] = result[piece : piece + 4]
    gain_o[...] = result[piece + 8 : piece + 9].reshape(width)
    gcbc_o[...] = result[piece + 17 : piece + 21, 0:wide]
    heads_o[...] = result[piece + 24 : piece + 27, 0:heads]
    gnw_o[...] = result[0:piece]


def outputs_call(result, piece, bc_shape, heads_shape):
    width = result.shape[1]
    out = lambda *s: jax.ShapeDtypeStruct(s, F32)
    return pl.pallas_call(
        outputs_kernel,
        in_specs=[VMEM],
        out_specs=[VMEM] * 5,
        out_shape=[
            out(4, width), out(*bc_shape), out(*heads_shape), out(width), out(piece, width),
        ],
        name="outputs",
    )(result)


def on_device(
    pre_x, pre_bc, gate_z, dt_raw, conv_x, conv_bc, head_params, norm_gain, w_out,
    t_conv_x, t_conv_bc, t_heads, t_gain, t_wout,
):
    count = lax.axis_size("seq")
    x, gx, bc, gbc, rowv, colv, logs, s0, gated, d_gated, sums, decays, halo_x, halo_bc, tw = forward_call(
        pre_x, pre_bc, dt_raw, gate_z, conv_x, t_conv_x, conv_bc, t_conv_bc, head_params, t_heads,
        t_wout.T, count,
    )
    back_y, gain_part, sum_z, sum_y, late_sums = middle_call(
        gated, d_gated, sums, gate_z, w_out, tw.reshape(-1, w_out.shape[0]), norm_gain, t_gain
    )
    result = adjoint_call(
        back_y, x, gx, pre_x, halo_x, bc, gbc, pre_bc, halo_bc, rowv, colv, s0, logs,
        gain_part, decays, head_params, sum_z, sum_y, late_sums, count, lax.axis_size("head"),
    )
    gn_conv_x, gn_conv_bc, gn_heads, gn_gain, gn_wout = outputs_call(
        result, t_wout.shape[1], conv_bc.shape, head_params.shape
    )
    return gn_conv_x, gn_conv_bc, gn_heads, gn_gain, gn_wout.T


def solution(mesh):
    in_specs = (
        P("seq", "head"), P("seq", None), P("seq", "head"), P("head", "seq"), P(None, "head"),
        P(), P(None, "head"), P("head"), P("head", None), P(None, "head"), P(), P(None, "head"),
        P("head"), P("head", "seq"),
    )
    out_specs = (P(None, "head"), P(), P(None, "head"), P("head"), P("head", "seq"))
    return jax.shard_map(
        on_device, mesh=mesh, in_specs=in_specs, out_specs=out_specs, check_vma=False
    )
```

```python
import jax
import jax.numpy as jnp
from jax import lax
from jax.experimental import pallas as pl
from jax.experimental.pallas import tpu as pltpu
from jax.sharding import PartitionSpec as P

QB = 128
HW = 64
F32 = jnp.float32
BF16 = jnp.bfloat16
MESH = pl.DeviceIdType.MESH
S_, DS_, C_, DC_, CS_, SG_, K_, DK_ = (16 * i for i in range(8))
LIMIT = 56 * 1024 * 1024
SCAN_AT = 4
TURN = (1, 3, 2, 4)


def split(a):
    high = a.astype(BF16)
    return high, (a - high.astype(F32)).astype(BF16)


def nn(a, b):
    return jnp.dot(a, b, preferred_element_type=F32)


def nt(a, b):
    return lax.dot_general(a, b, (((1,), (1,)), ((), ())), preferred_element_type=F32)


def nn3(a, b):
    (ah, al), (bh, bl) = split(a), split(b)
    return nn(ah, bh) + nn(ah, bl) + nn(al, bh)


def nt3(a, b):
    (ah, al), (bh, bl) = split(a), split(b)
    return nt(ah, bh) + nt(ah, bl) + nt(al, bh)


def lane_mask():
    return lax.broadcasted_iota(jnp.int32, (1, 128), 1) < HW


def bcast(cols, at):
    return jnp.broadcast_to(cols[:, at : at + 1], (cols.shape[0], 128))


def expand(cols, base, pair):
    return jnp.where(
        lane_mask(), bcast(cols, base + 2 * pair), bcast(cols, base + 2 * pair + 1)
    )


def expand_all(cols, base, heads):
    return jnp.concatenate([expand(cols, base, p) for p in range(heads // 2)], axis=1)


def load_window(window, halo, block, first):
    @pl.when(first)
    def _():
        window[0:8] = halo[...]

    @pl.when(jnp.logical_not(first))
    def _():
        window[0:8] = window[QB : QB + 8]

    window[8 : QB + 8] = block[...].astype(F32)


def conv_pair(window, weight, t_weight):
    z = jnp.zeros((QB, window.shape[1]), F32)
    dz = jnp.zeros((QB, window.shape[1]), F32)
    for k in range(4):
        rows = window[5 + k : 5 + k + QB, :]
        z = z + weight[k : k + 1, :] * rows
        dz = dz + t_weight[k : k + 1, :] * rows
    sig = jax.nn.sigmoid(z)
    slope = sig * (1.0 + z * (1.0 - sig))
    return z * sig, slope * dz, slope


def greet(peers):
    barrier = pltpu.get_barrier_semaphore()
    for peer in peers:
        pl.semaphore_signal(barrier, inc=1, device_id=peer, device_id_type=MESH)
    pl.semaphore_wait(barrier, len(peers))


def others(axis, count):
    me = lax.axis_index(axis)
    return [lax.rem(me + k, count) for k in range(1, count)]


def link(src, dst, send_sem, recv_sem, device):
    return pltpu.make_async_remote_copy(
        src_ref=src, dst_ref=dst, send_sem=send_sem, recv_sem=recv_sem,
        device_id=device, device_id_type=MESH,
    )


def send(*what):
    copy = link(*what)
    copy.start()
    return copy


VMEM = pl.BlockSpec(memory_space=pltpu.VMEM)


def column_of(row):
    heads = row.shape[1]
    at_i = lax.broadcasted_iota(jnp.int32, (heads, heads), 0)
    at_j = lax.broadcasted_iota(jnp.int32, (heads, heads), 1)
    return jnp.sum(jnp.where(at_i == at_j, row, 0.0), axis=1, keepdims=True)


def forward_kernel(
    pre_x, tail_x, pre_bc, tail_bc, dt, gate_z, cx, tcx, cbc, tcbc, hp, th, tw_in,
    x_o, gx_o, bc_o, gbc_o, row_o, col_o, log_o, s0_o, gated_o, dgated_o, sums_o, decay_o,
    halo_x_o, halo_bc_o, tw_o,
    wx, wbc, feat, state, d_state, logs, x_a, dx_a, bc_a, dbc_a, row_a, col_a, st_a, dst_a,
    log_a, y_a, dy_a, tile, got_x, got_bc, msg, landed, tiles, answer, start,
    halo_s, halo_r, tile_s, tile_r, s1_s, s1_r, s2_s, s2_r,
    own_m, gz_s, gz_r, gy_s, gy_r, hz_s, hz_r, hy_s, hy_r,
):
    step = pl.program_id(0)
    blocks = st_a.shape[0]
    heads = dt.shape[0]
    width = pre_x.shape[1]
    nst = cbc.shape[1] // 2
    count = landed.shape[0]
    me = lax.axis_index("seq")
    peers = others("seq", count)
    mask = lane_mask()

    my_y, my_z = me // 4, lax.rem(me, 4)
    y_peers = [{"seq": lax.rem(my_y + k, 4) * 4 + my_z} for k in range(1, 4)]
    z_peers = [{"seq": my_y * 4 + lax.rem(my_z + k, 4)} for k in range(1, 4)]
    piece = tw_in.shape[0]
    upper_rows, lower_rows = slice(0, piece // 2), slice(piece // 2, piece)

    def own_copy():
        return pltpu.make_async_copy(tw_in, tw_o.at[my_y, my_z], own_m.at[0])

    def gather_first():
        copies = []
        for k in (2, 1, 3):
            copies.append(
                link(
                    tw_in.at[upper_rows, :], tw_o.at[my_y, my_z, upper_rows, :],
                    gz_s.at[k], gz_r.at[k], z_peers[k - 1],
                )
            )
            copies.append(
                link(
                    tw_in.at[lower_rows, :], tw_o.at[my_y, my_z, lower_rows, :],
                    gy_s.at[k], gy_r.at[k], y_peers[k - 1],
                )
            )
        return copies

    def gather_second(k):
        along_y = tw_o.at[my_y, :, upper_rows, :]
        along_z = tw_o.at[:, my_z, lower_rows, :]
        return [
            link(along_y, along_y, hz_s.at[k], hz_r.at[k], y_peers[k - 1]),
            link(along_z, along_z, hy_s.at[k], hy_r.at[k], z_peers[k - 1]),
        ]

    def scan_copies():
        copies = []
        for k, to in enumerate(peers):
            at = {"seq": to}
            copies.append(link(msg.at[to], landed.at[me], s1_s.at[k], s1_r.at[k], at))
        for k, to in enumerate(peers):
            copies.append(link(tile, tiles.at[me], tile_s.at[k], tile_r.at[k], {"seq": to}))
        return copies

    def back_copies():
        return [
            link(answer.at[to], start.at[me], s2_s.at[k], s2_r.at[k], {"seq": to})
            for k, to in enumerate(peers)
        ]

    @pl.when(step == 0)
    def _():
        greet([{"seq": to} for to in peers])
        after = {"seq": lax.rem(me + 1, count)}
        tails = [
            send(tail_x, got_x, halo_s.at[0], halo_r.at[0], after),
            send(tail_bc, got_bc, halo_s.at[1], halo_r.at[1], after),
        ]
        state[...] = jnp.zeros_like(state)
        d_state[...] = jnp.zeros_like(d_state)
        logs[...] = jnp.zeros_like(logs)
        feat[...] = jnp.zeros_like(feat)
        tile[...] = jnp.zeros_like(tile)
        for copy in tails:
            copy.wait()
        halo_x_o[...] = jnp.where(me == 0, 0.0, got_x[...].astype(F32)[8:16])
        halo_bc_o[...] = jnp.where(me == 0, 0.0, got_bc[...].astype(F32)[8:16])
        own_copy().start()
        for copy in gather_first():
            copy.start()

    @pl.when(step == 3)
    def _():
        own_copy().wait()
        for copy in gather_first():
            copy.wait()
        for copy in gather_second(1) + gather_second(3):
            copy.start()

    @pl.when(step == blocks + SCAN_AT + 1)
    def _():
        for copy in gather_second(2):
            copy.start()

    @pl.when(step == 3 * blocks - 1)
    def _():
        for k in (1, 3, 2):
            for copy in gather_second(k):
                copy.wait()

    @pl.when(step < blocks)
    def _():
        load_window(wx, halo_x_o, pre_x, step == 0)
        load_window(wbc, halo_bc_o, pre_bc, step == 0)
        z = dt[...] + column_of(hp[0:1, :])
        rate = jnp.exp(column_of(hp[1:2, :]))
        t_bias, t_lrate = column_of(th[0:1, :]), column_of(th[1:2, :])
        size = jnp.maximum(z, 0.0) + jnp.log1p(jnp.exp(-jnp.abs(z)))
        sig = jax.nn.sigmoid(z)
        log_decay = -size * rate
        at_i = lax.broadcasted_iota(jnp.int32, (QB, QB), 1)
        at_j = lax.broadcasted_iota(jnp.int32, (QB, QB), 0)
        upper = jnp.where(at_j <= at_i, 1.0, 0.0).astype(F32)
        exact = dict(precision=lax.Precision.HIGHEST, preferred_element_type=F32)
        cumul = jnp.dot(log_decay, upper, **exact)
        sig_sum = jnp.dot(sig, upper, **exact)
        d_size = sig * t_bias
        d_cumul = cumul * t_lrate - rate * t_bias * sig_sum
        to_end = jnp.exp(cumul[:, QB - 1 : QB] - cumul)
        feat[S_ : S_ + heads] = size
        feat[DS_ : DS_ + heads] = d_size
        feat[C_ : C_ + heads] = cumul
        feat[DC_ : DC_ + heads] = d_cumul
        feat[CS_ : CS_ + heads] = sig_sum
        feat[SG_ : SG_ + heads] = sig
        feat[K_ : K_ + heads] = to_end * size
        feat[DK_ : DK_ + heads] = to_end * (
            d_size + size * (d_cumul[:, QB - 1 : QB] - d_cumul)
        )
        rows = feat[...]
        cols = rows.T
        row_o[...] = rows
        col_o[...] = cols
        row_a[step] = rows
        col_a[step] = cols

        bc, dbc, gbc = conv_pair(wbc, cbc, tcbc)
        bc_o[...] = bc
        gbc_o[...] = gbc
        bc_a[step] = bc
        dbc_a[step] = dbc
        x, dx, gx = conv_pair(wx, cx, tcx)
        x_o[...] = x
        gx_o[...] = gx
        x_a[step] = x
        dx_a[step] = dx

        last = cols[QB - 1 : QB, :]
        tile[0:1, :] = tile[0:1, :] + last
        own = expand_all(last, C_, heads)
        d_own = expand_all(last, DC_, heads)
        log = jnp.concatenate(
            [logs[0:1, :], logs[1:2, :], own, d_own, expand_all(last, CS_, heads)]
            + [jnp.zeros((3, width), F32)],
            axis=0,
        )
        log_o[0] = log
        log_a[step] = log
        logs[0:1, :] = logs[0:1, :] + own
        logs[1:2, :] = logs[1:2, :] + d_own

        st_a[step] = state[...]
        dst_a[step] = d_state[...]
        bt = bc[:, :nst].T
        dbt = dbc[:, :nst].T
        both_h, both_l = split(jnp.concatenate([bt, dbt], axis=1))
        for p in range(heads // 2):
            at = slice(128 * p, 128 * p + 128)
            k_x, dk_x = expand(cols, K_, p), expand(cols, DK_, p)
            ux = k_x * x[:, at]
            dux = k_x * dx[:, at] + dk_x * x[:, at]
            z_h, z_l = split(jnp.concatenate([dux, ux], axis=0))
            d_add = nn(both_h, z_h) + nn(both_h, z_l) + nn(both_l, z_h)
            b_h, b_l, u_h, u_l = both_h[:, :QB], both_l[:, :QB], z_h[QB:], z_l[QB:]
            add = nn(b_h, u_h) + nn(b_h, u_l) + nn(b_l, u_h)
            decay = jnp.exp(own[:, at])
            before = state[:, at]
            d_state[:, at] = decay * (d_state[:, at] + d_own[:, at] * before) + d_add
            state[:, at] = decay * before + add

    @pl.when(step == blocks - 1)
    def _():
        msg[:, 0:8, :] = state[...].reshape(count, 8, width)
        msg[:, 8:16, :] = d_state[...].reshape(count, 8, width)
        for copy in scan_copies():
            copy.start()

    @pl.when(step == blocks + SCAN_AT)
    def _():
        landed[me] = msg[me]
        tiles[me] = tile[...]
        for copy in scan_copies():
            copy.wait()
        total = jnp.zeros((8, width), F32)
        d_total = jnp.zeros((8, width), F32)
        features = tiles[...][:, 0, :]
        decays = jnp.exp(expand_all(features, C_, heads))
        d_logs = expand_all(features, DC_, heads)
        decay_o[...] = decays
        for i in range(count):
            answer[i, 0:8] = total
            answer[i, 8:16] = d_total
            decay = decays[i : i + 1]
            d_total = decay * (d_total + d_logs[i : i + 1] * total)
            d_total = d_total + landed[i, 8:16]
            total = decay * total + landed[i, 0:8]
        for copy in back_copies():
            copy.start()

    @pl.when((step >= blocks) & (step < 2 * blocks))
    def _():
        block = step - blocks
        bc, dbc = bc_a[block], dbc_a[block]
        b_mat, c_mat = bc[:, :nst], bc[:, nst:]
        db_mat, dc_mat = dbc[:, :nst], dbc[:, nst:]
        at_j = lax.broadcasted_iota(jnp.int32, (QB, QB), 1)
        at_i = lax.broadcasted_iota(jnp.int32, (QB, QB), 0)
        keep = at_i >= at_j
        inner = jnp.where(keep, nt3(c_mat, b_mat), 0.0)
        d_inner = jnp.where(
            keep,
            nt3(
                jnp.concatenate([dc_mat, c_mat], axis=1),
                jnp.concatenate([b_mat, db_mat], axis=1),
            ),
            0.0,
        )
        cols = col_a[block]
        rows = row_a[block]
        for p in range(heads // 2):
            at = slice(128 * p, 128 * p + 128)
            xp, dxp = x_a[block, :, at], dx_a[block, :, at]
            size, d_size = expand(cols, S_, p), expand(cols, DS_, p)
            z_h, z_l = split(size * xp)
            dz_h, dz_l = split(size * dxp + d_size * xp)
            mats, d_mats = [], []
            for h in (2 * p, 2 * p + 1):
                c_row = rows[C_ + h : C_ + h + 1, :]
                dc_row = rows[DC_ + h : DC_ + h + 1, :]
                level = jnp.exp(jnp.minimum(bcast(cols, C_ + h) - c_row, 0.0))
                m = inner * level
                mats.append(m)
                d_mats.append(d_inner * level + m * (bcast(cols, DC_ + h) - dc_row))
            a_h, a_l = split(jnp.concatenate(mats, axis=0))
            da_h, da_l = split(jnp.concatenate(d_mats, axis=0))
            zz_h = jnp.concatenate([z_h, dz_h], axis=1)
            big = nn(
                jnp.concatenate([a_h, a_l], axis=1), jnp.concatenate([zz_h, zz_h], axis=0)
            ) + nn(a_h, jnp.concatenate([z_l, dz_l], axis=1))
            small = nn(
                jnp.concatenate([da_h, da_l], axis=1), jnp.concatenate([z_h, z_h], axis=0)
            ) + nn(da_h, z_l)
            y2 = big[:, :128]
            dy2 = big[:, 128:] + small
            skip, d_skip = expand(hp[2:3, :], 0, p), expand(th[2:3, :], 0, p)
            y_a[block, :, at] = jnp.where(mask, y2[:QB], y2[QB:]) + skip * xp
            dy_a[block, :, at] = (
                jnp.where(mask, dy2[:QB], dy2[QB:]) + skip * dxp + d_skip * xp
            )

    @pl.when(step == 2 * blocks)
    def _():
        start[me] = answer[me]
        for copy in back_copies():
            copy.wait()

    @pl.when(step >= 2 * blocks)
    def _():
        block = step - 2 * blocks
        cols = col_a[block]
        c_h, c_l = split(bc_a[block][:, nst:])
        dc_h, dc_l = split(dbc_a[block][:, nst:])
        squares = jnp.zeros((QB, 128), F32)
        crossed = jnp.zeros((QB, 128), F32)
        for p in range(heads // 2):
            at = slice(128 * p, 128 * p + 128)
            reach = jnp.exp(log_a[block, 0:1, at])
            s_in = start[:, 0:8, at].reshape(nst, 128)
            ds_in = start[:, 8:16, at].reshape(nst, 128)
            s0 = st_a[block, :, at] + reach * s_in
            ds0 = dst_a[block, :, at] + reach * (ds_in + log_a[block, 1:2, at] * s_in)
            s0_o[0, :, at] = s0
            s_h, s_l = split(s0)
            ds_h, ds_l = split(ds0)
            big = (
                nn(c_h, jnp.concatenate([s_h, ds_h], axis=1))
                + nn(c_h, jnp.concatenate([s_l, ds_l], axis=1))
                + nn(c_l, jnp.concatenate([s_h, ds_h], axis=1))
            )
            low = nn(dc_h, s_h) + nn(dc_h, s_l) + nn(dc_l, s_h)
            lift = jnp.exp(expand(cols, C_, p))
            add = lift * big[:, :128]
            y = y_a[block, :, at] + add
            dy = (
                dy_a[block, :, at]
                + lift * (big[:, 128:] + low)
                + expand(cols, DC_, p) * add
            )
            gz = gate_z[:, at].astype(F32)
            gate = gz * jax.nn.sigmoid(gz)
            gated = y * gate
            dgated = dy * gate
            gated_o[:, at] = gated
            dgated_o[:, at] = dgated
            squares = squares + gated * gated
            crossed = crossed + 2.0 * gated * dgated
        sums_o[0:1, :] = jnp.sum(squares.T, axis=0, keepdims=True)
        sums_o[1:2, :] = jnp.sum(crossed.T, axis=0, keepdims=True)


def forward_call(pre_x, pre_bc, dt, gate_z, cx, tcx, cbc, tcbc, hp, th, tw, parts):
    length, width = pre_x.shape
    wide = pre_bc.shape[1]
    nst = wide // 2
    heads = dt.shape[0]
    count = length // QB
    first = lambda i: jnp.minimum(i, count - 1)
    last = lambda i: jnp.maximum(i - 2 * count, 0)
    whole = lambda a: pl.BlockSpec(a.shape, lambda i: (0,) * a.ndim)
    fixed = lambda *s: pl.BlockSpec(s, lambda i: (0,) * len(s))
    rows = lambda w, f: pl.BlockSpec((QB, w), lambda i: (f(i), 0))
    cube = lambda r, f: pl.BlockSpec((1, r, width), lambda i: (f(i), 0, 0))
    tail = lambda w: pl.BlockSpec((16, w), lambda i: (length // 16 - 1, 0))
    lanes = lambda r, f: pl.BlockSpec((r, QB), lambda i: (0, f(i)))
    out = lambda *s: jax.ShapeDtypeStruct(s, F32)
    vmem = lambda *s: pltpu.VMEM(s, F32)
    dma = pltpu.SemaphoreType.DMA
    return pl.pallas_call(
        forward_kernel,
        grid=(3 * count,),
        in_specs=[
            rows(width, first), tail(width), rows(wide, first), tail(wide), lanes(heads, first),
            rows(width, last), whole(cx), whole(tcx), whole(cbc), whole(tcbc), whole(hp),
            whole(th), pl.BlockSpec(memory_space=pl.ANY),
        ],
        out_specs=[
            rows(width, first), rows(width, first), rows(wide, first), rows(wide, first),
            lanes(128, first), rows(128, first), cube(8, first), cube(nst, last),
            rows(width, last), rows(width, last), lanes(2, last), fixed(parts, width),
            fixed(8, width), fixed(8, wide), pl.BlockSpec(memory_space=pl.ANY),
        ],
        out_shape=[
            out(length, width), out(length, width), out(length, wide), out(length, wide),
            out(128, length), out(length, 128), out(count, 8, width), out(count, nst, width),
            out(length, width), out(length, width), out(2, length), out(parts, width),
            out(8, width), out(8, wide),
            jax.ShapeDtypeStruct((4, 4, *tw.shape), BF16),
        ],
        scratch_shapes=[
            vmem(QB + 8, width), vmem(QB + 8, wide), vmem(128, QB), vmem(nst, width),
            vmem(nst, width), vmem(8, width), vmem(count, QB, width), vmem(count, QB, width),
            vmem(count, QB, wide), vmem(count, QB, wide), vmem(count, 128, QB),
            vmem(count, QB, 128), vmem(count, nst, width), vmem(count, nst, width),
            vmem(count, 8, width), vmem(count, QB, width), vmem(count, QB, width),
            vmem(8, 128), pltpu.VMEM((16, width), BF16), pltpu.VMEM((16, wide), BF16),
            vmem(parts, 16, width), vmem(parts, 16, width), vmem(parts, 8, 128),
            vmem(parts, 16, width), vmem(parts, 16, width),
            dma((2,)), dma((2,)), dma((parts,)), dma((parts,)), dma((parts,)), dma((parts,)),
            dma((parts,)), dma((parts,)), dma((1,)), dma((4,)), dma((4,)), dma((4,)), dma((4,)),
            dma((4,)), dma((4,)), dma((4,)), dma((4,)),
        ],
        compiler_params=pltpu.CompilerParams(
            collective_id=1, has_side_effects=True, vmem_limit_bytes=LIMIT
        ),
        name="forward",
    )(pre_x, pre_x, pre_bc, pre_bc, dt, gate_z, cx, tcx, cbc, tcbc, hp, th, tw)


def middle_kernel(
    gated, dgated, sums, gate_in, w_in, tw_in, gain_in, tgain_in,
    by_o, gain_o, sum_z_o, sum_y_o, late_o,
    got, scal, both, part, sib, far_src, far_dst, out_src, out_dst, probe, back, gnw, got_z, got_y,
    mix, mix_got, gains, gate_z, w, tw, fetch_m,
    sums_s, sums_r, sib_s, sib_r, far_s, far_r, out_s, out_r, ag_s, ag_r, mix_s, mix_r,
    az_s, az_r, ay_s, ay_r, one_s, one_r,
):
    length, width = gated.shape
    blocks, _, blk = probe.shape
    fetches = [
        pltpu.make_async_copy(src, dst, fetch_m.at[i])
        for i, (src, dst) in enumerate(((w_in, w), (tw_in, tw), (gate_in, gate_z)))
    ]
    for copy in fetches:
        copy.start()
    groups = width // 128
    channels = width * 8.0
    head = lax.axis_index("head")
    me = lax.axis_index("seq")
    my_y, my_z = me // 4, lax.rem(me, 4)
    mine = head // 2
    core = lax.rem(head, 2)
    right, left, far = (lax.rem(mine + k, 4) for k in (1, 3, 2))
    device = lambda chip, c: {"head": chip * 2 + c}
    to_right, to_left, to_sib = device(right, core), device(left, core), device(mine, 1 - core)
    y_peers = [{"seq": lax.rem(my_y + k, 4) * 4 + my_z} for k in range(1, 4)]
    z_peers = [{"seq": my_y * 4 + lax.rem(my_z + k, 4)} for k in range(1, 4)]
    peers = others("head", 8)
    greet([{"head": to} for to in peers] + y_peers + z_peers)
    copies = []
    for k, to in enumerate(peers):
        copies.append(send(sums, got.at[head], sums_s.at[k], sums_r.at[k], {"head": to}))
    got[head] = sums[...]
    gain_o[...] = jnp.zeros_like(gain_o)
    gains[0:1] = gain_in[...].reshape(1, width)
    gains[1:2] = tgain_in[...].reshape(1, width)
    gain, tgain = gains.at[0:1], gains.at[1:2]
    for copy in copies:
        copy.wait()
    total = got[0]
    for i in range(1, 8):
        total = total + got[i]
    inv = lax.rsqrt(total[0:1] / channels + 1e-05)
    scal[0:1] = inv
    scal[1:2] = -0.5 * inv * inv * inv * total[1:2] / channels

    def column(row, start):
        at = pl.ds(pl.multiple_of(start, 128), 128)
        return jnp.broadcast_to(scal[row : row + 1, at], (128, 128)).T

    def norm(i, carry):
        start = pl.multiple_of(i * 128, 128)
        rows = pl.ds(start, 128)
        inv_c, d_inv_c = column(0, start), column(1, start)
        for g in range(groups):
            at = slice(128 * g, 128 * g + 128)
            gt, dgt = gated[rows, at], dgated[rows, at]
            ga = gain[:, at]
            scaled = gt * inv_c
            normed = scaled * ga
            d_normed = (dgt * inv_c + gt * d_inv_c) * ga + scaled * tgain[:, at]
            both[rows, at] = d_normed.astype(BF16)
            both[rows, width + 128 * g : width + 128 * g + 128] = normed.astype(BF16)
        return carry

    lax.fori_loop(0, length // 128, norm, 0)

    def columns(i):
        return pl.ds(pl.multiple_of(lax.rem(my_y + TURN[i], 4) * blk, 128), blk)

    def compute(i):
        slot, at = i % 2, columns(i)

        res = nn(both[:, 0:width], w[:, at]) + nt(both[:, width:], tw[at, :])
        part[slot] = res.reshape(4, 2, 128, blk)
        return send(part.at[slot, :, 1 - core], sib.at[i], sib_s.at[i], sib_r.at[i], to_sib)

    def compute_first():
        copies = []
        for n, chip in enumerate((far, left, right, mine)):
            rows, at = pl.ds(pl.multiple_of(chip * 256, 256), 256), columns(0)
            res = nn(both[rows, 0:width], w[:, at]) + nt(both[rows, width:], tw[at, :])
            part[0, chip] = res.reshape(2, 128, blk)
            copies.append(
                send(
                    part.at[0, chip, 1 - core], sib.at[0, chip], one_s.at[n], one_r.at[n], to_sib
                )
            )
        return copies

    def pairs_first(copies):
        for n, (chip, copy) in enumerate(zip((far, left, right, mine), copies)):
            copy.wait()
            sib[0, chip] = sib[0, chip] + part[0, chip, core]
            if n == 0:
                far_src[0] = sib[0, far].astype(BF16)
                transit = send(far_src.at[0], far_dst.at[0], far_s.at[0], far_r.at[0], to_right)
            elif n == 1:
                out_src[0, 0] = sib[0, left].astype(BF16)
                direct = send(
                    out_src.at[0, 0], out_dst.at[0, 0], out_s.at[0, 0], out_r.at[0, 0], to_left
                )
        return transit, direct

    def pairs(i, copy):
        copy.wait()
        for chip in range(4):
            sib[i, chip] = sib[i, chip] + part[i % 2, chip, core]
        way, near = (to_right, to_left) if i % 2 == 0 else (to_left, to_right)
        near_chip = left if i % 2 == 0 else right
        far_src[i] = sib[i, far].astype(BF16)
        transit = send(far_src.at[i], far_dst.at[i], far_s.at[i], far_r.at[i], way)
        out_src[i, 0] = sib[i, near_chip].astype(BF16)
        direct = send(out_src.at[i, 0], out_dst.at[i, 0], out_s.at[i, 0], out_r.at[i, 0], near)
        return transit, direct

    def through(i, transit):
        transit.wait()
        way, chip = (to_right, right) if i % 2 == 0 else (to_left, left)
        out_src[i, 1] = (sib[i, chip] + far_dst[i].astype(F32)).astype(BF16)
        return send(out_src.at[i, 1], out_dst.at[i, 1], out_s.at[i, 1], out_r.at[i, 1], way)

    def pass_on(i, slot, chip, to):
        ref = probe.at[i, pl.ds(pl.multiple_of(chip * 256 + core * 128, 128), 128), :]
        return send(ref, ref, ag_s.at[i, slot], ag_r.at[i, slot], to)

    def own(i, direct, joined):
        direct.wait()
        joined.wait()
        rows = pl.ds(pl.multiple_of(mine * 256 + core * 128, 128), 128)
        res = sib[i, mine] + out_dst[i, 0].astype(F32) + out_dst[i, 1].astype(F32)
        probe[i, rows, :] = res.astype(BF16)
        go_right = pass_on(i, 0, mine, to_right)
        go_left = pass_on(i, 1, mine, to_left)
        return go_right, go_left, pass_on(i, 2, mine, to_sib)

    def forward(i, go_right, go_left):
        if i % 2 == 0:
            go_right.wait()
            onward = pass_on(i, 3, left, to_right)
            go_left.wait()
        else:
            go_left.wait()
            onward = pass_on(i, 3, right, to_left)
            go_right.wait()
        return onward, pass_on(i, 4, left, to_sib), pass_on(i, 5, right, to_sib)

    def last_hop(i, onward):
        onward.wait()
        return pass_on(i, 6, far, to_sib)

    def weight_part(i):
        return lax.dot_general(
            probe[i], both[:, width:], (((0,), (0,)), ((), ())), preferred_element_type=F32
        ).reshape(4, blk // 4, width)

    def back_block(i, waits):
        for copy in waits:
            copy.wait()
        at = columns(i)
        half = blk // 8
        sent = []
        if i < 2:
            gnw[i] = weight_part(i)
        for k in (2, 1, 3) if i < 2 else ():
            z = lax.rem(my_z + k, 4)
            sent.append(
                send(
                    gnw.at[i, z, 0:half, :], got_z.at[i, k - 1],
                    az_s.at[i, k], az_r.at[i, k], z_peers[k - 1],
                )
            )
        if i < 2:
            sent.append(
                send(
                    gnw.at[i, :, half : 2 * half, :], got_y.at[i],
                    ay_s.at[i], ay_r.at[i], y_peers[TURN[i] - 1],
                )
            )

        res = nt(probe[i], w[:, at])
        back[...] = res if i == 0 else back[...] + res
        return sent

    fetches[0].wait()
    fetches[1].wait()
    far0, dir0 = pairs_first(compute_first())
    sib1 = compute(1)
    sib2 = compute(2)
    far1, dir1 = pairs(1, sib1)
    join0 = through(0, far0)
    far2, dir2 = pairs(2, sib2)
    join1 = through(1, far1)
    sib3 = compute(3)
    ag0 = own(0, dir0, join0)
    ag1 = own(1, dir1, join1)
    fwd0 = forward(0, ag0[0], ag0[1])
    join2 = through(2, far2)
    far3, dir3 = pairs(3, sib3)
    fwd1 = forward(1, ag1[0], ag1[1])
    end0 = last_hop(0, fwd0[0])
    join3 = through(3, far3)
    sent = back_block(0, [ag0[2], fwd0[1], fwd0[2], end0])
    end1 = last_hop(1, fwd1[0])
    ag2 = own(2, dir2, join2)
    ag3 = own(3, dir3, join3)
    fwd2 = forward(2, ag2[0], ag2[1])
    sent = sent + back_block(1, [ag1[2], fwd1[1], fwd1[2], end1])
    fwd3 = forward(3, ag3[0], ag3[1])
    end2 = last_hop(2, fwd2[0])
    end3 = last_hop(3, fwd3[0])
    sent = sent + back_block(2, [ag2[2], fwd2[1], fwd2[2], end2])
    sent = sent + back_block(3, [ag3[2], fwd3[1], fwd3[2], end3])

    def mixing(i, carry):
        start = pl.multiple_of(i * 128, 128)
        rows = pl.ds(start, 128)
        inv_c = column(0, start)
        mixed = jnp.zeros((128, 128), F32)
        for g in range(groups):
            at = slice(128 * g, 128 * g + 128)
            prod = back[rows, at] * gated[rows, at]
            gain_o[:, at] = gain_o[:, at] + fold(prod * inv_c)
            mixed = mixed + prod * gain[:, at]
        mix[pl.ds(i, 1), :] = jnp.sum(mixed.T, axis=0, keepdims=True)
        return carry

    lax.fori_loop(0, length // 128, mixing, 0)
    copies = []
    for k, to in enumerate(peers):
        copies.append(send(mix, mix_got.at[head], mix_s.at[k], mix_r.at[k], {"head": to}))
    mix_got[head] = mix[...]
    for i in range(2):
        late_o[i] = weight_part(2 + i)
    for copy in copies:
        copy.wait()
    total = mix_got[0]
    for i in range(1, 8):
        total = total + mix_got[i]
    mix[...] = total / channels

    def finish(i, carry):
        start = pl.multiple_of(i * 128, 128)
        rows = pl.ds(start, 128)
        inv_c = column(0, start)
        mixed_c = jnp.broadcast_to(mix[pl.ds(i, 1), :], (128, 128)).T * (inv_c * inv_c * inv_c)
        for g in range(groups):
            at = slice(128 * g, 128 * g + 128)
            gz = gate_z[rows, at].astype(F32)
            gate = gz * jax.nn.sigmoid(gz)
            by_o[rows, at] = (
                back[rows, at] * gain[:, at] * inv_c - gated[rows, at] * mixed_c
            ) * gate
        return carry

    fetches[2].wait()
    lax.fori_loop(0, length // 128, finish, 0)
    for copy in sent:
        copy.wait()
    half = blk // 8
    for i in range(2):
        sum_z_o[i] = gnw[i, my_z, 0:half, :] + got_z[i, 0] + got_z[i, 1] + got_z[i, 2]
    sum_y_o[...] = late_o[1, :, half : 2 * half, :] + got_y[0] + got_y[1]


def middle_call(gated, dgated, sums, gate_z, w, tw, gain, tgain):
    length, width = gated.shape
    cols = w.shape[1]
    blk = cols // 4
    half = blk // 8
    out = lambda *s: jax.ShapeDtypeStruct(s, F32)
    dma = pltpu.SemaphoreType.DMA
    return pl.pallas_call(
        middle_kernel,
        in_specs=[VMEM] * 3 + [pl.BlockSpec(memory_space=pl.ANY)] * 3 + [VMEM] * 2,
        out_specs=[VMEM] * 5,
        out_shape=[
            out(length, width), out(8, width), out(2, half, width), out(4, half, width),
            out(2, 4, blk // 4, width),
        ],
        scratch_shapes=[
            pltpu.VMEM((8, 2, length), F32),
            pltpu.VMEM((8, length), F32),
            pltpu.VMEM((length, 2 * width), BF16),
            pltpu.VMEM((2, 4, 2, 128, blk), F32),
            pltpu.VMEM((4, 4, 128, blk), F32),
            pltpu.VMEM((4, 128, blk), BF16),
            pltpu.VMEM((4, 128, blk), BF16),
            pltpu.VMEM((4, 2, 128, blk), BF16),
            pltpu.VMEM((4, 2, 128, blk), BF16),
            pltpu.VMEM((4, length, blk), BF16),
            pltpu.VMEM((length, width), F32),
            pltpu.VMEM((2, 4, blk // 4, width), F32),
            pltpu.VMEM((2, 3, half, width), F32),
            pltpu.VMEM((2, 4, half, width), F32),
            pltpu.VMEM((8, 128), F32),
            pltpu.VMEM((8, 8, 128), F32),
            pltpu.VMEM((8, width), F32),
            pltpu.VMEM(gate_z.shape, BF16), pltpu.VMEM(w.shape, BF16), pltpu.VMEM(tw.shape, BF16),
            dma((3,)),
            dma((8,)), dma((8,)), dma((4,)), dma((4,)), dma((4,)), dma((4,)),
            dma((4, 2)), dma((4, 2)), dma((4, 7)), dma((4, 7)), dma((8,)), dma((8,)),
            dma((2, 4)), dma((2, 4)), dma((2,)), dma((2,)), dma((4,)), dma((4,)),
        ],
        compiler_params=pltpu.CompilerParams(
            collective_id=3, has_side_effects=True, vmem_limit_bytes=61 * 1024 * 1024
        ),
        name="probe_and_back",
    )(gated, dgated, sums, gate_z, w, tw, gain, tgain)


def fold(a):
    return jnp.sum(a.reshape(a.shape[0] // 8, 8, a.shape[1]), axis=0)


def adjoint_kernel(
    by, x, gx, pre_x, halo_x, bc, gbc, pre_bc, halo_bc, rowv, colv, s0_b, log, last_log,
    gain, decays, hp, sum_z, sum_y, late,
    result_o,
    wx, wbc, head_o, pack_o, lam, back_u_a, back_bc_a, state, msg, landed, answer, s_end,
    own_z, own_y, got_z, got_y, end_z, end_y, pack_z, landed_z, landed_y, part, landed_q,
    az_s, az_r, ay_s, ay_r, bz_s, bz_r, by_s, by_r,
    s1_s, s1_r, s2_s, s2_r, f1_s, f1_r, f3_s, f3_r, f2_s, f2_r,
):
    step = pl.program_id(0)
    half = lam.shape[0]
    nst = bc.shape[1] // 2
    width = by.shape[1]
    heads = width // HW
    count, n_head = landed.shape[0], landed_q.shape[0]
    me, head = lax.axis_index("seq"), lax.axis_index("head")
    my_y, my_z = me // 4, lax.rem(me, 4)
    seq_peers, head_peers = others("seq", count), others("head", n_head)
    rows_half = sum_z.shape[1]
    mask = lane_mask()

    y_peers = [{"seq": lax.rem(my_y + k, 4) * 4 + my_z} for k in range(1, 4)]
    z_peers = [{"seq": my_y * 4 + lax.rem(my_z + k, 4)} for k in range(1, 4)]

    def late_copies(part_at):
        copies = []
        for i, k in ((0, 1), (0, 3)) if part_at % 2 == 0 else ((0, 2),):
            i = i + part_at // 2
            copies.append(
                link(
                    late.at[i, lax.rem(my_z + k, 4), 0:rows_half, :], got_z.at[i, k - 1],
                    az_s.at[i, k], az_r.at[i, k], z_peers[k - 1],
                )
            )
        copies.append(
            link(
                late.at[0, part_at, rows_half : 2 * rows_half, :], got_y.at[part_at],
                ay_s.at[part_at], ay_r.at[part_at], y_peers[TURN[2] - 1],
            )
        )
        return copies

    def early_last():
        return [
            link(sum_z.at[i], end_z.at[i], bz_s.at[i], bz_r.at[i], y_peers[TURN[i] - 1])
            for i in range(2)
        ]

    def last_copies():
        copies = [link(own_z, end_z.at[2], bz_s.at[2], bz_r.at[2], y_peers[TURN[2] - 1])]
        for k in (2, 1, 3):
            z = lax.rem(my_z + k, 4)
            copies.append(
                link(own_y.at[z], end_y.at[k - 1], by_s.at[k], by_r.at[k], z_peers[k - 1])
            )
        return copies

    for part_at, when in enumerate((0, 3, half + SCAN_AT + 1, half + SCAN_AT + 2)):

        @pl.when(step == when)
        def _(part_at=part_at):
            if part_at == 0:
                greet([{"seq": to} for to in seq_peers] + [{"head": to} for to in head_peers])
            for copy in late_copies(part_at) + (early_last() if part_at == 3 else []):
                copy.start()

    @pl.when(step == 0)
    def _():
        state[...] = jnp.zeros_like(state)
        head_o[...] = jnp.zeros_like(head_o)
        pack_o[...] = jnp.zeros_like(pack_o)
        pack_o[8:9, :] = jnp.sum(gain[...], axis=0, keepdims=True)

    @pl.when(step < half)
    def _():
        lam[half - 1 - step] = state[...]
        cols = colv[...]
        ct_h, ct_l = split(bc[:, nst:].T)
        for p in range(heads // 2):
            at = slice(128 * p, 128 * p + 128)
            lifted = jnp.exp(expand(cols, C_, p)) * by[:, at]
            l_h, l_l = split(lifted)
            add = nn(ct_h, l_h) + nn(ct_h, l_l) + nn(ct_l, l_h)
            state[:, at] = jnp.exp(log[0, 2:3, at]) * state[:, at] + add

    def scan_copies():
        return [
            link(msg.at[to], landed.at[me], s1_s.at[k], s1_r.at[k], {"seq": to})
            for k, to in enumerate(seq_peers)
        ]

    def back_copies():
        return [
            link(answer.at[to], s_end.at[me], s2_s.at[k], s2_r.at[k], {"seq": to})
            for k, to in enumerate(seq_peers)
        ]

    @pl.when(step == half - 1)
    def _():
        msg[...] = state[...].reshape(count, 8, width)
        for copy in scan_copies():
            copy.start()

    @pl.when(step == half + SCAN_AT)
    def _():
        landed[me] = msg[me]
        for copy in scan_copies():
            copy.wait()
        adjoint = jnp.zeros((8, width), F32)
        for i in range(count - 1, -1, -1):
            answer[i] = adjoint
            adjoint = decays[i : i + 1, :] * adjoint + landed[i]
        for copy in back_copies():
            copy.start()

    @pl.when((step >= half) & (step < 2 * half))
    def _():
        block = step - half
        b_mat, c_mat = bc[:, :nst], bc[:, nst:]
        at_i = lax.broadcasted_iota(jnp.int32, (QB, QB), 1)
        at_j = lax.broadcasted_iota(jnp.int32, (QB, QB), 0)
        keep = at_i >= at_j
        inner_t = jnp.where(keep, nt3(b_mat, c_mat), 0.0)
        cols = colv[...]
        rows = rowv[...]
        back_inner_t = jnp.zeros((QB, QB), F32)
        for p in range(heads // 2):
            at = slice(128 * p, 128 * p + 128)
            byp = by[:, at]
            u = expand(cols, S_, p) * x[:, at]
            y_h, y_l = split(byp)
            u_h, u_l = split(
                jnp.concatenate([jnp.where(mask, u, 0.0), jnp.where(mask, 0.0, u)], axis=0)
            )
            back_mts = nt(
                jnp.concatenate([u_h, u_l], axis=1), jnp.concatenate([y_h, y_h], axis=1)
            ) + nt(u_h, y_l)
            mats = []
            for s in range(2):
                h = 2 * p + s
                c_row = rows[C_ + h : C_ + h + 1, :]
                cs_row = rows[CS_ + h : CS_ + h + 1, :]
                back_mt = back_mts[s * QB : s * QB + QB]
                diff = jnp.minimum(c_row - bcast(cols, C_ + h), 0.0)
                level = jnp.exp(diff)
                back_inner_t = back_inner_t + level * back_mt
                m_t = inner_t * level
                prod = m_t * back_mt
                head_o[h, 0] = head_o[h, 0] + fold(prod * diff)
                head_o[h, 1] = head_o[h, 1] + fold(prod * (cs_row - bcast(cols, CS_ + h)))
                mats.append(m_t)
            a_h, a_l = split(jnp.concatenate(mats, axis=0))
            back_u2 = nn(
                jnp.concatenate([a_h, a_l], axis=1), jnp.concatenate([y_h, y_h], axis=0)
            ) + nn(a_h, y_l)
            back_u_a[block, :, at] = jnp.where(mask, back_u2[:QB], back_u2[QB:])
        back_inner_t = jnp.where(keep, back_inner_t, 0.0)
        back_bc_a[block, :, 0:nst] = nn3(back_inner_t, c_mat)
        back_bc_a[block, :, nst:] = nn3(back_inner_t.T, b_mat)

    @pl.when(step == 2 * half)
    def _():
        s_end[me] = answer[me]
        for copy in back_copies():
            copy.wait()

    @pl.when(step >= 2 * half)
    def _():
        block = step - 2 * half
        load_window(wx, halo_x, pre_x, step == 2 * half)
        load_window(wbc, halo_bc, pre_bc, step == 2 * half)
        b_h, b_l = split(bc[:, :nst])
        c_h, c_l = split(bc[:, nst:])
        cols = colv[...]
        back_b = back_bc_a[block, :, 0:nst]
        back_c = back_bc_a[block, :, nst:]
        for p in range(heads // 2):
            at = slice(128 * p, 128 * p + 128)
            own, sig_own = log[0, 2:3, at], log[0, 4:5, at]
            reach = jnp.exp(last_log[0, 0:1, at] + last_log[0, 2:3, at] - log[0, 0:1, at] - own)
            s1 = lam[block, :, at] + reach * s_end[:, :, at].reshape(nst, 128)
            s0 = s0_b[0, :, at]
            byp, xp = by[:, at], x[:, at]
            size = expand(cols, S_, p)
            c_cols, cs_cols = expand(cols, C_, p), expand(cols, CS_, p)
            left = own - c_cols
            to_end = jnp.exp(left)
            u = size * xp
            lifted = jnp.exp(c_cols) * byp
            s0_h, s0_l = split(s0)
            s1_h, s1_l = split(s1)
            l_h, l_l = split(lifted)
            e_h, e_l = split(to_end * u)
            back_c = back_c + nt(
                jnp.concatenate([l_h, l_l], axis=1), jnp.concatenate([s0_h, s0_h], axis=1)
            ) + nt(l_h, s0_l)
            back_b = back_b + nt(
                jnp.concatenate([e_h, e_l], axis=1), jnp.concatenate([s1_h, s1_h], axis=1)
            ) + nt(e_h, s1_l)
            through_c = lifted * (nn(c_h, s0_h) + nn(c_h, s0_l) + nn(c_l, s0_h))
            from_end = to_end * (nn(b_h, s1_h) + nn(b_h, s1_l) + nn(b_l, s1_h))
            through_b = u * from_end
            back_u = back_u_a[block, :, at] + from_end
            back_x = back_u * size + expand(hp[2:3, :], 0, p) * byp
            carried = jnp.sum(s1 * s0, axis=0, keepdims=True) * jnp.exp(own)
            total = lambda a: jnp.sum(a, axis=0, keepdims=True)
            pack_o[4:5, at] = pack_o[4:5, at] + total(expand(cols, SG_, p) * (back_u * xp))
            pack_o[5:6, at] = (
                pack_o[5:6, at] + carried * own + total(through_c * c_cols + through_b * left)
            )
            pack_o[6:7, at] = (
                pack_o[6:7, at]
                + carried * sig_own
                + total(through_c * cs_cols + through_b * (sig_own - cs_cols))
            )
            pack_o[7:8, at] = pack_o[7:8, at] + total(byp * xp)
            back_z = back_x * gx[:, at]
            for k in range(4):
                pack_o[k : k + 1, at] = pack_o[k : k + 1, at] + total(
                    back_z * wx[5 + k : 5 + k + QB, at]
                )
        back_zbc = jnp.concatenate([back_b, back_c], axis=1) * gbc[...]
        for k in range(4):
            pack_o[9 + k : 10 + k, 0 : 2 * nst] = pack_o[
                9 + k : 10 + k, 0 : 2 * nst
            ] + jnp.sum(back_zbc * wbc[5 + k : 5 + k + QB, :], axis=0, keepdims=True)

    @pl.when(step == 3 * half - 5)
    def _():
        for part_at in range(4):
            for copy in late_copies(part_at):
                copy.wait()
        own_z[...] = late[0, my_z, 0:rows_half, :] + got_z[0, 0] + got_z[0, 1] + got_z[0, 2]
        own_y[...] = sum_y[...] + got_y[...]
        for copy in last_copies():
            copy.start()

    @pl.when(step == 3 * half - 1)
    def _():
        for p in range(heads // 2):
            at = slice(128 * p, 128 * p + 128)
            for kind in range(2):
                even, odd = head_o[2 * p, kind], head_o[2 * p + 1, kind]
                even = even + pltpu.roll(even, HW, 1)
                odd = odd + pltpu.roll(odd, HW, 1)
                both = jnp.sum(jnp.where(mask, even, odd), axis=0, keepdims=True)
                pack_o[5 + kind : 6 + kind, at] = pack_o[5 + kind : 6 + kind, at] + both
        for slots, group, sems, mine in (
            (landed_z, z_peers, (f1_s, f1_r), pack_o),
            (landed_y, y_peers, (f3_s, f3_r), pack_z),
        ):
            copies = []
            for k, to in enumerate(group):
                copies.append(send(mine, slots.at[k], sems[0].at[k], sems[1].at[k], to))
            for copy in copies:
                copy.wait()
            if slots is landed_z:
                for z in range(4):
                    k = lax.rem(my_z + 3 - z, 4)
                    term = jnp.where(z == my_z, pack_o[...], slots[jnp.minimum(k, 2)])
                    total = term if z == 0 else total + term
                pack_z[...] = total
            else:
                for y in range(4):
                    k = lax.rem(my_y + 3 - y, 4)
                    term = jnp.where(y == my_y, pack_z[...], slots[jnp.minimum(k, 2)])
                    total = term if y == 0 else total + term
        part[...] = total[8:16, 0 : 2 * nst]
        copies = []
        for k, to in enumerate(head_peers):
            copies.append(send(part, landed_q.at[head], f2_s.at[k], f2_r.at[k], {"head": to}))
        landed_q[head] = part[...]
        result_o[2 * rows_half : 2 * rows_half + 16] = total
        at = lax.broadcasted_iota(jnp.int32, (width, 128), 0)
        to = lax.broadcasted_iota(jnp.int32, (width, 128), 1) * HW
        pick = jnp.where((at >= to) & (at < to + HW), 1.0, 0.0).astype(F32)
        sums = jnp.dot(
            total, pick, precision=lax.Precision.HIGHEST, preferred_element_type=F32
        )[:, :heads]
        at = 2 * rows_half + 24
        result_o[at : at + 1, 0:heads] = sums[4:5] - jnp.exp(hp[1:2]) * sums[6:7]
        result_o[at + 1 : at + 2, 0:heads] = sums[5:6]
        result_o[at + 2 : at + 3, 0:heads] = sums[7:8]
        for copy in early_last() + last_copies():
            copy.wait()
        total = late[1, my_z, 0:rows_half, :] + got_z[1, 0] + got_z[1, 1] + got_z[1, 2]
        result_o[0:rows_half] = total + end_z[0] + end_z[1] + end_z[2]
        result_o[rows_half : 2 * rows_half] = own_y[my_z] + end_y[0] + end_y[1] + end_y[2]
        for copy in copies:
            copy.wait()
        total2 = landed_q[0]
        for i in range(1, n_head):
            total2 = total2 + landed_q[i]
        result_o[2 * rows_half + 16 : 2 * rows_half + 24, 0 : 2 * nst] = total2


def adjoint_call(
    by, x, gx, pre_x, halo_x, bc, gbc, pre_bc, halo_bc, rowv, colv, s0, logs, gain, decays,
    hp, sum_z, sum_y, late_sums, count, n_head,
):
    length, width = by.shape
    wide = bc.shape[1]
    nst = wide // 2
    heads = width // HW
    half = length // QB
    rows_half = sum_z.shape[1]
    piece = 2 * rows_half
    every = lambda i: jnp.where(i < half, half - 1 - i, lax.rem(i, half))
    mid = lambda i: jnp.where(i < half, 0, lax.rem(i, half))
    late = lambda i: jnp.maximum(i - 2 * half, 0)
    whole = lambda a: pl.BlockSpec(a.shape, lambda i: (0,) * a.ndim)
    rows = lambda w, f: pl.BlockSpec((QB, w), lambda i: (f(i), 0))
    cube = lambda r, f: pl.BlockSpec((1, r, width), lambda i: (f(i), 0, 0))
    out = lambda *s: jax.ShapeDtypeStruct(s, F32)
    fixed = lambda *s: pl.BlockSpec(s, lambda i: (0,) * len(s))
    dma = pltpu.SemaphoreType.DMA
    return pl.pallas_call(
        adjoint_kernel,
        grid=(3 * half,),
        in_specs=[
            rows(width, every), rows(width, mid), rows(width, late), rows(width, late),
            whole(halo_x), rows(wide, every), rows(wide, late), rows(wide, late), whole(halo_bc),
            pl.BlockSpec((128, QB), lambda i: (0, mid(i))), rows(128, every),
            cube(nst, late), cube(8, every),
            pl.BlockSpec((1, 8, width), lambda i: (half - 1, 0, 0)),
            whole(gain), whole(decays), whole(hp),
            whole(sum_z), whole(sum_y), VMEM,
        ],
        out_specs=fixed(256, width),
        out_shape=out(256, width),
        scratch_shapes=[
            pltpu.VMEM((QB + 8, width), F32), pltpu.VMEM((QB + 8, wide), F32),
            pltpu.VMEM((heads, 2, 8, 128), F32), pltpu.VMEM((16, width), F32),
            pltpu.VMEM((half, nst, width), F32), pltpu.VMEM((half, QB, width), F32),
            pltpu.VMEM((half, QB, wide), F32), pltpu.VMEM((nst, width), F32),
            pltpu.VMEM((count, 8, width), F32), pltpu.VMEM((count, 8, width), F32),
            pltpu.VMEM((count, 8, width), F32), pltpu.VMEM((count, 8, width), F32),
            pltpu.VMEM((rows_half, width), F32), pltpu.VMEM((4, rows_half, width), F32),
            pltpu.VMEM((2, 3, rows_half, width), F32), pltpu.VMEM((4, rows_half, width), F32),
            pltpu.VMEM((3, rows_half, width), F32), pltpu.VMEM((3, rows_half, width), F32),
            pltpu.VMEM((16, width), F32), pltpu.VMEM((3, 16, width), F32),
            pltpu.VMEM((3, 16, width), F32), pltpu.VMEM((8, wide), F32),
            pltpu.VMEM((n_head, 8, wide), F32),
            dma((2, 4)), dma((2, 4)), dma((4,)), dma((4,)),
            dma((4,)), dma((4,)), dma((4,)), dma((4,)),
            dma((count,)), dma((count,)), dma((count,)), dma((count,)),
            dma((3,)), dma((3,)), dma((3,)), dma((3,)), dma((n_head,)), dma((n_head,)),
        ],
        compiler_params=pltpu.CompilerParams(
            collective_id=2, has_side_effects=True, vmem_limit_bytes=LIMIT
        ),
        name="adjoint",
    )(
        by, x, gx, pre_x, halo_x, bc, gbc, pre_bc, halo_bc, rowv, colv, s0, logs, logs,
        gain, decays, hp, sum_z, sum_y, late_sums,
    )


def outputs_kernel(result, gcx_o, gcbc_o, heads_o, gain_o, gnw_o):
    piece, heads, wide = gnw_o.shape[0], heads_o.shape[1], gcbc_o.shape[1]
    width = result.shape[1]
    gcx_o[...] = result[piece : piece + 4]
    gain_o[...] = result[piece + 8 : piece + 9].reshape(width)
    gcbc_o[...] = result[piece + 17 : piece + 21, 0:wide]
    heads_o[...] = result[piece + 24 : piece + 27, 0:heads]
    gnw_o[...] = result[0:piece]


def outputs_call(result, piece, bc_shape, heads_shape):
    width = result.shape[1]
    out = lambda *s: jax.ShapeDtypeStruct(s, F32)
    return pl.pallas_call(
        outputs_kernel,
        in_specs=[VMEM],
        out_specs=[VMEM] * 5,
        out_shape=[
            out(4, width), out(*bc_shape), out(*heads_shape), out(width), out(piece, width),
        ],
        name="outputs",
    )(result)


def on_device(
    pre_x, pre_bc, gate_z, dt_raw, conv_x, conv_bc, head_params, norm_gain, w_out,
    t_conv_x, t_conv_bc, t_heads, t_gain, t_wout,
):
    count = lax.axis_size("seq")
    x, gx, bc, gbc, rowv, colv, logs, s0, gated, d_gated, sums, decays, halo_x, halo_bc, tw = forward_call(
        pre_x, pre_bc, dt_raw, gate_z, conv_x, t_conv_x, conv_bc, t_conv_bc, head_params, t_heads,
        t_wout.T, count,
    )
    back_y, gain_part, sum_z, sum_y, late_sums = middle_call(
        gated, d_gated, sums, gate_z, w_out, tw.reshape(-1, w_out.shape[0]), norm_gain, t_gain
    )
    result = adjoint_call(
        back_y, x, gx, pre_x, halo_x, bc, gbc, pre_bc, halo_bc, rowv, colv, s0, logs,
        gain_part, decays, head_params, sum_z, sum_y, late_sums, count, lax.axis_size("head"),
    )
    gn_conv_x, gn_conv_bc, gn_heads, gn_gain, gn_wout = outputs_call(
        result, t_wout.shape[1], conv_bc.shape, head_params.shape
    )
    return gn_conv_x, gn_conv_bc, gn_heads, gn_gain, gn_wout.T


def solution(mesh):
    in_specs = (
        P("seq", "head"), P("seq", None), P("seq", "head"), P("head", "seq"), P(None, "head"),
        P(), P(None, "head"), P("head"), P("head", None), P(None, "head"), P(), P(None, "head"),
        P("head"), P("head", "seq"),
    )
    out_specs = (P(None, "head"), P(), P(None, "head"), P("head"), P("head", "seq"))
    return jax.shard_map(
        on_device, mesh=mesh, in_specs=in_specs, out_specs=out_specs, check_vma=False
    )
```

```python
import jax
import jax.numpy as jnp
from jax import lax
from jax.experimental import pallas as pl
from jax.experimental.pallas import tpu as pltpu
from jax.sharding import PartitionSpec as P

QB = 128
HW = 64
F32 = jnp.float32
BF16 = jnp.bfloat16
MESH = pl.DeviceIdType.MESH
S_, DS_, C_, DC_, CS_, SG_, K_, DK_ = (16 * i for i in range(8))
LIMIT = 56 * 1024 * 1024
SCAN_AT = 4
TURN = (1, 3, 2, 4)


def split(a):
    high = a.astype(BF16)
    return high, (a - high.astype(F32)).astype(BF16)


def nn(a, b):
    return jnp.dot(a, b, preferred_element_type=F32)


def nt(a, b):
    return lax.dot_general(a, b, (((1,), (1,)), ((), ())), preferred_element_type=F32)


def nn3(a, b):
    (ah, al), (bh, bl) = split(a), split(b)
    return nn(ah, bh) + nn(ah, bl) + nn(al, bh)


def nt3(a, b):
    (ah, al), (bh, bl) = split(a), split(b)
    return nt(ah, bh) + nt(ah, bl) + nt(al, bh)


def lane_mask():
    return lax.broadcasted_iota(jnp.int32, (1, 128), 1) < HW


def bcast(cols, at):
    return jnp.broadcast_to(cols[:, at : at + 1], (cols.shape[0], 128))


def expand(cols, base, pair):
    return jnp.where(
        lane_mask(), bcast(cols, base + 2 * pair), bcast(cols, base + 2 * pair + 1)
    )


def expand_all(cols, base, heads):
    return jnp.concatenate([expand(cols, base, p) for p in range(heads // 2)], axis=1)


def load_window(window, halo, block, first):
    @pl.when(first)
    def _():
        window[0:8] = halo[...]

    @pl.when(jnp.logical_not(first))
    def _():
        window[0:8] = window[QB : QB + 8]

    window[8 : QB + 8] = block[...].astype(F32)


def conv_pair(window, weight, t_weight):
    z = jnp.zeros((QB, window.shape[1]), F32)
    dz = jnp.zeros((QB, window.shape[1]), F32)
    for k in range(4):
        rows = window[5 + k : 5 + k + QB, :]
        z = z + weight[k : k + 1, :] * rows
        dz = dz + t_weight[k : k + 1, :] * rows
    sig = jax.nn.sigmoid(z)
    slope = sig * (1.0 + z * (1.0 - sig))
    return z * sig, slope * dz, slope


def greet(peers):
    barrier = pltpu.get_barrier_semaphore()
    for peer in peers:
        pl.semaphore_signal(barrier, inc=1, device_id=peer, device_id_type=MESH)
    pl.semaphore_wait(barrier, len(peers))


def others(axis, count):
    me = lax.axis_index(axis)
    return [lax.rem(me + k, count) for k in range(1, count)]


def link(src, dst, send_sem, recv_sem, device):
    return pltpu.make_async_remote_copy(
        src_ref=src, dst_ref=dst, send_sem=send_sem, recv_sem=recv_sem,
        device_id=device, device_id_type=MESH,
    )


def send(*what):
    copy = link(*what)
    copy.start()
    return copy


VMEM = pl.BlockSpec(memory_space=pltpu.VMEM)


def column_of(row):
    heads = row.shape[1]
    at_i = lax.broadcasted_iota(jnp.int32, (heads, heads), 0)
    at_j = lax.broadcasted_iota(jnp.int32, (heads, heads), 1)
    return jnp.sum(jnp.where(at_i == at_j, row, 0.0), axis=1, keepdims=True)


def forward_kernel(
    pre_x, tail_x, pre_bc, tail_bc, dt, gate_z, cx, tcx, cbc, tcbc, hp, th, tw_in,
    x_o, gx_o, bc_o, gbc_o, row_o, col_o, log_o, s0_o, gated_o, dgated_o, sums_o, decay_o,
    halo_x_o, halo_bc_o, tw_o,
    wx, wbc, feat, state, d_state, logs, x_a, dx_a, bc_a, dbc_a, row_a, col_a, st_a, dst_a,
    log_a, y_a, dy_a, tile, got_x, got_bc, msg, landed, tiles, answer, start,
    halo_s, halo_r, tile_s, tile_r, s1_s, s1_r, s2_s, s2_r,
    own_m, gz_s, gz_r, gy_s, gy_r, hz_s, hz_r, hy_s, hy_r,
):
    step = pl.program_id(0)
    blocks = st_a.shape[0]
    heads = dt.shape[0]
    width = pre_x.shape[1]
    nst = cbc.shape[1] // 2
    count = landed.shape[0]
    me = lax.axis_index("seq")
    peers = others("seq", count)
    mask = lane_mask()

    my_y, my_z = me // 4, lax.rem(me, 4)
    y_peers = [{"seq": lax.rem(my_y + k, 4) * 4 + my_z} for k in range(1, 4)]
    z_peers = [{"seq": my_y * 4 + lax.rem(my_z + k, 4)} for k in range(1, 4)]
    piece = tw_in.shape[0]
    upper_rows, lower_rows = slice(0, piece // 2), slice(piece // 2, piece)

    def own_copy():
        return pltpu.make_async_copy(tw_in, tw_o.at[my_y, my_z], own_m.at[0])

    def gather_first():
        copies = []
        for k in (2, 1, 3):
            copies.append(
                link(
                    tw_in.at[upper_rows, :], tw_o.at[my_y, my_z, upper_rows, :],
                    gz_s.at[k], gz_r.at[k], z_peers[k - 1],
                )
            )
            copies.append(
                link(
                    tw_in.at[lower_rows, :], tw_o.at[my_y, my_z, lower_rows, :],
                    gy_s.at[k], gy_r.at[k], y_peers[k - 1],
                )
            )
        return copies

    def gather_second(k):
        along_y = tw_o.at[my_y, :, upper_rows, :]
        along_z = tw_o.at[:, my_z, lower_rows, :]
        return [
            link(along_y, along_y, hz_s.at[k], hz_r.at[k], y_peers[k - 1]),
            link(along_z, along_z, hy_s.at[k], hy_r.at[k], z_peers[k - 1]),
        ]

    def scan_copies():
        copies = []
        for k, to in enumerate(peers):
            at = {"seq": to}
            copies.append(link(tile, tiles.at[me], tile_s.at[k], tile_r.at[k], at))
            copies.append(link(msg.at[to], landed.at[me], s1_s.at[k], s1_r.at[k], at))
        return copies

    def back_copies():
        return [
            link(answer.at[to], start.at[me], s2_s.at[k], s2_r.at[k], {"seq": to})
            for k, to in enumerate(peers)
        ]

    @pl.when(step == 0)
    def _():
        greet([{"seq": to} for to in peers])
        after = {"seq": lax.rem(me + 1, count)}
        tails = [
            send(tail_x, got_x, halo_s.at[0], halo_r.at[0], after),
            send(tail_bc, got_bc, halo_s.at[1], halo_r.at[1], after),
        ]
        state[...] = jnp.zeros_like(state)
        d_state[...] = jnp.zeros_like(d_state)
        logs[...] = jnp.zeros_like(logs)
        feat[...] = jnp.zeros_like(feat)
        tile[...] = jnp.zeros_like(tile)
        for copy in tails:
            copy.wait()
        halo_x_o[...] = jnp.where(me == 0, 0.0, got_x[...].astype(F32)[8:16])
        halo_bc_o[...] = jnp.where(me == 0, 0.0, got_bc[...].astype(F32)[8:16])
        own_copy().start()
        for copy in gather_first():
            copy.start()

    @pl.when(step == 3)
    def _():
        own_copy().wait()
        for copy in gather_first():
            copy.wait()
        for copy in gather_second(1) + gather_second(3):
            copy.start()

    @pl.when(step == 3 * blocks - 1)
    def _():
        for k in (1, 3, 2):
            for copy in gather_second(k):
                copy.wait()

    @pl.when(step < blocks)
    def _():
        load_window(wx, halo_x_o, pre_x, step == 0)
        load_window(wbc, halo_bc_o, pre_bc, step == 0)
        z = dt[...] + column_of(hp[0:1, :])
        rate = jnp.exp(column_of(hp[1:2, :]))
        t_bias, t_lrate = column_of(th[0:1, :]), column_of(th[1:2, :])
        size = jnp.maximum(z, 0.0) + jnp.log1p(jnp.exp(-jnp.abs(z)))
        sig = jax.nn.sigmoid(z)
        log_decay = -size * rate
        at_i = lax.broadcasted_iota(jnp.int32, (QB, QB), 1)
        at_j = lax.broadcasted_iota(jnp.int32, (QB, QB), 0)
        upper = jnp.where(at_j <= at_i, 1.0, 0.0).astype(F32)
        exact = dict(precision=lax.Precision.HIGHEST, preferred_element_type=F32)
        cumul = jnp.dot(log_decay, upper, **exact)
        sig_sum = jnp.dot(sig, upper, **exact)
        d_size = sig * t_bias
        d_cumul = cumul * t_lrate - rate * t_bias * sig_sum
        to_end = jnp.exp(cumul[:, QB - 1 : QB] - cumul)
        feat[S_ : S_ + heads] = size
        feat[DS_ : DS_ + heads] = d_size
        feat[C_ : C_ + heads] = cumul
        feat[DC_ : DC_ + heads] = d_cumul
        feat[CS_ : CS_ + heads] = sig_sum
        feat[SG_ : SG_ + heads] = sig
        feat[K_ : K_ + heads] = to_end * size
        feat[DK_ : DK_ + heads] = to_end * (
            d_size + size * (d_cumul[:, QB - 1 : QB] - d_cumul)
        )
        rows = feat[...]
        cols = rows.T
        row_o[...] = rows
        col_o[...] = cols
        row_a[step] = rows
        col_a[step] = cols

        bc, dbc, gbc = conv_pair(wbc, cbc, tcbc)
        bc_o[...] = bc
        gbc_o[...] = gbc
        bc_a[step] = bc
        dbc_a[step] = dbc
        x, dx, gx = conv_pair(wx, cx, tcx)
        x_o[...] = x
        gx_o[...] = gx
        x_a[step] = x
        dx_a[step] = dx

        last = cols[QB - 1 : QB, :]
        tile[0:1, :] = tile[0:1, :] + last
        own = expand_all(last, C_, heads)
        d_own = expand_all(last, DC_, heads)
        log = jnp.concatenate(
            [logs[0:1, :], logs[1:2, :], own, d_own, expand_all(last, CS_, heads)]
            + [jnp.zeros((3, width), F32)],
            axis=0,
        )
        log_o[0] = log
        log_a[step] = log
        logs[0:1, :] = logs[0:1, :] + own
        logs[1:2, :] = logs[1:2, :] + d_own

        st_a[step] = state[...]
        dst_a[step] = d_state[...]
        bt = bc[:, :nst].T
        dbt = dbc[:, :nst].T
        both_h, both_l = split(jnp.concatenate([bt, dbt], axis=1))
        for p in range(heads // 2):
            at = slice(128 * p, 128 * p + 128)
            k_x, dk_x = expand(cols, K_, p), expand(cols, DK_, p)
            ux = k_x * x[:, at]
            dux = k_x * dx[:, at] + dk_x * x[:, at]
            z_h, z_l = split(jnp.concatenate([dux, ux], axis=0))
            d_add = nn(both_h, z_h) + nn(both_h, z_l) + nn(both_l, z_h)
            b_h, b_l, u_h, u_l = both_h[:, :QB], both_l[:, :QB], z_h[QB:], z_l[QB:]
            add = nn(b_h, u_h) + nn(b_h, u_l) + nn(b_l, u_h)
            decay = jnp.exp(own[:, at])
            before = state[:, at]
            d_state[:, at] = decay * (d_state[:, at] + d_own[:, at] * before) + d_add
            state[:, at] = decay * before + add

    @pl.when(step == blocks - 1)
    def _():
        msg[:, 0:8, :] = state[...].reshape(count, 8, width)
        msg[:, 8:16, :] = d_state[...].reshape(count, 8, width)
        for copy in scan_copies():
            copy.start()

    @pl.when(step == blocks + SCAN_AT)
    def _():
        landed[me] = msg[me]
        tiles[me] = tile[...]
        for copy in scan_copies():
            copy.wait()
        total = jnp.zeros((8, width), F32)
        d_total = jnp.zeros((8, width), F32)
        features = tiles[...][:, 0, :]
        decays = jnp.exp(expand_all(features, C_, heads))
        d_logs = expand_all(features, DC_, heads)
        decay_o[...] = decays
        for i in range(count):
            answer[i, 0:8] = total
            answer[i, 8:16] = d_total
            decay = decays[i : i + 1]
            d_total = decay * (d_total + d_logs[i : i + 1] * total)
            d_total = d_total + landed[i, 8:16]
            total = decay * total + landed[i, 0:8]
        for copy in back_copies():
            copy.start()

    @pl.when((step >= blocks) & (step < 2 * blocks))
    def _():
        block = step - blocks
        bc, dbc = bc_a[block], dbc_a[block]
        b_mat, c_mat = bc[:, :nst], bc[:, nst:]
        db_mat, dc_mat = dbc[:, :nst], dbc[:, nst:]
        at_j = lax.broadcasted_iota(jnp.int32, (QB, QB), 1)
        at_i = lax.broadcasted_iota(jnp.int32, (QB, QB), 0)
        keep = at_i >= at_j
        inner = jnp.where(keep, nt3(c_mat, b_mat), 0.0)
        d_inner = jnp.where(
            keep,
            nt3(
                jnp.concatenate([dc_mat, c_mat], axis=1),
                jnp.concatenate([b_mat, db_mat], axis=1),
            ),
            0.0,
        )
        cols = col_a[block]
        rows = row_a[block]
        for p in range(heads // 2):
            at = slice(128 * p, 128 * p + 128)
            xp, dxp = x_a[block, :, at], dx_a[block, :, at]
            size, d_size = expand(cols, S_, p), expand(cols, DS_, p)
            z_h, z_l = split(size * xp)
            dz_h, dz_l = split(size * dxp + d_size * xp)
            mats, d_mats = [], []
            for h in (2 * p, 2 * p + 1):
                c_row = rows[C_ + h : C_ + h + 1, :]
                dc_row = rows[DC_ + h : DC_ + h + 1, :]
                level = jnp.exp(jnp.minimum(bcast(cols, C_ + h) - c_row, 0.0))
                m = inner * level
                mats.append(m)
                d_mats.append(d_inner * level + m * (bcast(cols, DC_ + h) - dc_row))
            a_h, a_l = split(jnp.concatenate(mats, axis=0))
            da_h, da_l = split(jnp.concatenate(d_mats, axis=0))
            zz_h = jnp.concatenate([z_h, dz_h], axis=1)
            big = nn(
                jnp.concatenate([a_h, a_l], axis=1), jnp.concatenate([zz_h, zz_h], axis=0)
            ) + nn(a_h, jnp.concatenate([z_l, dz_l], axis=1))
            small = nn(
                jnp.concatenate([da_h, da_l], axis=1), jnp.concatenate([z_h, z_h], axis=0)
            ) + nn(da_h, z_l)
            y2 = big[:, :128]
            dy2 = big[:, 128:] + small
            skip, d_skip = expand(hp[2:3, :], 0, p), expand(th[2:3, :], 0, p)
            y_a[block, :, at] = jnp.where(mask, y2[:QB], y2[QB:]) + skip * xp
            dy_a[block, :, at] = (
                jnp.where(mask, dy2[:QB], dy2[QB:]) + skip * dxp + d_skip * xp
            )

    @pl.when(step == 2 * blocks)
    def _():
        start[me] = answer[me]
        for copy in back_copies():
            copy.wait()
        for copy in gather_second(2):
            copy.start()

    @pl.when(step >= 2 * blocks)
    def _():
        block = step - 2 * blocks
        cols = col_a[block]
        c_h, c_l = split(bc_a[block][:, nst:])
        dc_h, dc_l = split(dbc_a[block][:, nst:])
        squares = jnp.zeros((QB, 128), F32)
        crossed = jnp.zeros((QB, 128), F32)
        for p in range(heads // 2):
            at = slice(128 * p, 128 * p + 128)
            reach = jnp.exp(log_a[block, 0:1, at])
            s_in = start[:, 0:8, at].reshape(nst, 128)
            ds_in = start[:, 8:16, at].reshape(nst, 128)
            s0 = st_a[block, :, at] + reach * s_in
            ds0 = dst_a[block, :, at] + reach * (ds_in + log_a[block, 1:2, at] * s_in)
            s0_o[0, :, at] = s0
            s_h, s_l = split(s0)
            ds_h, ds_l = split(ds0)
            big = (
                nn(c_h, jnp.concatenate([s_h, ds_h], axis=1))
                + nn(c_h, jnp.concatenate([s_l, ds_l], axis=1))
                + nn(c_l, jnp.concatenate([s_h, ds_h], axis=1))
            )
            low = nn(dc_h, s_h) + nn(dc_h, s_l) + nn(dc_l, s_h)
            lift = jnp.exp(expand(cols, C_, p))
            add = lift * big[:, :128]
            y = y_a[block, :, at] + add
            dy = (
                dy_a[block, :, at]
                + lift * (big[:, 128:] + low)
                + expand(cols, DC_, p) * add
            )
            gz = gate_z[:, at].astype(F32)
            gate = gz * jax.nn.sigmoid(gz)
            gated = y * gate
            dgated = dy * gate
            gated_o[:, at] = gated
            dgated_o[:, at] = dgated
            squares = squares + gated * gated
            crossed = crossed + 2.0 * gated * dgated
        sums_o[0:1, :] = jnp.sum(squares.T, axis=0, keepdims=True)
        sums_o[1:2, :] = jnp.sum(crossed.T, axis=0, keepdims=True)


def forward_call(pre_x, pre_bc, dt, gate_z, cx, tcx, cbc, tcbc, hp, th, tw, parts):
    length, width = pre_x.shape
    wide = pre_bc.shape[1]
    nst = wide // 2
    heads = dt.shape[0]
    count = length // QB
    first = lambda i: jnp.minimum(i, count - 1)
    last = lambda i: jnp.maximum(i - 2 * count, 0)
    whole = lambda a: pl.BlockSpec(a.shape, lambda i: (0,) * a.ndim)
    fixed = lambda *s: pl.BlockSpec(s, lambda i: (0,) * len(s))
    rows = lambda w, f: pl.BlockSpec((QB, w), lambda i: (f(i), 0))
    cube = lambda r, f: pl.BlockSpec((1, r, width), lambda i: (f(i), 0, 0))
    tail = lambda w: pl.BlockSpec((16, w), lambda i: (length // 16 - 1, 0))
    lanes = lambda r, f: pl.BlockSpec((r, QB), lambda i: (0, f(i)))
    out = lambda *s: jax.ShapeDtypeStruct(s, F32)
    vmem = lambda *s: pltpu.VMEM(s, F32)
    dma = pltpu.SemaphoreType.DMA
    return pl.pallas_call(
        forward_kernel,
        grid=(3 * count,),
        in_specs=[
            rows(width, first), tail(width), rows(wide, first), tail(wide), lanes(heads, first),
            rows(width, last), whole(cx), whole(tcx), whole(cbc), whole(tcbc), whole(hp),
            whole(th), pl.BlockSpec(memory_space=pl.ANY),
        ],
        out_specs=[
            rows(width, first), rows(width, first), rows(wide, first), rows(wide, first),
            lanes(128, first), rows(128, first), cube(8, first), cube(nst, last),
            rows(width, last), rows(width, last), lanes(2, last), fixed(parts, width),
            fixed(8, width), fixed(8, wide), pl.BlockSpec(memory_space=pl.ANY),
        ],
        out_shape=[
            out(length, width), out(length, width), out(length, wide), out(length, wide),
            out(128, length), out(length, 128), out(count, 8, width), out(count, nst, width),
            out(length, width), out(length, width), out(2, length), out(parts, width),
            out(8, width), out(8, wide),
            jax.ShapeDtypeStruct((4, 4, *tw.shape), BF16),
        ],
        scratch_shapes=[
            vmem(QB + 8, width), vmem(QB + 8, wide), vmem(128, QB), vmem(nst, width),
            vmem(nst, width), vmem(8, width), vmem(count, QB, width), vmem(count, QB, width),
            vmem(count, QB, wide), vmem(count, QB, wide), vmem(count, 128, QB),
            vmem(count, QB, 128), vmem(count, nst, width), vmem(count, nst, width),
            vmem(count, 8, width), vmem(count, QB, width), vmem(count, QB, width),
            vmem(8, 128), pltpu.VMEM((16, width), BF16), pltpu.VMEM((16, wide), BF16),
            vmem(parts, 16, width), vmem(parts, 16, width), vmem(parts, 8, 128),
            vmem(parts, 16, width), vmem(parts, 16, width),
            dma((2,)), dma((2,)), dma((parts,)), dma((parts,)), dma((parts,)), dma((parts,)),
            dma((parts,)), dma((parts,)), dma((1,)), dma((4,)), dma((4,)), dma((4,)), dma((4,)),
            dma((4,)), dma((4,)), dma((4,)), dma((4,)),
        ],
        compiler_params=pltpu.CompilerParams(
            collective_id=1, has_side_effects=True, vmem_limit_bytes=LIMIT
        ),
        name="forward",
    )(pre_x, pre_x, pre_bc, pre_bc, dt, gate_z, cx, tcx, cbc, tcbc, hp, th, tw)


def middle_kernel(
    gated, dgated, sums, gate_in, w_in, tw_in, gain_in, tgain_in,
    by_o, gain_o, sum_z_o, sum_y_o, late_o,
    got, scal, both, part, sib, far_src, far_dst, out_src, out_dst, probe, back, gnw, got_z, got_y,
    mix, mix_got, gains, gate_z, w, tw, fetch_m,
    sums_s, sums_r, sib_s, sib_r, far_s, far_r, out_s, out_r, ag_s, ag_r, mix_s, mix_r,
    az_s, az_r, ay_s, ay_r,
):
    length, width = gated.shape
    blocks, _, blk = probe.shape
    fetches = [
        pltpu.make_async_copy(src, dst, fetch_m.at[i])
        for i, (src, dst) in enumerate(((w_in, w), (tw_in, tw), (gate_in, gate_z)))
    ]
    for copy in fetches:
        copy.start()
    groups = width // 128
    channels = width * 8.0
    head = lax.axis_index("head")
    me = lax.axis_index("seq")
    my_y, my_z = me // 4, lax.rem(me, 4)
    mine = head // 2
    core = lax.rem(head, 2)
    right, left, far = (lax.rem(mine + k, 4) for k in (1, 3, 2))
    device = lambda chip, c: {"head": chip * 2 + c}
    to_right, to_left, to_sib = device(right, core), device(left, core), device(mine, 1 - core)
    y_peers = [{"seq": lax.rem(my_y + k, 4) * 4 + my_z} for k in range(1, 4)]
    z_peers = [{"seq": my_y * 4 + lax.rem(my_z + k, 4)} for k in range(1, 4)]
    peers = others("head", 8)
    greet([{"head": to} for to in peers] + y_peers + z_peers)
    copies = []
    for k, to in enumerate(peers):
        copies.append(send(sums, got.at[head], sums_s.at[k], sums_r.at[k], {"head": to}))
    got[head] = sums[...]
    gain_o[...] = jnp.zeros_like(gain_o)
    gains[0:1] = gain_in[...].reshape(1, width)
    gains[1:2] = tgain_in[...].reshape(1, width)
    gain, tgain = gains.at[0:1], gains.at[1:2]
    for copy in copies:
        copy.wait()
    total = got[0]
    for i in range(1, 8):
        total = total + got[i]
    inv = lax.rsqrt(total[0:1] / channels + 1e-05)
    scal[0:1] = inv
    scal[1:2] = -0.5 * inv * inv * inv * total[1:2] / channels

    def column(row, start):
        at = pl.ds(pl.multiple_of(start, 128), 128)
        return jnp.broadcast_to(scal[row : row + 1, at], (128, 128)).T

    def norm(i, carry):
        start = pl.multiple_of(i * 128, 128)
        rows = pl.ds(start, 128)
        inv_c, d_inv_c = column(0, start), column(1, start)
        for g in range(groups):
            at = slice(128 * g, 128 * g + 128)
            gt, dgt = gated[rows, at], dgated[rows, at]
            ga = gain[:, at]
            scaled = gt * inv_c
            normed = scaled * ga
            d_normed = (dgt * inv_c + gt * d_inv_c) * ga + scaled * tgain[:, at]
            both[rows, at] = d_normed.astype(BF16)
            both[rows, width + 128 * g : width + 128 * g + 128] = normed.astype(BF16)
        return carry

    lax.fori_loop(0, length // 128, norm, 0)

    def columns(i):
        return pl.ds(pl.multiple_of(lax.rem(my_y + TURN[i], 4) * blk, 128), blk)

    def compute(i):
        slot, at = i % 2, columns(i)

        res = nn(both[:, 0:width], w[:, at]) + nt(both[:, width:], tw[at, :])
        part[slot] = res.reshape(4, 2, 128, blk)
        return send(part.at[slot, :, 1 - core], sib.at[i], sib_s.at[i], sib_r.at[i], to_sib)

    def pairs(i, copy):
        copy.wait()
        for chip in range(4):
            sib[i, chip] = sib[i, chip] + part[i % 2, chip, core]
        way, near = (to_right, to_left) if i % 2 == 0 else (to_left, to_right)
        near_chip = left if i % 2 == 0 else right
        far_src[i] = sib[i, far].astype(BF16)
        transit = send(far_src.at[i], far_dst.at[i], far_s.at[i], far_r.at[i], way)
        out_src[i, 0] = sib[i, near_chip].astype(BF16)
        direct = send(out_src.at[i, 0], out_dst.at[i, 0], out_s.at[i, 0], out_r.at[i, 0], near)
        return transit, direct

    def through(i, transit):
        transit.wait()
        way, chip = (to_right, right) if i % 2 == 0 else (to_left, left)
        out_src[i, 1] = (sib[i, chip] + far_dst[i].astype(F32)).astype(BF16)
        return send(out_src.at[i, 1], out_dst.at[i, 1], out_s.at[i, 1], out_r.at[i, 1], way)

    def pass_on(i, slot, chip, to):
        ref = probe.at[i, pl.ds(pl.multiple_of(chip * 256 + core * 128, 128), 128), :]
        return send(ref, ref, ag_s.at[i, slot], ag_r.at[i, slot], to)

    def own(i, direct, joined):
        direct.wait()
        joined.wait()
        rows = pl.ds(pl.multiple_of(mine * 256 + core * 128, 128), 128)
        res = sib[i, mine] + out_dst[i, 0].astype(F32) + out_dst[i, 1].astype(F32)
        probe[i, rows, :] = res.astype(BF16)
        go_right = pass_on(i, 0, mine, to_right)
        go_left = pass_on(i, 1, mine, to_left)
        return go_right, go_left, pass_on(i, 2, mine, to_sib)

    def forward(i, go_right, go_left):
        if i % 2 == 0:
            go_right.wait()
            onward = pass_on(i, 3, left, to_right)
            go_left.wait()
        else:
            go_left.wait()
            onward = pass_on(i, 3, right, to_left)
            go_right.wait()
        return onward, pass_on(i, 4, left, to_sib), pass_on(i, 5, right, to_sib)

    def last_hop(i, onward):
        onward.wait()
        return pass_on(i, 6, far, to_sib)

    def back_block(i, waits):
        for copy in waits:
            copy.wait()
        at = columns(i)
        summed = lax.dot_general(
            probe[i], both[:, width:], (((0,), (0,)), ((), ())), preferred_element_type=F32
        ).reshape(4, blk // 4, width)
        half = blk // 8
        sent = []
        if i < 2:
            gnw[i] = summed
        else:
            late_o[i - 2] = summed
        for k in (2, 1, 3) if i < 2 else ():
            z = lax.rem(my_z + k, 4)
            sent.append(
                send(
                    gnw.at[i, z, 0:half, :], got_z.at[i, k - 1],
                    az_s.at[i, k], az_r.at[i, k], z_peers[k - 1],
                )
            )
        if i < 2:
            sent.append(
                send(
                    gnw.at[i, :, half : 2 * half, :], got_y.at[i],
                    ay_s.at[i], ay_r.at[i], y_peers[TURN[i] - 1],
                )
            )

        res = nt(probe[i], w[:, at])
        back[...] = res if i == 0 else back[...] + res
        return sent

    fetches[0].wait()
    fetches[1].wait()
    sib0 = compute(0)
    sib1 = compute(1)
    far0, dir0 = pairs(0, sib0)
    sib2 = compute(2)
    far1, dir1 = pairs(1, sib1)
    join0 = through(0, far0)
    far2, dir2 = pairs(2, sib2)
    join1 = through(1, far1)
    sib3 = compute(3)
    ag0 = own(0, dir0, join0)
    ag1 = own(1, dir1, join1)
    fwd0 = forward(0, ag0[0], ag0[1])
    join2 = through(2, far2)
    far3, dir3 = pairs(3, sib3)
    fwd1 = forward(1, ag1[0], ag1[1])
    end0 = last_hop(0, fwd0[0])
    join3 = through(3, far3)
    sent = back_block(0, [ag0[2], fwd0[1], fwd0[2], end0])
    end1 = last_hop(1, fwd1[0])
    ag2 = own(2, dir2, join2)
    ag3 = own(3, dir3, join3)
    fwd2 = forward(2, ag2[0], ag2[1])
    sent = sent + back_block(1, [ag1[2], fwd1[1], fwd1[2], end1])
    fwd3 = forward(3, ag3[0], ag3[1])
    end2 = last_hop(2, fwd2[0])
    end3 = last_hop(3, fwd3[0])
    sent = sent + back_block(2, [ag2[2], fwd2[1], fwd2[2], end2])
    sent = sent + back_block(3, [ag3[2], fwd3[1], fwd3[2], end3])

    def mixing(i, carry):
        start = pl.multiple_of(i * 128, 128)
        rows = pl.ds(start, 128)
        inv_c = column(0, start)
        mixed = jnp.zeros((128, 128), F32)
        for g in range(groups):
            at = slice(128 * g, 128 * g + 128)
            prod = back[rows, at] * gated[rows, at]
            gain_o[:, at] = gain_o[:, at] + fold(prod * inv_c)
            mixed = mixed + prod * gain[:, at]
        mix[pl.ds(i, 1), :] = jnp.sum(mixed.T, axis=0, keepdims=True)
        return carry

    lax.fori_loop(0, length // 128, mixing, 0)
    copies = []
    for k, to in enumerate(peers):
        copies.append(send(mix, mix_got.at[head], mix_s.at[k], mix_r.at[k], {"head": to}))
    mix_got[head] = mix[...]
    for copy in copies:
        copy.wait()
    total = mix_got[0]
    for i in range(1, 8):
        total = total + mix_got[i]
    mix[...] = total / channels

    def finish(i, carry):
        start = pl.multiple_of(i * 128, 128)
        rows = pl.ds(start, 128)
        inv_c = column(0, start)
        mixed_c = jnp.broadcast_to(mix[pl.ds(i, 1), :], (128, 128)).T * (inv_c * inv_c * inv_c)
        for g in range(groups):
            at = slice(128 * g, 128 * g + 128)
            gz = gate_z[rows, at].astype(F32)
            gate = gz * jax.nn.sigmoid(gz)
            by_o[rows, at] = (
                back[rows, at] * gain[:, at] * inv_c - gated[rows, at] * mixed_c
            ) * gate
        return carry

    fetches[2].wait()
    lax.fori_loop(0, length // 128, finish, 0)
    for copy in sent:
        copy.wait()
    half = blk // 8
    for i in range(2):
        sum_z_o[i] = gnw[i, my_z, 0:half, :] + got_z[i, 0] + got_z[i, 1] + got_z[i, 2]
    sum_y_o[...] = late_o[1, :, half : 2 * half, :] + got_y[0] + got_y[1]


def middle_call(gated, dgated, sums, gate_z, w, tw, gain, tgain):
    length, width = gated.shape
    cols = w.shape[1]
    blk = cols // 4
    half = blk // 8
    out = lambda *s: jax.ShapeDtypeStruct(s, F32)
    dma = pltpu.SemaphoreType.DMA
    return pl.pallas_call(
        middle_kernel,
        in_specs=[VMEM] * 3 + [pl.BlockSpec(memory_space=pl.ANY)] * 3 + [VMEM] * 2,
        out_specs=[VMEM] * 5,
        out_shape=[
            out(length, width), out(8, width), out(2, half, width), out(4, half, width),
            out(2, 4, blk // 4, width),
        ],
        scratch_shapes=[
            pltpu.VMEM((8, 2, length), F32),
            pltpu.VMEM((8, length), F32),
            pltpu.VMEM((length, 2 * width), BF16),
            pltpu.VMEM((2, 4, 2, 128, blk), F32),
            pltpu.VMEM((4, 4, 128, blk), F32),
            pltpu.VMEM((4, 128, blk), BF16),
            pltpu.VMEM((4, 128, blk), BF16),
            pltpu.VMEM((4, 2, 128, blk), BF16),
            pltpu.VMEM((4, 2, 128, blk), BF16),
            pltpu.VMEM((4, length, blk), BF16),
            pltpu.VMEM((length, width), F32),
            pltpu.VMEM((2, 4, blk // 4, width), F32),
            pltpu.VMEM((2, 3, half, width), F32),
            pltpu.VMEM((2, 4, half, width), F32),
            pltpu.VMEM((8, 128), F32),
            pltpu.VMEM((8, 8, 128), F32),
            pltpu.VMEM((8, width), F32),
            pltpu.VMEM(gate_z.shape, BF16), pltpu.VMEM(w.shape, BF16), pltpu.VMEM(tw.shape, BF16),
            dma((3,)),
            dma((8,)), dma((8,)), dma((4,)), dma((4,)), dma((4,)), dma((4,)),
            dma((4, 2)), dma((4, 2)), dma((4, 7)), dma((4, 7)), dma((8,)), dma((8,)),
            dma((2, 4)), dma((2, 4)), dma((2,)), dma((2,)),
        ],
        compiler_params=pltpu.CompilerParams(
            collective_id=3, has_side_effects=True, vmem_limit_bytes=61 * 1024 * 1024
        ),
        name="probe_and_back",
    )(gated, dgated, sums, gate_z, w, tw, gain, tgain)


def fold(a):
    return jnp.sum(a.reshape(a.shape[0] // 8, 8, a.shape[1]), axis=0)


def adjoint_kernel(
    by, x, gx, pre_x, halo_x, bc, gbc, pre_bc, halo_bc, rowv, colv, s0_b, log, last_log,
    gain, decays, hp, sum_z, sum_y, late,
    result_o,
    wx, wbc, head_o, pack_o, lam, back_u_a, back_bc_a, state, msg, landed, answer, s_end,
    own_z, own_y, got_z, got_y, end_z, end_y, pack_z, landed_z, landed_y, part, landed_q,
    az_s, az_r, ay_s, ay_r, bz_s, bz_r, by_s, by_r,
    s1_s, s1_r, s2_s, s2_r, f1_s, f1_r, f3_s, f3_r, f2_s, f2_r,
):
    step = pl.program_id(0)
    half = lam.shape[0]
    nst = bc.shape[1] // 2
    width = by.shape[1]
    heads = width // HW
    count, n_head = landed.shape[0], landed_q.shape[0]
    me, head = lax.axis_index("seq"), lax.axis_index("head")
    my_y, my_z = me // 4, lax.rem(me, 4)
    seq_peers, head_peers = others("seq", count), others("head", n_head)
    rows_half = sum_z.shape[1]
    mask = lane_mask()

    y_peers = [{"seq": lax.rem(my_y + k, 4) * 4 + my_z} for k in range(1, 4)]
    z_peers = [{"seq": my_y * 4 + lax.rem(my_z + k, 4)} for k in range(1, 4)]

    def late_copies(part_at):
        copies = []
        for i, k in ((0, 1), (0, 3)) if part_at % 2 == 0 else ((0, 2),):
            i = i + part_at // 2
            copies.append(
                link(
                    late.at[i, lax.rem(my_z + k, 4), 0:rows_half, :], got_z.at[i, k - 1],
                    az_s.at[i, k], az_r.at[i, k], z_peers[k - 1],
                )
            )
        copies.append(
            link(
                late.at[0, part_at, rows_half : 2 * rows_half, :], got_y.at[part_at],
                ay_s.at[part_at], ay_r.at[part_at], y_peers[TURN[2] - 1],
            )
        )
        return copies

    def early_last():
        return [
            link(sum_z.at[i], end_z.at[i], bz_s.at[i], bz_r.at[i], y_peers[TURN[i] - 1])
            for i in range(2)
        ]

    def last_copies():
        copies = [link(own_z, end_z.at[2], bz_s.at[2], bz_r.at[2], y_peers[TURN[2] - 1])]
        for k in (2, 1, 3):
            z = lax.rem(my_z + k, 4)
            copies.append(
                link(own_y.at[z], end_y.at[k - 1], by_s.at[k], by_r.at[k], z_peers[k - 1])
            )
        return copies

    for part_at, when in enumerate((0, 3, half + SCAN_AT + 1, half + SCAN_AT + 2)):

        @pl.when(step == when)
        def _(part_at=part_at):
            if part_at == 0:
                greet([{"seq": to} for to in seq_peers] + [{"head": to} for to in head_peers])
            for copy in late_copies(part_at) + (early_last() if part_at == 3 else []):
                copy.start()

    @pl.when(step == 0)
    def _():
        state[...] = jnp.zeros_like(state)
        head_o[...] = jnp.zeros_like(head_o)
        pack_o[...] = jnp.zeros_like(pack_o)
        pack_o[8:9, :] = jnp.sum(gain[...], axis=0, keepdims=True)

    @pl.when(step < half)
    def _():
        lam[half - 1 - step] = state[...]
        cols = colv[...]
        ct_h, ct_l = split(bc[:, nst:].T)
        for p in range(heads // 2):
            at = slice(128 * p, 128 * p + 128)
            lifted = jnp.exp(expand(cols, C_, p)) * by[:, at]
            l_h, l_l = split(lifted)
            add = nn(ct_h, l_h) + nn(ct_h, l_l) + nn(ct_l, l_h)
            state[:, at] = jnp.exp(log[0, 2:3, at]) * state[:, at] + add

    def scan_copies():
        return [
            link(msg.at[to], landed.at[me], s1_s.at[k], s1_r.at[k], {"seq": to})
            for k, to in enumerate(seq_peers)
        ]

    def back_copies():
        return [
            link(answer.at[to], s_end.at[me], s2_s.at[k], s2_r.at[k], {"seq": to})
            for k, to in enumerate(seq_peers)
        ]

    @pl.when(step == half - 1)
    def _():
        msg[...] = state[...].reshape(count, 8, width)
        for copy in scan_copies():
            copy.start()

    @pl.when(step == half + SCAN_AT)
    def _():
        landed[me] = msg[me]
        for copy in scan_copies():
            copy.wait()
        adjoint = jnp.zeros((8, width), F32)
        for i in range(count - 1, -1, -1):
            answer[i] = adjoint
            adjoint = decays[i : i + 1, :] * adjoint + landed[i]
        for copy in back_copies():
            copy.start()

    @pl.when((step >= half) & (step < 2 * half))
    def _():
        block = step - half
        b_mat, c_mat = bc[:, :nst], bc[:, nst:]
        at_i = lax.broadcasted_iota(jnp.int32, (QB, QB), 1)
        at_j = lax.broadcasted_iota(jnp.int32, (QB, QB), 0)
        keep = at_i >= at_j
        inner_t = jnp.where(keep, nt3(b_mat, c_mat), 0.0)
        cols = colv[...]
        rows = rowv[...]
        back_inner_t = jnp.zeros((QB, QB), F32)
        for p in range(heads // 2):
            at = slice(128 * p, 128 * p + 128)
            byp = by[:, at]
            u = expand(cols, S_, p) * x[:, at]
            y_h, y_l = split(byp)
            u_h, u_l = split(
                jnp.concatenate([jnp.where(mask, u, 0.0), jnp.where(mask, 0.0, u)], axis=0)
            )
            back_mts = nt(
                jnp.concatenate([u_h, u_l], axis=1), jnp.concatenate([y_h, y_h], axis=1)
            ) + nt(u_h, y_l)
            mats = []
            for s in range(2):
                h = 2 * p + s
                c_row = rows[C_ + h : C_ + h + 1, :]
                cs_row = rows[CS_ + h : CS_ + h + 1, :]
                back_mt = back_mts[s * QB : s * QB + QB]
                diff = jnp.minimum(c_row - bcast(cols, C_ + h), 0.0)
                level = jnp.exp(diff)
                back_inner_t = back_inner_t + level * back_mt
                m_t = inner_t * level
                prod = m_t * back_mt
                head_o[h, 0] = head_o[h, 0] + fold(prod * diff)
                head_o[h, 1] = head_o[h, 1] + fold(prod * (cs_row - bcast(cols, CS_ + h)))
                mats.append(m_t)
            a_h, a_l = split(jnp.concatenate(mats, axis=0))
            back_u2 = nn(
                jnp.concatenate([a_h, a_l], axis=1), jnp.concatenate([y_h, y_h], axis=0)
            ) + nn(a_h, y_l)
            back_u_a[block, :, at] = jnp.where(mask, back_u2[:QB], back_u2[QB:])
        back_inner_t = jnp.where(keep, back_inner_t, 0.0)
        back_bc_a[block, :, 0:nst] = nn3(back_inner_t, c_mat)
        back_bc_a[block, :, nst:] = nn3(back_inner_t.T, b_mat)

    @pl.when(step == 2 * half)
    def _():
        s_end[me] = answer[me]
        for copy in back_copies():
            copy.wait()

    @pl.when(step >= 2 * half)
    def _():
        block = step - 2 * half
        load_window(wx, halo_x, pre_x, step == 2 * half)
        load_window(wbc, halo_bc, pre_bc, step == 2 * half)
        b_h, b_l = split(bc[:, :nst])
        c_h, c_l = split(bc[:, nst:])
        cols = colv[...]
        back_b = back_bc_a[block, :, 0:nst]
        back_c = back_bc_a[block, :, nst:]
        for p in range(heads // 2):
            at = slice(128 * p, 128 * p + 128)
            own, sig_own = log[0, 2:3, at], log[0, 4:5, at]
            reach = jnp.exp(last_log[0, 0:1, at] + last_log[0, 2:3, at] - log[0, 0:1, at] - own)
            s1 = lam[block, :, at] + reach * s_end[:, :, at].reshape(nst, 128)
            s0 = s0_b[0, :, at]
            byp, xp = by[:, at], x[:, at]
            size = expand(cols, S_, p)
            c_cols, cs_cols = expand(cols, C_, p), expand(cols, CS_, p)
            left = own - c_cols
            to_end = jnp.exp(left)
            u = size * xp
            lifted = jnp.exp(c_cols) * byp
            s0_h, s0_l = split(s0)
            s1_h, s1_l = split(s1)
            l_h, l_l = split(lifted)
            e_h, e_l = split(to_end * u)
            back_c = back_c + nt(
                jnp.concatenate([l_h, l_l], axis=1), jnp.concatenate([s0_h, s0_h], axis=1)
            ) + nt(l_h, s0_l)
            back_b = back_b + nt(
                jnp.concatenate([e_h, e_l], axis=1), jnp.concatenate([s1_h, s1_h], axis=1)
            ) + nt(e_h, s1_l)
            through_c = lifted * (nn(c_h, s0_h) + nn(c_h, s0_l) + nn(c_l, s0_h))
            from_end = to_end * (nn(b_h, s1_h) + nn(b_h, s1_l) + nn(b_l, s1_h))
            through_b = u * from_end
            back_u = back_u_a[block, :, at] + from_end
            back_x = back_u * size + expand(hp[2:3, :], 0, p) * byp
            carried = jnp.sum(s1 * s0, axis=0, keepdims=True) * jnp.exp(own)
            total = lambda a: jnp.sum(a, axis=0, keepdims=True)
            pack_o[4:5, at] = pack_o[4:5, at] + total(expand(cols, SG_, p) * (back_u * xp))
            pack_o[5:6, at] = (
                pack_o[5:6, at] + carried * own + total(through_c * c_cols + through_b * left)
            )
            pack_o[6:7, at] = (
                pack_o[6:7, at]
                + carried * sig_own
                + total(through_c * cs_cols + through_b * (sig_own - cs_cols))
            )
            pack_o[7:8, at] = pack_o[7:8, at] + total(byp * xp)
            back_z = back_x * gx[:, at]
            for k in range(4):
                pack_o[k : k + 1, at] = pack_o[k : k + 1, at] + total(
                    back_z * wx[5 + k : 5 + k + QB, at]
                )
        back_zbc = jnp.concatenate([back_b, back_c], axis=1) * gbc[...]
        for k in range(4):
            pack_o[9 + k : 10 + k, 0 : 2 * nst] = pack_o[
                9 + k : 10 + k, 0 : 2 * nst
            ] + jnp.sum(back_zbc * wbc[5 + k : 5 + k + QB, :], axis=0, keepdims=True)

    @pl.when(step == 3 * half - 5)
    def _():
        for part_at in range(4):
            for copy in late_copies(part_at):
                copy.wait()
        own_z[...] = late[0, my_z, 0:rows_half, :] + got_z[0, 0] + got_z[0, 1] + got_z[0, 2]
        own_y[...] = sum_y[...] + got_y[...]
        for copy in last_copies():
            copy.start()

    @pl.when(step == 3 * half - 1)
    def _():
        for p in range(heads // 2):
            at = slice(128 * p, 128 * p + 128)
            for kind in range(2):
                even, odd = head_o[2 * p, kind], head_o[2 * p + 1, kind]
                even = even + pltpu.roll(even, HW, 1)
                odd = odd + pltpu.roll(odd, HW, 1)
                both = jnp.sum(jnp.where(mask, even, odd), axis=0, keepdims=True)
                pack_o[5 + kind : 6 + kind, at] = pack_o[5 + kind : 6 + kind, at] + both
        for slots, group, sems, mine in (
            (landed_z, z_peers, (f1_s, f1_r), pack_o),
            (landed_y, y_peers, (f3_s, f3_r), pack_z),
        ):
            copies = []
            for k, to in enumerate(group):
                copies.append(send(mine, slots.at[k], sems[0].at[k], sems[1].at[k], to))
            for copy in copies:
                copy.wait()
            if slots is landed_z:
                for z in range(4):
                    k = lax.rem(my_z + 3 - z, 4)
                    term = jnp.where(z == my_z, pack_o[...], slots[jnp.minimum(k, 2)])
                    total = term if z == 0 else total + term
                pack_z[...] = total
            else:
                for y in range(4):
                    k = lax.rem(my_y + 3 - y, 4)
                    term = jnp.where(y == my_y, pack_z[...], slots[jnp.minimum(k, 2)])
                    total = term if y == 0 else total + term
        part[...] = total[8:16, 0 : 2 * nst]
        copies = []
        for k, to in enumerate(head_peers):
            copies.append(send(part, landed_q.at[head], f2_s.at[k], f2_r.at[k], {"head": to}))
        landed_q[head] = part[...]
        result_o[2 * rows_half : 2 * rows_half + 16] = total
        at = lax.broadcasted_iota(jnp.int32, (width, 128), 0)
        to = lax.broadcasted_iota(jnp.int32, (width, 128), 1) * HW
        pick = jnp.where((at >= to) & (at < to + HW), 1.0, 0.0).astype(F32)
        sums = jnp.dot(
            total, pick, precision=lax.Precision.HIGHEST, preferred_element_type=F32
        )[:, :heads]
        at = 2 * rows_half + 24
        result_o[at : at + 1, 0:heads] = sums[4:5] - jnp.exp(hp[1:2]) * sums[6:7]
        result_o[at + 1 : at + 2, 0:heads] = sums[5:6]
        result_o[at + 2 : at + 3, 0:heads] = sums[7:8]
        for copy in early_last() + last_copies():
            copy.wait()
        total = late[1, my_z, 0:rows_half, :] + got_z[1, 0] + got_z[1, 1] + got_z[1, 2]
        result_o[0:rows_half] = total + end_z[0] + end_z[1] + end_z[2]
        result_o[rows_half : 2 * rows_half] = own_y[my_z] + end_y[0] + end_y[1] + end_y[2]
        for copy in copies:
            copy.wait()
        total2 = landed_q[0]
        for i in range(1, n_head):
            total2 = total2 + landed_q[i]
        result_o[2 * rows_half + 16 : 2 * rows_half + 24, 0 : 2 * nst] = total2


def adjoint_call(
    by, x, gx, pre_x, halo_x, bc, gbc, pre_bc, halo_bc, rowv, colv, s0, logs, gain, decays,
    hp, sum_z, sum_y, late_sums, count, n_head,
):
    length, width = by.shape
    wide = bc.shape[1]
    nst = wide // 2
    heads = width // HW
    half = length // QB
    rows_half = sum_z.shape[1]
    piece = 2 * rows_half
    every = lambda i: jnp.where(i < half, half - 1 - i, lax.rem(i, half))
    mid = lambda i: jnp.where(i < half, 0, lax.rem(i, half))
    late = lambda i: jnp.maximum(i - 2 * half, 0)
    whole = lambda a: pl.BlockSpec(a.shape, lambda i: (0,) * a.ndim)
    rows = lambda w, f: pl.BlockSpec((QB, w), lambda i: (f(i), 0))
    cube = lambda r, f: pl.BlockSpec((1, r, width), lambda i: (f(i), 0, 0))
    out = lambda *s: jax.ShapeDtypeStruct(s, F32)
    fixed = lambda *s: pl.BlockSpec(s, lambda i: (0,) * len(s))
    dma = pltpu.SemaphoreType.DMA
    return pl.pallas_call(
        adjoint_kernel,
        grid=(3 * half,),
        in_specs=[
            rows(width, every), rows(width, mid), rows(width, late), rows(width, late),
            whole(halo_x), rows(wide, every), rows(wide, late), rows(wide, late), whole(halo_bc),
            pl.BlockSpec((128, QB), lambda i: (0, mid(i))), rows(128, every),
            cube(nst, late), cube(8, every),
            pl.BlockSpec((1, 8, width), lambda i: (half - 1, 0, 0)),
            whole(gain), whole(decays), whole(hp),
            whole(sum_z), whole(sum_y), VMEM,
        ],
        out_specs=fixed(256, width),
        out_shape=out(256, width),
        scratch_shapes=[
            pltpu.VMEM((QB + 8, width), F32), pltpu.VMEM((QB + 8, wide), F32),
            pltpu.VMEM((heads, 2, 8, 128), F32), pltpu.VMEM((16, width), F32),
            pltpu.VMEM((half, nst, width), F32), pltpu.VMEM((half, QB, width), F32),
            pltpu.VMEM((half, QB, wide), F32), pltpu.VMEM((nst, width), F32),
            pltpu.VMEM((count, 8, width), F32), pltpu.VMEM((count, 8, width), F32),
            pltpu.VMEM((count, 8, width), F32), pltpu.VMEM((count, 8, width), F32),
            pltpu.VMEM((rows_half, width), F32), pltpu.VMEM((4, rows_half, width), F32),
            pltpu.VMEM((2, 3, rows_half, width), F32), pltpu.VMEM((4, rows_half, width), F32),
            pltpu.VMEM((3, rows_half, width), F32), pltpu.VMEM((3, rows_half, width), F32),
            pltpu.VMEM((16, width), F32), pltpu.VMEM((3, 16, width), F32),
            pltpu.VMEM((3, 16, width), F32), pltpu.VMEM((8, wide), F32),
            pltpu.VMEM((n_head, 8, wide), F32),
            dma((2, 4)), dma((2, 4)), dma((4,)), dma((4,)),
            dma((4,)), dma((4,)), dma((4,)), dma((4,)),
            dma((count,)), dma((count,)), dma((count,)), dma((count,)),
            dma((3,)), dma((3,)), dma((3,)), dma((3,)), dma((n_head,)), dma((n_head,)),
        ],
        compiler_params=pltpu.CompilerParams(
            collective_id=2, has_side_effects=True, vmem_limit_bytes=LIMIT
        ),
        name="adjoint",
    )(
        by, x, gx, pre_x, halo_x, bc, gbc, pre_bc, halo_bc, rowv, colv, s0, logs, logs,
        gain, decays, hp, sum_z, sum_y, late_sums,
    )


def outputs_kernel(result, gcx_o, gcbc_o, heads_o, gain_o, gnw_o):
    piece, heads, wide = gnw_o.shape[0], heads_o.shape[1], gcbc_o.shape[1]
    width = result.shape[1]
    gcx_o[...] = result[piece : piece + 4]
    gain_o[...] = result[piece + 8 : piece + 9].reshape(width)
    gcbc_o[...] = result[piece + 17 : piece + 21, 0:wide]
    heads_o[...] = result[piece + 24 : piece + 27, 0:heads]
    gnw_o[...] = result[0:piece]


def outputs_call(result, piece, bc_shape, heads_shape):
    width = result.shape[1]
    out = lambda *s: jax.ShapeDtypeStruct(s, F32)
    return pl.pallas_call(
        outputs_kernel,
        in_specs=[VMEM],
        out_specs=[VMEM] * 5,
        out_shape=[
            out(4, width), out(*bc_shape), out(*heads_shape), out(width), out(piece, width),
        ],
        name="outputs",
    )(result)


def on_device(
    pre_x, pre_bc, gate_z, dt_raw, conv_x, conv_bc, head_params, norm_gain, w_out,
    t_conv_x, t_conv_bc, t_heads, t_gain, t_wout,
):
    count = lax.axis_size("seq")
    x, gx, bc, gbc, rowv, colv, logs, s0, gated, d_gated, sums, decays, halo_x, halo_bc, tw = forward_call(
        pre_x, pre_bc, dt_raw, gate_z, conv_x, t_conv_x, conv_bc, t_conv_bc, head_params, t_heads,
        t_wout.T, count,
    )
    back_y, gain_part, sum_z, sum_y, late_sums = middle_call(
        gated, d_gated, sums, gate_z, w_out, tw.reshape(-1, w_out.shape[0]), norm_gain, t_gain
    )
    result = adjoint_call(
        back_y, x, gx, pre_x, halo_x, bc, gbc, pre_bc, halo_bc, rowv, colv, s0, logs,
        gain_part, decays, head_params, sum_z, sum_y, late_sums, count, lax.axis_size("head"),
    )
    gn_conv_x, gn_conv_bc, gn_heads, gn_gain, gn_wout = outputs_call(
        result, t_wout.shape[1], conv_bc.shape, head_params.shape
    )
    return gn_conv_x, gn_conv_bc, gn_heads, gn_gain, gn_wout.T


def solution(mesh):
    in_specs = (
        P("seq", "head"), P("seq", None), P("seq", "head"), P("head", "seq"), P(None, "head"),
        P(), P(None, "head"), P("head"), P("head", None), P(None, "head"), P(), P(None, "head"),
        P("head"), P("head", "seq"),
    )
    out_specs = (P(None, "head"), P(), P(None, "head"), P("head"), P("head", "seq"))
    return jax.shard_map(
        on_device, mesh=mesh, in_specs=in_specs, out_specs=out_specs, check_vma=False
    )
```
